32 devices in a mesh: dp: 8 (over z, x), tensor: 4 (over y, core).
Axes of the slice: x: 2, y: 2, z: 4, core: 2. Of those that a mesh axis runs over, the one named last changes fastest.
Arguments:
- tokens: bfloat16 [256, 128, 512], P('dp', 'tensor'), may hold values from -6 to 6
- memory: bfloat16 [256, 512, 512], P('dp', 'tensor'), may hold values from -6 to 6
- cotangent: bfloat16 [256, 128, 512], P('dp', 'tensor'), may hold values from -27 to 27
- buckets: int32 [256, 128, 128], P('dp'), may hold values from 0 to 31, as said below
- key_mask: int32 [256, 128, 128], P('dp'), may hold values from 0 to 1, as said below
- task_groups: int32 [256], P('dp'), may hold values from 0 to 3
- weights_in: float32 [6, 512, 512], P(None, 'dp', 'tensor'), may hold values from -0.25 to 0.25
- weights_out: float32 [2, 512, 512], P(None, 'tensor', 'dp'), may hold values from -0.75 to 0.75
- weights_up: float32 [512, 2048], P('dp', 'tensor'), may hold values from -0.25 to 0.25
- weights_down: float32 [2048, 512], P('tensor', 'dp'), may hold values from -0.1875 to 0.1875
- gains: float32 [3, 512], replicated, may hold values from 0.25 to 2.7
- position_bias: float32 [32, 8], P(None, 'tensor'), may hold values from -3 to 3
- momentum_in: float32 [6, 512, 512], P(None, 'dp', 'tensor'), may hold values from -0.005859375 to 0.005859375
- average_in: float32 [6, 512, 512], P(None, 'dp', 'tensor'), may hold values from -0.25 to 0.25
- momentum_out: float32 [2, 512, 512], P(None, 'tensor', 'dp'), may hold values from -0.005859375 to 0.005859375
- average_out: float32 [2, 512, 512], P(None, 'tensor', 'dp'), may hold values from -0.75 to 0.75
- momentum_up: float32 [512, 2048], P('dp', 'tensor'), may hold values from -0.005859375 to 0.005859375
- average_up: float32 [512, 2048], P('dp', 'tensor'), may hold values from -0.25 to 0.25
- momentum_down: float32 [2048, 512], P('tensor', 'dp'), may hold values from -0.005859375 to 0.005859375
- average_down: float32 [2048, 512], P('tensor', 'dp'), may hold values from -0.1875 to 0.1875
- momentum_gain: float32 [3, 512], P(None, 'tensor'), may hold values from -0.0234375 to 0.0234375
- average_gain: float32 [3, 512], P(None, 'tensor'), may hold values from 0.5 to 1.5
- momentum_bias: float32 [32, 8], P(None, 'tensor'), may hold values from -0.0234375 to 0.0234375
- average_bias: float32 [32, 8], P(None, 'tensor'), may hold values from -3 to 3
Outputs:
- output: bfloat16 [256, 128, 512], P('dp', 'tensor')
- tokens_grad: float32 [256, 128, 512], P('dp', 'tensor')
- memory_grad: float32 [256, 512, 512], P('dp', 'tensor')
- example_norms: float32 [256], P('dp')
- velocity_in: float32 [6, 512, 512], P(None, 'dp', 'tensor')
- averaged_in: float32 [6, 512, 512], P(None, 'dp', 'tensor')
- updated_in: float32 [6, 512, 512], P(None, 'dp', 'tensor')
- velocity_out: float32 [2, 512, 512], P(None, 'tensor', 'dp')
- averaged_out: float32 [2, 512, 512], P(None, 'tensor', 'dp')
- updated_out: float32 [2, 512, 512], P(None, 'tensor', 'dp')
- velocity_up: float32 [512, 2048], P('dp', 'tensor')
- averaged_up: float32 [512, 2048], P('dp', 'tensor')
- updated_up: float32 [512, 2048], P('dp', 'tensor')
- velocity_down: float32 [2048, 512], P('tensor', 'dp')
- averaged_down: float32 [2048, 512], P('tensor', 'dp')
- updated_down: float32 [2048, 512], P('tensor', 'dp')
- velocity_gain: float32 [3, 512], P(None, 'tensor')
- averaged_gain: float32 [3, 512], P(None, 'tensor')
- updated_gain: float32 [3, 512], P(None, 'tensor')
- velocity_bias: float32 [32, 8], P(None, 'tensor')
- averaged_bias: float32 [32, 8], P(None, 'tensor')
- updated_bias: float32 [32, 8], P(None, 'tensor')
The draws below stay inside these ranges and needn't reach their ends.
Inputs may be any that keep to these rules, and one draw needn't show every extreme that they name: buckets[e, i, j] is the bucket of the distance from key j's position back to query i's, the same for all heads. key_mask is 0 above the diagonal and 1 on it.
All inputs are finite; a program needn't handle non-finite values.
Results may differ from the reference program's by a relative error of at most 0.023.
The reference program's roundings to bfloat16 on the way count: a program that leaves them out, or rounds other values in their place, can miss the bound.
Values may be sent and summed in bfloat16 or wider, within the bound.
No kernel may reach another device: no remote copies, remote signals or barrier semaphores. Data moves between devices by JAX's collectives and lax.ppermute only.
A program may use at most 512 MiB of HBM per device.

```python
import math
import jax
import jax.numpy as jnp
from jax import lax

D = 512
HEADS = 8
HEAD_DIM = 64
FF = 2048
BUCKETS = 32
GROUPS = 4
SEQ = 128
MEM = 512
EXAMPLES = 256


bucket_edges = (19, 21, 24, 27, 31, 35, 40, 46, 52, 59, 67, 77, 87, 99, 113)


def layout(key):
    first_key, second_key = jax.random.split(key)
    starts = (jax.random.randint(first_key, (EXAMPLES, SEQ), 0, 12) == 0).astype(jnp.int32)
    segment = jnp.cumsum(starts, 1)
    places = jnp.cumsum(jax.random.randint(second_key, (EXAMPLES, SEQ), 1, 3), 1)
    return (segment, places)


def draw_key_mask(key, part):
    segment, places = layout(key)
    order = jnp.arange(SEQ)
    causal = order[:, None] >= order[None, :]
    same = segment[:, :, None] == segment[:, None, :]
    return (causal[None] & same).astype(jnp.int32)


def draw_buckets(key, part):
    segment, places = layout(key)
    distance = jnp.maximum(places[:, :, None] - places[:, None, :], 0)
    bucket = jnp.minimum(distance, 16)
    for edge in bucket_edges:
        bucket = bucket + (distance >= edge).astype(jnp.int32)
    return bucket.astype(jnp.int32)


def draw_cotangent(key, part):
    key = jax.random.fold_in(key, 11)
    noise_key, scale_key = jax.random.split(key)
    order = jnp.arange(EXAMPLES, dtype=jnp.float32) / max(EXAMPLES - 1, 1)
    jitter = jnp.exp(jax.random.uniform(scale_key, (EXAMPLES,), jnp.float32, -0.8, 0.8))
    base = jax.random.truncated_normal(noise_key, -4.0, 4.0, (EXAMPLES, SEQ, D), jnp.float32)
    rise = 1.0 + 2.0 * order
    return (base * (rise * jitter)[:, None, None]).astype(jnp.bfloat16)


def draw_gains(key, part):
    key = jax.random.fold_in(key, 17)
    order = jnp.arange(D, dtype=jnp.float32) / (D - 1)
    rise = 0.6 + 1.2 * order
    noise = 0.1 * jax.random.truncated_normal(key, -3.0, 3.0, (3, D), jnp.float32)
    return (rise[None, :] * (1.0 + noise)).astype(jnp.float32)


def set_ends(drawn, stream_key, low, largest):
    dims = drawn.shape
    spot = [jax.random.randint(jax.random.fold_in(stream_key, axis), (), 0, dims[axis]) for axis in range(len(dims))]
    drawn = drawn.at[tuple(spot)].set(low)
    longest = dims.index(max(dims))
    spot[longest] = (spot[longest] + 1) % dims[longest]
    return drawn.at[tuple(spot)].set(largest)


def level_of(own_key, dims, cuts, low, largest):
    def one(dim, blocks):
        heights = jax.random.uniform(jax.random.fold_in(jax.random.fold_in(own_key, 6), dim), (blocks,), jnp.float32, low / len(cuts), largest / len(cuts))
        return jnp.repeat(jnp.exp(heights), dims[dim] // blocks).reshape((-1,) + (1,) * (len(dims) - dim - 1))

    factor_of = one(*cuts[0])
    for cut in cuts[1:]:
        factor_of = factor_of * one(*cut)
    return factor_of


def centred(rng, extent, deviation, bound, pieces=(), kind=jnp.bfloat16):
    loudness = level_of(rng, extent, pieces, -0.22, 0.18) if pieces else 1.0
    drawn = jax.random.normal(rng, extent, jnp.float32) * deviation * loudness
    return jnp.minimum(jnp.maximum(drawn, -bound), bound).astype(kind)


def setup_inputs(seed: int = 0) -> dict:
    key_list = jax.random.split(jax.random.key(seed), 25)
    return {
        "tokens": centred(key_list[0], (EXAMPLES, SEQ, D), 1.0, 6.0, ((0, 8), (1, 4))),
        "memory": centred(key_list[1], (EXAMPLES, MEM, D), 1.0, 6.0, ((0, 8), (1, 4))),
        "cotangent": draw_cotangent(jax.random.fold_in(key_list[24], 71), 0),
        "buckets": draw_buckets(jax.random.fold_in(key_list[24], 71), 0),
        "key_mask": draw_key_mask(jax.random.fold_in(key_list[24], 71), 0),
        "task_groups": set_ends(jax.random.randint(key_list[5], (EXAMPLES,), 0, GROUPS), jax.random.fold_in(key_list[5], 1), 0, GROUPS - 1).astype(jnp.int32),
        "weights_in": centred(key_list[6], (6, D, HEADS * HEAD_DIM), D ** -0.5, 0.25, ((1, 8), (2, 4)), jnp.float32),
        "weights_out": centred(key_list[7], (2, HEADS * HEAD_DIM, D), (HEADS * HEAD_DIM // 8) ** -0.5, 0.75, ((1, 4), (2, 8)), jnp.float32),
        "weights_up": centred(key_list[8], (D, FF), D ** -0.5, 0.25, ((0, 8), (1, 4)), jnp.float32),
        "weights_down": centred(key_list[9], (FF, D), (FF // 2) ** -0.5, 0.1875, ((0, 4), (1, 8)), jnp.float32),
        "gains": draw_gains(jax.random.fold_in(key_list[24], 71), 0),
        "position_bias": centred(key_list[11], (BUCKETS, HEADS), 0.5, 3.0, ((1, 4),), jnp.float32),
        "momentum_in": centred(key_list[12], (6, D, HEADS * HEAD_DIM), (2 / (8 * D * HEADS * HEAD_DIM + 2 * D * FF) ** 0.5), 0.005859375, ((1, 8), (2, 4)), jnp.float32),
        "average_in": centred(key_list[13], (6, D, HEADS * HEAD_DIM), D ** -0.5, 0.25, ((1, 8), (2, 4)), jnp.float32),
        "momentum_out": centred(key_list[14], (2, HEADS * HEAD_DIM, D), (2 / (8 * D * HEADS * HEAD_DIM + 2 * D * FF) ** 0.5), 0.005859375, ((1, 4), (2, 8)), jnp.float32),
        "average_out": centred(key_list[15], (2, HEADS * HEAD_DIM, D), (HEADS * HEAD_DIM // 8) ** -0.5, 0.75, ((1, 4), (2, 8)), jnp.float32),
        "momentum_up": centred(key_list[16], (D, FF), (2 / (8 * D * HEADS * HEAD_DIM + 2 * D * FF) ** 0.5), 0.005859375, ((0, 8), (1, 4)), jnp.float32),
        "average_up": centred(key_list[17], (D, FF), D ** -0.5, 0.25, ((0, 8), (1, 4)), jnp.float32),
        "momentum_down": centred(key_list[18], (FF, D), (2 / (8 * D * HEADS * HEAD_DIM + 2 * D * FF) ** 0.5), 0.005859375, ((0, 4), (1, 8)), jnp.float32),
        "average_down": centred(key_list[19], (FF, D), (FF // 2) ** -0.5, 0.1875, ((0, 4), (1, 8)), jnp.float32),
        "momentum_gain": centred(key_list[20], (3, D), (8 / (8 * D * HEADS * HEAD_DIM + 2 * D * FF) ** 0.5), 0.0234375, ((1, 4),), jnp.float32),
        "average_gain": jnp.clip(1.0 + 0.1 * jax.random.normal(key_list[21], (3, D), jnp.float32), 0.5, 1.5),
        "momentum_bias": centred(key_list[22], (BUCKETS, HEADS), (8 / (8 * D * HEADS * HEAD_DIM + 2 * D * FF) ** 0.5), 0.0234375, ((1, 4),), jnp.float32),
        "average_bias": centred(key_list[23], (BUCKETS, HEADS), 0.5, 3.0, ((1, 4),), jnp.float32),
    }


epsilon = 1e-06
momentum_decay = 0.9
average_decay = 0.7
matrix_rate = 10.0
output_rate = 40.0
small_rate = 50.0
group_limits = (0.6, 0.85, 1.2, 1.7)

@jax.custom_vjp
def low(v):
    return lax.optimization_barrier(v.astype(jnp.bfloat16)).astype(jnp.float32)

@jax.custom_vjp
def low_back(v):
    return v

def low_keep(v):
    return (low(v), None)

def low_pass(kept, grad):
    return (grad,)

def back_keep(v):
    return (v, None)

def back_low(kept, grad):
    return (low(grad),)
low.defvjp(low_keep, low_pass)
low_back.defvjp(back_keep, back_low)

def layer(params, rows_in, memory_rows, bucket_ids, keep_mask):
    weights_in, weights_out, weights_up, weights_down, gains, position_bias = params
    highest = lax.Precision.HIGHEST
    proj_in = low(weights_in)
    proj_out = low(weights_out)
    proj_up = low(weights_up)
    proj_down = low(weights_down)

    def normed(residual, which):
        rounded = low(residual)
        scaling = lax.rsqrt(lax.optimization_barrier(jnp.mean(rounded * rounded, -1, keepdims=True)) + epsilon)
        return low(rounded * scaling * gains[which])

    def project(left, right):
        return jnp.dot(left, right, precision=highest)

    def heads(left, right):
        value = project(left, right).reshape(left.shape[0], HEADS, HEAD_DIM)
        return low_back(low(value))

    def attention(queries, key_rows, value_rows, bias_add, keep):
        scores = jnp.einsum('shd,thd->hst', queries, key_rows, precision=highest) * (1.0 / math.sqrt(HEAD_DIM))
        if bias_add is not None:
            scores = jnp.where(keep[None], scores + bias_add, -1000000000.0)
        scores = low_back(scores)
        soft_weights = low(jax.nn.softmax(scores, axis=-1))
        mixture = jnp.einsum('hst,thd->shd', soft_weights, value_rows, precision=highest)
        return low_back(low(mixture)).reshape(queries.shape[0], HEADS * HEAD_DIM)
    first = normed(rows_in, 0)
    bias_add = jnp.transpose(position_bias[bucket_ids], (2, 0, 1))
    self_mix = attention(heads(first, proj_in[0]), heads(first, proj_in[1]), heads(first, proj_in[2]), bias_add, keep_mask > 0)
    middle = rows_in + low_back(project(self_mix, proj_out[0]))
    second = normed(middle, 1)
    memory_low = low(memory_rows)
    cross_mix = attention(heads(second, proj_in[3]), heads(memory_low, proj_in[4]), heads(memory_low, proj_in[5]), None, None)
    late = middle + low_back(project(cross_mix, proj_out[1]))
    third = normed(late, 2)
    hidden = low_back(project(third, proj_up))
    active = low(jax.nn.gelu(hidden))
    return late + low_back(project(active, proj_down))

def stepper(parameter, gradient, momentum, average, step_rate):
    velocity = momentum_decay * momentum + gradient
    updated = parameter - step_rate * (gradient + momentum_decay * velocity)
    averaged = average_decay * average + (1.0 - average_decay) * updated
    return (velocity, averaged, updated)

def reference(tokens, memory, cotangent, buckets, key_mask, task_groups, weights_in, weights_out, weights_up, weights_down, gains, position_bias, momentum_in, average_in, momentum_out, average_out, momentum_up, average_up, momentum_down, average_down, momentum_gain, average_gain, momentum_bias, average_bias):
    wide = jnp.float32
    params = tuple((item.astype(wide) for item in (weights_in, weights_out, weights_up, weights_down, gains, position_bias)))
    bundle = math.gcd(EXAMPLES, 16)

    def blocked(operand):
        return operand.reshape((EXAMPLES // bundle, bundle) + operand.shape[1:])

    def example_grads(tokens_one, memory_one, cotangent_one, bucket_one, keep_one):

        def forward(params_in, rows, memory_rows):
            return layer(params_in, rows, memory_rows, bucket_one, keep_one)
        value, pull = jax.vjp(forward, params, tokens_one, memory_one)
        grads, d_rows, d_memory = pull(cotangent_one)
        return (value, grads, d_rows, d_memory)
    batched = jax.vmap(example_grads)

    def first_pass(carry, items):
        tokens_b, memory_b, cotangent_b, bucket_b, keep_b = items
        value, grads, d_rows, d_memory = batched(tokens_b.astype(wide), memory_b.astype(wide), cotangent_b.astype(wide), bucket_b, keep_b)
        squares = sum((lax.optimization_barrier(jnp.sum(piece * piece, axis=tuple(range(1, piece.ndim)))) for piece in grads))
        return (carry, (value.astype(jnp.bfloat16), d_rows, d_memory, squares))
    blocks_in = (blocked(tokens), blocked(memory), blocked(cotangent), blocked(buckets), blocked(key_mask))
    unused, (output, tokens_grad, memory_grad, squares) = lax.scan(first_pass, jnp.zeros((), wide), blocks_in)
    output = output.reshape(EXAMPLES, SEQ, D)
    tokens_grad = tokens_grad.reshape(EXAMPLES, SEQ, D)
    memory_grad = memory_grad.reshape(EXAMPLES, MEM, D)
    example_norms = jnp.sqrt(squares.reshape(EXAMPLES) + epsilon)
    limits = jnp.asarray(group_limits, wide)[task_groups]
    clip_weights = jnp.minimum(1.0 / jnp.mean(example_norms), limits / example_norms)

    def second_pass(totals, items):
        tokens_b, memory_b, cotangent_b, bucket_b, keep_b, clip_b = items
        value, grads, d_rows, d_memory = batched(tokens_b.astype(wide), memory_b.astype(wide), cotangent_b.astype(wide), bucket_b, keep_b)
        totals = jax.tree.map(lambda running, piece: running + jnp.einsum('e,e...->...', clip_b, piece, precision=lax.Precision.HIGHEST), totals, grads)
        return (totals, None)
    totals, unused_two = lax.scan(second_pass, tuple((jnp.zeros_like(item) for item in params)), blocks_in + (blocked(clip_weights),))
    shrink = 1.0 / math.sqrt(EXAMPLES)
    grads = tuple((item * shrink for item in totals))
    velocity_in, averaged_in, updated_in = stepper(params[0], grads[0], momentum_in, average_in, matrix_rate)
    velocity_out, averaged_out, updated_out = stepper(params[1], grads[1], momentum_out, average_out, output_rate)
    velocity_up, averaged_up, updated_up = stepper(params[2], grads[2], momentum_up, average_up, matrix_rate)
    velocity_down, averaged_down, updated_down = stepper(params[3], grads[3], momentum_down, average_down, matrix_rate)
    velocity_gain, averaged_gain, updated_gain = stepper(params[4], grads[4], momentum_gain, average_gain, small_rate)
    velocity_bias, averaged_bias, updated_bias = stepper(params[5], grads[5], momentum_bias, average_bias, small_rate)
    return (output, tokens_grad, memory_grad, example_norms, velocity_in, averaged_in, updated_in, velocity_out, averaged_out, updated_out, velocity_up, averaged_up, updated_up, velocity_down, averaged_down, updated_down, velocity_gain, averaged_gain, updated_gain, velocity_bias, averaged_bias, updated_bias)
```

```python
import functools
import math

import jax
import jax.numpy as jnp
from jax import lax
from jax.experimental import pallas as pl
from jax.experimental.pallas import tpu as pltpu
from jax.sharding import PartitionSpec as P

epsilon = 1e-06
momentum_decay = 0.9
average_decay = 0.7
matrix_rate = 10.0
output_rate = 40.0
small_rate = 50.0
group_limits = (0.6, 0.85, 1.2, 1.7)
head_dim = 64
quad = 4
quad_width = quad * head_dim
dp_slots = 8
tensor_slots = 4
wide = jnp.float32
narrow = jnp.bfloat16
vmem_bytes = 58 * 2**20

core = ("tensor", 1)
row = ("tensor", 2)
side = ("dp", 1)
near = ("dp", 2)
far = ("dp", 4)
gather_orders = ((row, near, far, side, core), (row, side, near, far, core))
reduce_orders = (
    (core, side, row, near, far),
    (core, row, side, near, far),
    (core, near, far, side, row),
    (core, side, near, far, row),
)


def dot_nn(left, right):
    return lax.dot_general(left, right, (((1,), (0,)), ((), ())), preferred_element_type=wide)


def dot_nt(left, right):
    return lax.dot_general(left, right, (((1,), (1,)), ((), ())), preferred_element_type=wide)


def dot_tn(left, right):
    return lax.dot_general(left, right, (((0,), (0,)), ((), ())), preferred_element_type=wide)


def head_masks(dtype):
    lanes = lax.broadcasted_iota(jnp.int32, (1, quad_width), 1) // head_dim
    return [(lanes == head).astype(wide).astype(dtype) for head in range(quad)]


def stack_heads(block, masks):
    return jnp.concatenate([block * mask for mask in masks], 0)


def unstack_heads(block, masks):
    rows = block.shape[0] // quad
    total = block[:rows] * masks[0]
    for head in range(1, quad):
        total = total + block[head * rows : (head + 1) * rows] * masks[head]
    return total


def norm_scale(rows):
    return lax.rsqrt(jnp.mean(rows * rows, -1, keepdims=True) + epsilon)


def norm_back(rows, gain, d_normed):
    scaling = norm_scale(rows)
    weighted = d_normed * gain
    cubed = scaling * scaling * scaling
    d_rows = scaling * weighted - rows * cubed * jnp.mean(rows * weighted, -1, keepdims=True)
    return d_rows, d_normed * rows * scaling


def softmax_keys(scores):
    peak = jnp.max(scores, 0, keepdims=True)
    weights = jnp.exp(scores - peak)
    return weights * (1.0 / jnp.sum(weights, 0, keepdims=True))


def gram_squares(left, right_grams):
    return jnp.sum(dot_nt(left, left) * right_grams, 0, keepdims=True)


def fold_lanes(row_sums):
    width = row_sums.shape[1]
    total = row_sums[:, :128]
    for start in range(128, width, 128):
        total = total + row_sums[:, start : start + 128]
    return total


def slot_places(order, first_is_high):
    places = []
    count = len(order)
    for slot in range(1 << count):
        index = {"dp": 0, "tensor": 0}
        for stage, (axis, bit) in enumerate(order):
            place = count - 1 - stage if first_is_high else stage
            if (slot >> place) & 1:
                index[axis] |= bit
        places.append((index["dp"], index["tensor"]))
    return places


def start_weights(info, pieces, plans, held, sems):
    me_dp, me_tensor = info[0], info[1]
    for piece, (first, count, places), sem in zip(pieces, plans, sems):
        for slot, (dp_index, tensor_index) in enumerate(places):
            high = pl.multiple_of((dp_index ^ me_dp) * 64, 64)
            left = pl.multiple_of((tensor_index ^ me_tensor) * 128, 128)
            pltpu.make_async_copy(
                piece.at[slot],
                held.at[pl.ds(first, count), pl.ds(high, 64), pl.ds(left, 128)],
                sem,
            ).start()


def wait_weights(plans, held, sems):
    for (first, count, places), sem in zip(plans, sems):
        whole = held.at[pl.ds(first, count)]
        pltpu.make_async_copy(whole, whole, sem).wait()


def place_rows(info, parts, held):
    rows = parts[0].shape[1]
    for index, part in enumerate(parts):
        start = pl.multiple_of((info[2] ^ index) * rows, rows)
        held[:, pl.ds(start, rows), :] = part[...]


def split_rows(info, held, parts):
    rows = parts[0].shape[1]
    for index, part in enumerate(parts):
        start = pl.multiple_of((info[2] ^ index) * rows, rows)
        part[...] = held[:, pl.ds(start, rows), :].astype(part.dtype)


def self_forward_kernel(shards, plans, heads_local, *refs):
    refs = list(refs)

    def take(count):
        taken = refs[:count]
        del refs[:count]
        return taken

    (info,) = take(1)
    parts = take(shards)
    buckets, key_mask, gains, table = take(4)
    pieces = take(len(plans))
    rows_out, normed_out, qkv_out, weights_out, mix_out, mid_out = take(6)
    held, sems, rows_held, mix_held = take(4)
    sem_list = [sems.at[index] for index in range(len(plans))]

    @pl.when(pl.program_id(0) == 0)
    def _():
        start_weights(info, pieces, plans, held, sem_list)
        wait_weights(plans, held, sem_list)

    masks = head_masks(narrow)
    masks_wide = head_masks(wide)
    place_rows(info, parts, rows_held)
    rows_out[...] = rows_held[...]
    bundle, seq, width = rows_held.shape
    flat = rows_held[...].reshape(bundle * seq, width).astype(wide)
    normed = (flat * norm_scale(flat) * gains[0:1, :]).astype(narrow)
    normed_out[...] = normed.reshape(bundle, seq, width)
    for index in range(3):
        value = dot_nn(normed, held[index]).astype(narrow)
        qkv_out[index] = value.reshape(bundle, seq, width)
    for example in range(bundle):
        code = jnp.where(key_mask[example] > 0, buckets[example], -1).T
        safe = jnp.maximum(code, 0)
        code_all = jnp.concatenate([code] * quad, 1)
        for group in range(width // quad_width):
            columns = slice(group * quad_width, (group + 1) * quad_width)
            bias = []
            for head in range(group * quad, (group + 1) * quad):
                spot = ((head // heads_local) ^ info[2]) * heads_local + head % heads_local
                line = jnp.broadcast_to(table[pl.ds(spot, 1), :], (seq, 128))
                bias.append(jnp.take_along_axis(line, safe, axis=1))
            queries = stack_heads(qkv_out[0, example, :, columns], masks)
            scores = dot_nt(qkv_out[1, example, :, columns], queries) * (
                1.0 / math.sqrt(head_dim)
            ) + jnp.concatenate(bias, 1)
            weights = softmax_keys(jnp.where(code_all >= 0, scores, -1000000000.0))
            weights_out[example, group] = weights
            mixture = dot_tn(weights.astype(narrow), qkv_out[2, example, :, columns])
            mix_held[example, :, columns] = unstack_heads(mixture, masks_wide).astype(narrow)
    mix_out[...] = mix_held[...]
    mix = mix_held[...].reshape(bundle * seq, width)
    mid_out[...] = (flat + dot_nt(mix, held[3])).reshape(bundle, seq, width)


def cross_kernel(shards, plans, *refs):
    refs = list(refs)

    def take(count):
        taken = refs[:count]
        del refs[:count]
        return taken

    (info,) = take(1)
    memory_parts = take(shards)
    cotangent_parts = take(shards)
    mid_in, gains = take(2)
    pieces = take(len(plans))
    output_parts = take(shards)
    memory_grads = take(shards)
    (
        early_out,
        normed_b_out,
        d_query_out,
        d_keys_out,
        d_values_out,
        mix_out,
        d_mid_out,
        normed_c_out,
        d_hidden_out,
        active_out,
        d_top_out,
        d_gain_b_out,
        d_gain_c_out,
        squares_out,
    ) = take(14)
    held, sems, memory_held, keys_held, values_held, weights_held, rows_held, query_held = take(8)
    sem_list = [sems.at[index] for index in range(len(plans))]

    @pl.when(pl.program_id(0) == 0)
    def _():
        start_weights(info, pieces, plans, held, sem_list)
        wait_weights(plans, held, sem_list)

    masks = head_masks(narrow)
    masks_wide = head_masks(wide)
    scaling = 1.0 / math.sqrt(head_dim)
    bundle, seq, width = mid_in.shape
    memory_rows = memory_parts[0].shape[1]
    memory_len = memory_held.shape[1]
    groups = width // quad_width

    def flatten(block):
        return block.reshape(block.shape[0] * block.shape[1], block.shape[2])

    def unflatten(block):
        return block.reshape(bundle, block.shape[0] // bundle, block.shape[1])

    for index, part in enumerate(memory_parts):
        memory_held[:, index * memory_rows : (index + 1) * memory_rows, :] = part[...]
    place_rows(info, cotangent_parts, d_top_out)
    mid = flatten(mid_in[...])
    rows_b = mid.astype(narrow).astype(wide)
    normed_b = (rows_b * norm_scale(rows_b) * gains[1:2, :]).astype(narrow)
    normed_b_out[...] = unflatten(normed_b)
    query_held[...] = unflatten(dot_nn(normed_b, held[0]).astype(narrow))
    memory_flat = flatten(memory_held[...])
    keys_held[...] = unflatten(dot_nn(memory_flat, held[1]).astype(narrow))
    values_held[...] = unflatten(dot_nn(memory_flat, held[2]).astype(narrow))
    for example in range(bundle):
        for group in range(groups):
            columns = slice(group * quad_width, (group + 1) * quad_width)
            queries = stack_heads(query_held[example, :, columns], masks)
            scores = dot_nt(keys_held[example, :, columns], queries) * scaling
            weights = softmax_keys(scores)
            weights_held[example, group] = weights
            mixture = dot_tn(weights.astype(narrow), values_held[example, :, columns])
            mix_out[example, :, columns] = unstack_heads(mixture, masks_wide).astype(narrow)
    late = mid + dot_nt(flatten(mix_out[...]), held[3])
    rows_c = late.astype(narrow).astype(wide)
    normed_c = (rows_c * norm_scale(rows_c) * gains[2:3, :]).astype(narrow)
    normed_c_out[...] = unflatten(normed_c)
    d_top = flatten(d_top_out[...])
    total = late
    d_normed = jnp.zeros((bundle * seq, width), wide)
    up_grams = [jnp.zeros((seq, seq), wide) for _ in range(bundle)]
    down_grams = [jnp.zeros((seq, seq), wide) for _ in range(bundle)]
    slope = math.sqrt(2.0 / math.pi)
    for index in range(4):
        hidden = dot_nn(normed_c, held[4 + index])
        square = hidden * hidden
        bend = jnp.tanh(slope * hidden * (1.0 + 0.044715 * square))
        half = 0.5 * (1.0 + bend)
        active = (hidden * half).astype(narrow)
        steep = half + 0.5 * hidden * (1.0 - bend * bend) * (
            slope * (1.0 + (3.0 * 0.044715) * square)
        )
        total = total + dot_nt(active, held[8 + index])
        d_hidden = (dot_nn(d_top, held[8 + index]) * steep).astype(narrow)
        d_normed = d_normed + dot_nt(d_hidden, held[4 + index])
        active_out[index] = unflatten(active)
        d_hidden_out[index] = unflatten(d_hidden)
        for example in range(bundle):
            span = slice(example * seq, (example + 1) * seq)
            up_grams[example] += dot_nt(d_hidden[span], d_hidden[span])
            down_grams[example] += dot_nt(active[span], active[span])
    rows_held[...] = unflatten(total)
    split_rows(info, rows_held, output_parts)
    d_rows, d_gain_rows = norm_back(rows_c, gains[2:3, :], d_normed)
    d_gain_c = jnp.sum(unflatten(d_gain_rows), 1, keepdims=True)
    d_gain_c_out[...] = d_gain_c
    d_mid = d_top.astype(wide) + d_rows
    d_mid_low = d_mid.astype(narrow)
    d_mid_out[...] = unflatten(d_mid_low)
    d_mix = dot_nn(d_mid_low, held[3]).astype(narrow)
    squares = []
    for example in range(bundle):
        span = slice(example * seq, (example + 1) * seq)
        for group in range(groups):
            columns = slice(group * quad_width, (group + 1) * quad_width)
            keys = keys_held[example, :, columns]
            queries = stack_heads(query_held[example, :, columns], masks)
            d_mixes = stack_heads(d_mix[span, columns], masks)
            weights = weights_held[example, group]
            d_weights = dot_nt(values_held[example, :, columns], d_mixes)
            inner = jnp.sum(weights * d_weights, 0, keepdims=True)
            d_scores = (weights * (d_weights - inner)).astype(narrow)
            d_query_out[example, :, columns] = (
                unstack_heads(dot_tn(d_scores, keys), masks_wide) * scaling
            ).astype(narrow)
            d_keys_out[example, :, columns] = (dot_nn(d_scores, queries) * scaling).astype(narrow)
            d_values_out[example, :, columns] = dot_nn(weights.astype(narrow), d_mixes).astype(
                narrow
            )
        memory_grad = dot_nt(d_keys_out[example], held[1]) + dot_nt(d_values_out[example], held[2])
        for index, part in enumerate(memory_grads):
            part[example] = memory_grad[
                index * memory_rows : (index + 1) * memory_rows
            ].astype(part.dtype)
        d_query = d_query_out[example]
        mix = mix_out[example]
        square_sum = gram_squares(normed_b[span], dot_nt(d_query, d_query))
        square_sum += gram_squares(mix, dot_nt(d_mid_low[span], d_mid_low[span]))
        square_sum += gram_squares(normed_c[span], up_grams[example])
        square_sum += gram_squares(d_top[span], down_grams[example])
        for block in (d_keys_out, d_values_out):
            product = dot_tn(memory_held[example], block[example])
            square_sum += fold_lanes(jnp.sum(product * product, 0, keepdims=True))
        square_sum += fold_lanes(d_gain_c[example] * d_gain_c[example])
        squares.append(square_sum)
    d_normed_b = dot_nt(flatten(d_query_out[...]), held[0])
    d_rows_b, d_gain_rows = norm_back(rows_b, gains[1:2, :], d_normed_b)
    d_gain_b = jnp.sum(unflatten(d_gain_rows), 1, keepdims=True)
    d_gain_b_out[...] = d_gain_b
    for example in range(bundle):
        squares_out[example] = squares[example] + fold_lanes(
            d_gain_b[example] * d_gain_b[example]
        )
    early_out[...] = unflatten(d_mid + d_rows_b)


def self_backward_kernel(shards, plans, *refs):
    refs = list(refs)

    def take(count):
        taken = refs[:count]
        del refs[:count]
        return taken

    info, early_in, rows_in, normed_in, qkv_in, weights_in, mix_in = take(7)
    squares_in, buckets, gains = take(3)
    pieces = take(len(plans))
    tokens_grads = take(shards)
    d_qkv_out, d_early_out, d_gain_out, d_bias_out, squares_out = take(5)
    held, sems, rows_held = take(3)
    sem_list = [sems.at[index] for index in range(len(plans))]

    @pl.when(pl.program_id(0) == 0)
    def _():
        start_weights(info, pieces, plans, held, sem_list)
        wait_weights(plans, held, sem_list)

    masks = head_masks(narrow)
    masks_wide = head_masks(wide)
    scaling = 1.0 / math.sqrt(head_dim)
    bundle, seq, width = early_in.shape
    groups = width // quad_width
    bucket_count = d_bias_out.shape[2]

    def flatten(block):
        return block.reshape(block.shape[0] * block.shape[1], block.shape[2])

    def unflatten(block):
        return block.reshape(bundle, block.shape[0] // bundle, block.shape[1])

    early = flatten(early_in[...])
    d_early = early.astype(narrow)
    d_early_out[...] = unflatten(d_early)
    d_mix = dot_nn(d_early, held[3]).astype(narrow)
    squares = []
    for example in range(bundle):
        span = slice(example * seq, (example + 1) * seq)
        code = buckets[example].T
        for group in range(groups):
            columns = slice(group * quad_width, (group + 1) * quad_width)
            keys = qkv_in[1, example, :, columns]
            queries = stack_heads(qkv_in[0, example, :, columns], masks)
            d_mixes = stack_heads(d_mix[span, columns], masks)
            weights = weights_in[example, group]
            d_weights = dot_nt(qkv_in[2, example, :, columns], d_mixes)
            inner = jnp.sum(weights * d_weights, 0, keepdims=True)
            d_scores = (weights * (d_weights - inner)).astype(narrow)
            d_qkv_out[0, example, :, columns] = (
                unstack_heads(dot_tn(d_scores, keys), masks_wide) * scaling
            ).astype(narrow)
            d_qkv_out[1, example, :, columns] = (dot_nn(d_scores, queries) * scaling).astype(
                narrow
            )
            d_qkv_out[2, example, :, columns] = dot_nn(weights.astype(narrow), d_mixes).astype(
                narrow
            )
            d_wide = d_scores.astype(wide)
            for bucket in range(bucket_count):
                chosen = code == bucket
                for head in range(quad):
                    picked = jnp.where(chosen, d_wide[:, head * seq : (head + 1) * seq], 0.0)
                    d_bias_out[example, group * quad + head, pl.ds(bucket, 1), :] = jnp.sum(
                        picked, 0, keepdims=True
                    )
        grams = jnp.zeros((seq, seq), wide)
        for index in range(3):
            block = d_qkv_out[index, example]
            grams = grams + dot_nt(block, block)
        square_sum = gram_squares(normed_in[example], grams)
        square_sum += gram_squares(mix_in[example], dot_nt(d_early[span], d_early[span]))
        squares.append(square_sum)
    d_normed = dot_nt(flatten(d_qkv_out[0]), held[0])
    d_normed = d_normed + dot_nt(flatten(d_qkv_out[1]), held[1])
    d_normed = d_normed + dot_nt(flatten(d_qkv_out[2]), held[2])
    d_rows, d_gain_rows = norm_back(flatten(rows_in[...]).astype(wide), gains[0:1, :], d_normed)
    d_gain = jnp.sum(unflatten(d_gain_rows), 1, keepdims=True)
    d_gain_out[...] = d_gain
    for example in range(bundle):
        squares_out[example] = (
            squares[example]
            + squares_in[example]
            + fold_lanes(d_gain[example] * d_gain[example])
        )
    rows_held[...] = unflatten(early + d_rows)
    split_rows(info, rows_held, tokens_grads)


def pair_gradient_kernel(layouts, places, bundle_sizes, *refs):
    refs = list(refs)

    def take(count):
        taken = refs[:count]
        del refs[:count]
        return taken

    info, clip = take(2)
    unit_refs = [(take(lefts), take(rights)) for lefts, rights in layouts]
    out, scaled, tile = refs
    me_dp, me_tensor = info[0], info[1]
    for unit, (lefts, rights) in enumerate(unit_refs):
        total = None
        example = 0
        for left, right in zip(lefts, rights):
            count = left.shape[0]
            for index in range(count):
                scaled[index] = (left[index].astype(wide) * clip[example + index]).astype(narrow)
            example += count
            block = dot_tn(
                scaled[0:count].reshape(count * left.shape[1], left.shape[2]),
                right[...].reshape(count * left.shape[1], right.shape[-1]),
            )
            total = block if total is None else total + block
        tile[...] = total.astype(narrow)
        for slot, (dp_index, tensor_index) in enumerate(places):
            high = pl.multiple_of((dp_index ^ me_dp) * 64, 64)
            left_edge = pl.multiple_of((tensor_index ^ me_tensor) * 128, 128)
            out[slot, unit] = tile[pl.ds(high, 64), pl.ds(left_edge, 128)]


def memory_gradient_kernel(shards, chunks, places, steps, *refs):
    refs = list(refs)

    def take(count):
        taken = refs[:count]
        del refs[:count]
        return taken

    info, clip = take(2)
    memory_parts = [take(shards) for _ in range(chunks)]
    d_keys = take(chunks)
    d_values = take(chunks)
    out, scaled, total, tile = refs
    me_dp, me_tensor = info[0], info[1]
    step = pl.program_id(0)

    @pl.when(step == 0)
    def _():
        total[...] = jnp.zeros_like(total)

    for chunk in range(chunks):

        @pl.when(step // steps == chunk)
        def _(chunk=chunk):
            factor = clip[step]
            for index, part in enumerate(memory_parts[chunk]):
                rows = part.shape[1]
                scaled[index * rows : (index + 1) * rows, :] = (
                    part[0].astype(wide) * factor
                ).astype(narrow)
            total[0] += dot_tn(scaled[...], d_keys[chunk][0])
            total[1] += dot_tn(scaled[...], d_values[chunk][0])

    @pl.when(step == steps * chunks - 1)
    def _():
        for unit in range(2):
            tile[...] = total[unit].astype(narrow)
            for slot, (dp_index, tensor_index) in enumerate(places):
                high = pl.multiple_of((dp_index ^ me_dp) * 64, 64)
                left_edge = pl.multiple_of((tensor_index ^ me_tensor) * 128, 128)
                out[slot, unit] = tile[pl.ds(high, 64), pl.ds(left_edge, 128)]


def swap(value, axis, bit):
    size = lax.axis_size(axis)
    return lax.ppermute(value, axis, [(index, index ^ bit) for index in range(size)])


def gather_slots(shard, order):
    gathered = shard[None]
    for axis, bit in order:
        gathered = jnp.concatenate([gathered, swap(gathered, axis, bit)], 0)
    return gathered


def reduce_slots(slots, order):
    for axis, bit in order:
        half = slots.shape[0] // 2
        arrived = swap(slots[half:], axis, bit)
        slots = (slots[:half].astype(wide) + arrived.astype(wide)).astype(narrow)
    return slots[0]


def sum_everywhere(value):
    for axis in ("tensor", "dp"):
        bit = 1
        while bit < lax.axis_size(axis):
            value = value + swap(value, axis, bit)
            bit *= 2
    return value


def stepper(parameter, gradient, momentum, average, step_rate):
    velocity = momentum_decay * momentum + gradient
    updated = parameter - step_rate * (gradient + momentum_decay * velocity)
    averaged = average_decay * average + (1.0 - average_decay) * updated
    return (velocity, averaged, updated)


def on_device(
    tokens,
    memory,
    cotangent,
    buckets,
    key_mask,
    task_groups,
    weights_in,
    weights_out,
    weights_up,
    weights_down,
    gains,
    position_bias,
    momentum_in,
    average_in,
    momentum_out,
    average_out,
    momentum_up,
    average_up,
    momentum_down,
    average_down,
    momentum_gain,
    average_gain,
    momentum_bias,
    average_bias,
):
    shards = lax.axis_size("tensor")
    replicas = lax.axis_size("dp")
    me_tensor = lax.axis_index("tensor")
    me_dp = lax.axis_index("dp")
    width = tokens.shape[2]
    seq = buckets.shape[1]
    seq_rows = tokens.shape[1]
    memory_rows = memory.shape[1]
    memory_len = memory_rows * shards
    group_count = tokens.shape[0]
    local = group_count // shards
    chunks = 2 if local % 2 == 0 else 1
    per_chunk = local // chunks
    bundle = 2 if per_chunk % 2 == 0 else 1
    steps = per_chunk // bundle
    bucket_count, heads_local = position_bias.shape
    heads = heads_local * shards
    gain_width = momentum_gain.shape[1]
    staged = shards == tensor_slots and replicas == dp_slots

    slot_base = [me_dp, me_tensor] if staged else [0 * me_dp, 0 * me_tensor]
    kernel_info = jnp.stack(slot_base + [me_tensor]).astype(jnp.int32)

    def square_shards():
        high, across = weights_in.shape[1], weights_in.shape[2]
        split = lambda block: block.reshape(high, -1, across).transpose(1, 0, 2)
        return (
            weights_in.astype(narrow),
            weights_out.astype(narrow).transpose(0, 2, 1),
            split(weights_up.astype(narrow)),
            split(weights_down.astype(narrow).T),
        )

    shard_in, shard_out, shard_up, shard_down = square_shards()

    def gather_group(blocks):
        count = blocks.shape[0]
        if staged:
            half = count // 2
            pieces = [
                gather_slots(blocks[:half], gather_orders[0]),
                gather_slots(blocks[half:], gather_orders[1]),
            ]
            plans = [
                (0, half, slot_places(gather_orders[0], False)),
                (half, count - half, slot_places(gather_orders[1], False)),
            ]
            return pieces, plans
        whole = lax.all_gather(blocks, "dp", axis=1, tiled=True)
        whole = lax.all_gather(whole, "tensor", axis=2, tiled=True)
        whole = whole.reshape(count, dp_slots, 64, tensor_slots, 128).transpose(1, 3, 0, 2, 4)
        whole = whole.reshape(dp_slots * tensor_slots, count, 64, 128)
        places = [(slot // tensor_slots, slot % tensor_slots) for slot in range(32)]
        return [whole], [(0, count, places)]

    def exchange(value, start, count):
        found = []
        for index in range(shards):
            first = (me_tensor ^ index) * local + start
            block = lax.dynamic_slice_in_dim(value, first, count, 0)
            found.append(swap(block, "tensor", index) if index else block)
        return found

    table = jnp.pad(position_bias.T, ((0, 0), (0, 128 - bucket_count)))
    table_all = jnp.concatenate(
        [swap(table, "tensor", index) if index else table for index in range(shards)], 0
    )
    self_pieces, self_plans = gather_group(jnp.concatenate([shard_in[:3], shard_out[:1]], 0))
    token_parts = exchange(tokens, 0, local)
    cross_pieces, cross_plans = gather_group(jnp.concatenate([shard_in[3:6], shard_out[1:2]], 0))
    inner_pieces, inner_plans = gather_group(jnp.concatenate([shard_up, shard_down], 0))
    cross_pieces = cross_pieces + inner_pieces
    cross_plans = cross_plans + [
        (first + 4, count, places) for first, count, places in inner_plans
    ]
    memory_parts = [exchange(memory, chunk * per_chunk, per_chunk) for chunk in range(chunks)]
    cotangent_parts = exchange(cotangent, 0, local)
    bucket_mine = lax.dynamic_slice_in_dim(buckets, me_tensor * local, local, 0)
    mask_mine = lax.dynamic_slice_in_dim(key_mask, me_tensor * local, local, 0)
    groups_mine = lax.dynamic_slice_in_dim(task_groups, me_tensor * local, local, 0)

    smem = pl.BlockSpec(memory_space=pltpu.SMEM)
    anywhere = pl.BlockSpec(memory_space=pl.ANY)
    params = pltpu.CompilerParams(
        vmem_limit_bytes=vmem_bytes, dimension_semantics=("arbitrary",)
    )

    def part_spec(shape, offset=0, lead=None):
        rest = tuple(shape)
        zeros = (0,) * len(rest)
        if lead is None:
            return pl.BlockSpec((bundle,) + rest, lambda step: (step + offset,) + zeros)
        return pl.BlockSpec((lead, bundle) + rest, lambda step: (0, step + offset) + zeros)

    def whole_spec(shape):
        return pl.BlockSpec(tuple(shape), lambda step: (0,) * len(shape))

    def shaped(shape, dtype, lead=None):
        front = (per_chunk,) if lead is None else (lead, per_chunk)
        return jax.ShapeDtypeStruct(front + tuple(shape), dtype)

    groups = width // quad_width
    row_block = (seq, width)

    def self_forward(chunk):
        offset = chunk * steps
        kernel = functools.partial(self_forward_kernel, shards, self_plans, heads_local)
        return pl.pallas_call(
            kernel,
            grid=(steps,),
            in_specs=[smem]
            + [part_spec((seq_rows, width), offset)] * shards
            + [part_spec((seq, seq), offset)] * 2
            + [whole_spec(gains.shape), whole_spec(table_all.shape)]
            + [anywhere] * len(self_pieces),
            out_specs=[
                part_spec(row_block),
                part_spec(row_block),
                part_spec(row_block, lead=3),
                part_spec((groups, seq, quad * seq)),
                part_spec(row_block),
                part_spec(row_block),
            ],
            out_shape=[
                shaped(row_block, narrow),
                shaped(row_block, narrow),
                shaped(row_block, narrow, 3),
                shaped((groups, seq, quad * seq), wide),
                shaped(row_block, narrow),
                shaped(row_block, wide),
            ],
            scratch_shapes=[
                pltpu.VMEM((4, width, width), narrow),
                pltpu.SemaphoreType.DMA((len(self_pieces),)),
                pltpu.VMEM((bundle,) + row_block, narrow),
                pltpu.VMEM((bundle,) + row_block, narrow),
            ],
            compiler_params=params,
            name="self_forward",
            cost_estimate=pl.CostEstimate(
                flops=per_chunk * 400_000_000, bytes_accessed=per_chunk * 2_000_000, transcendentals=0
            ),
        )(
            kernel_info,
            *token_parts,
            bucket_mine,
            mask_mine,
            gains,
            table_all,
            *self_pieces,
        )

    def cross(chunk, mid):
        offset = chunk * steps
        kernel = functools.partial(cross_kernel, shards, cross_plans)
        gain_block = (1, width)
        return pl.pallas_call(
            kernel,
            grid=(steps,),
            in_specs=[smem]
            + [part_spec((memory_rows, width))] * shards
            + [part_spec((seq_rows, width), offset)] * shards
            + [part_spec(row_block), whole_spec(gains.shape)]
            + [anywhere] * len(cross_pieces),
            out_specs=[part_spec((seq_rows, width))] * shards
            + [part_spec((memory_rows, width))] * shards
            + [
                part_spec(row_block),
                part_spec(row_block),
                part_spec(row_block),
                part_spec((memory_len, width)),
                part_spec((memory_len, width)),
                part_spec(row_block),
                part_spec(row_block),
                part_spec(row_block),
                part_spec(row_block, lead=4),
                part_spec(row_block, lead=4),
                part_spec(row_block),
                part_spec(gain_block),
                part_spec(gain_block),
                part_spec((1, 128)),
            ],
            out_shape=[shaped((seq_rows, width), narrow)] * shards
            + [shaped((memory_rows, width), narrow if index else wide) for index in range(shards)]
            + [
                shaped(row_block, wide),
                shaped(row_block, narrow),
                shaped(row_block, narrow),
                shaped((memory_len, width), narrow),
                shaped((memory_len, width), narrow),
                shaped(row_block, narrow),
                shaped(row_block, narrow),
                shaped(row_block, narrow),
                shaped(row_block, narrow, 4),
                shaped(row_block, narrow, 4),
                shaped(row_block, narrow),
                shaped(gain_block, wide),
                shaped(gain_block, wide),
                shaped((1, 128), wide),
            ],
            scratch_shapes=[
                pltpu.VMEM((12, width, width), narrow),
                pltpu.SemaphoreType.DMA((len(cross_pieces),)),
                pltpu.VMEM((bundle, memory_len, width), narrow),
                pltpu.VMEM((bundle, memory_len, width), narrow),
                pltpu.VMEM((bundle, memory_len, width), narrow),
                pltpu.VMEM((bundle, groups, memory_len, quad * seq), wide),
                pltpu.VMEM((bundle,) + row_block, wide),
                pltpu.VMEM((bundle,) + row_block, narrow),
            ],
            compiler_params=params,
            name="cross",
            cost_estimate=pl.CostEstimate(
                flops=per_chunk * 8_000_000_000, bytes_accessed=per_chunk * 6_000_000, transcendentals=0
            ),
        )(kernel_info, *memory_parts[chunk], *cotangent_parts, mid, gains, *cross_pieces)

    def self_backward(chunk, early, rows, normed, qkv, weights, mix, squares):
        offset = chunk * steps
        kernel = functools.partial(self_backward_kernel, shards, self_plans)
        return pl.pallas_call(
            kernel,
            grid=(steps,),
            in_specs=[
                smem,
                part_spec(row_block),
                part_spec(row_block),
                part_spec(row_block),
                part_spec(row_block, lead=3),
                part_spec((groups, seq, quad * seq)),
                part_spec(row_block),
                part_spec((1, 128)),
                part_spec((seq, seq), offset),
                whole_spec(gains.shape),
            ]
            + [anywhere] * len(self_pieces),
            out_specs=[part_spec((seq_rows, width))] * shards
            + [
                part_spec(row_block, lead=3),
                part_spec(row_block),
                part_spec((1, width)),
                part_spec((heads, bucket_count, 128)),
                part_spec((1, 128)),
            ],
            out_shape=[
                shaped((seq_rows, width), narrow if index else wide) for index in range(shards)
            ]
            + [
                shaped(row_block, narrow, 3),
                shaped(row_block, narrow),
                shaped((1, width), wide),
                shaped((heads, bucket_count, 128), wide),
                shaped((1, 128), wide),
            ],
            scratch_shapes=[
                pltpu.VMEM((4, width, width), narrow),
                pltpu.SemaphoreType.DMA((len(self_pieces),)),
                pltpu.VMEM((bundle,) + row_block, wide),
            ],
            compiler_params=params,
            name="self_backward",
            cost_estimate=pl.CostEstimate(
                flops=per_chunk * 1_500_000_000, bytes_accessed=per_chunk * 3_000_000, transcendentals=0
            ),
        )(
            kernel_info,
            early,
            rows,
            normed,
            qkv,
            weights,
            mix,
            squares,
            bucket_mine,
            gains,
            *self_pieces,
        )

    span = range(chunks)
    first = [self_forward(chunk) for chunk in span]
    second = [cross(chunk, first[chunk][5]) for chunk in span]
    third = []
    for chunk in span:
        rows, normed, qkv, weights, mix, mid = first[chunk]
        tail = second[chunk][2 * shards :]
        third.append(self_backward(chunk, tail[0], rows, normed, qkv, weights, mix, tail[13]))

    def give_back(blocks_of, dtype, rows):
        whole = jnp.zeros((group_count, rows, width), dtype)
        for chunk in span:
            for index, block in enumerate(blocks_of(chunk)):
                arrived = swap(block, "tensor", index) if index else block
                place = (me_tensor ^ index) * local + chunk * per_chunk
                whole = lax.dynamic_update_slice_in_dim(whole, arrived.astype(dtype), place, 0)
        return whole

    output = give_back(lambda chunk: second[chunk][:shards], narrow, seq_rows)
    memory_grad = give_back(lambda chunk: second[chunk][shards : 2 * shards], wide, memory_rows)
    tokens_grad = give_back(lambda chunk: third[chunk][:shards], wide, seq_rows)

    tails = [second[chunk][2 * shards :] for chunk in span]
    ends = [third[chunk][shards:] for chunk in span]

    def joined(pieces):
        return jnp.concatenate(pieces, 0)

    grad_bias = jnp.sum(joined([end[3] for end in ends]), -1)
    squares = jnp.sum(joined([end[4] for end in ends]), (1, 2)) + jnp.sum(
        grad_bias * grad_bias, (1, 2)
    )
    norms_mine = jnp.sqrt(squares + epsilon)
    norm_total = sum_everywhere(jnp.full((8, 128), jnp.sum(norms_mine)))[0, 0]
    mean_norm = norm_total / (group_count * replicas)
    norm_parts = jnp.zeros((group_count,), wide)
    padded = jnp.broadcast_to(norms_mine[:, None], (local, 128))
    for index in range(shards):
        arrived = swap(padded, "tensor", index) if index else padded
        norm_parts = lax.dynamic_update_slice_in_dim(
            norm_parts, arrived[:, 0], (me_tensor ^ index) * local, 0
        )
    example_norms = norm_parts
    limits = jnp.sum(
        (groups_mine[:, None] == jnp.arange(len(group_limits), dtype=jnp.int32))
        * jnp.asarray(group_limits, wide),
        1,
    )
    clip_weights = jnp.minimum(1.0 / mean_norm, limits / norms_mine)

    grad_gain = jnp.concatenate(
        [
            joined([end[2] for end in ends]),
            joined([tail[11] for tail in tails]),
            joined([tail[12] for tail in tails]),
        ],
        1,
    )
    sum_gain = jnp.sum(clip_weights[:, None, None] * grad_gain, 0)
    sum_bias = jnp.sum(clip_weights[:, None, None] * grad_bias, 0)
    small = jnp.concatenate([sum_gain.reshape(-1), sum_bias.reshape(-1)])
    small = lax.psum(small.reshape(-1, 128), ("dp", "tensor")).reshape(-1)
    gain_total = small[: 3 * width].reshape(3, width)
    bias_total = small[3 * width :].reshape(heads, bucket_count).T

    slot_count = dp_slots * tensor_slots

    def places_of(order):
        if staged:
            return slot_places(order, True)
        return [(slot // tensor_slots, slot % tensor_slots) for slot in range(slot_count)]

    def pair_gradient(order, units):
        layouts = [(len(lefts), len(rights)) for lefts, rights, lead in units]
        operands, specs = [], []
        for lefts, rights, lead in units:
            for block in lefts:
                operands.append(block)
                specs.append(pl.BlockSpec(memory_space=pltpu.VMEM))
            for block in rights:
                operands.append(block)
                if lead is None:
                    specs.append(pl.BlockSpec(memory_space=pltpu.VMEM))
                else:
                    specs.append(
                        pl.BlockSpec(
                            (None,) + block.shape[1:], lambda step, lead=lead: (lead, 0, 0, 0)
                        )
                    )
        specs = [
            whole_spec(block.shape) if spec.memory_space is pltpu.VMEM else spec
            for block, spec in zip(operands, specs)
        ]
        return pl.pallas_call(
            functools.partial(pair_gradient_kernel, layouts, places_of(order), per_chunk),
            grid=(1,),
            in_specs=[smem, smem] + specs,
            out_specs=whole_spec((slot_count, 2, 64, 128)),
            out_shape=jax.ShapeDtypeStruct((slot_count, 2, 64, 128), narrow),
            scratch_shapes=[
                pltpu.VMEM((per_chunk, seq, width), narrow),
                pltpu.VMEM((width, width), narrow),
            ],
            compiler_params=params,
            name="pair_gradient",
            cost_estimate=pl.CostEstimate(
                flops=2_000_000_000, bytes_accessed=5_000_000, transcendentals=0
            ),
        )(kernel_info, clip_weights, *operands)

    def memory_gradient(order):
        def example_spec(rows, chunk):
            return pl.BlockSpec(
                (1, rows, width),
                lambda step: (jnp.clip(step - chunk * per_chunk, 0, per_chunk - 1), 0, 0),
            )

        operands, specs = [], []
        for chunk in span:
            for block in memory_parts[chunk]:
                operands.append(block)
                specs.append(example_spec(memory_rows, chunk))
        for place in (3, 4):
            for chunk in span:
                operands.append(tails[chunk][place])
                specs.append(example_spec(memory_len, chunk))
        return pl.pallas_call(
            functools.partial(
                memory_gradient_kernel, shards, chunks, places_of(order), per_chunk
            ),
            grid=(local,),
            in_specs=[smem, smem] + specs,
            out_specs=whole_spec((slot_count, 2, 64, 128)),
            out_shape=jax.ShapeDtypeStruct((slot_count, 2, 64, 128), narrow),
            scratch_shapes=[
                pltpu.VMEM((memory_len, width), narrow),
                pltpu.VMEM((2, width, width), wide),
                pltpu.VMEM((width, width), narrow),
            ],
            compiler_params=params,
            name="memory_gradient",
            cost_estimate=pl.CostEstimate(
                flops=5_000_000_000, bytes_accessed=12_000_000, transcendentals=0
            ),
        )(kernel_info, clip_weights, *operands)

    normed_a = [first[chunk][1] for chunk in span]
    mix_a = [first[chunk][4] for chunk in span]
    d_qkv = [end[0] for end in ends]
    d_early = [end[1] for end in ends]
    normed_b = [tail[1] for tail in tails]
    d_query_b = [tail[2] for tail in tails]
    mix_b = [tail[5] for tail in tails]
    d_mid = [tail[6] for tail in tails]
    normed_c = [tail[7] for tail in tails]
    d_hidden = [tail[8] for tail in tails]
    active = [tail[9] for tail in tails]
    d_top = [tail[10] for tail in tails]
    jobs = []
    for index in range(2):
        jobs.append(
            [(normed_c, d_hidden, 2 * index), (normed_c, d_hidden, 2 * index + 1)]
        )
    for index in range(2):
        jobs.append([(d_top, active, 2 * index), (d_top, active, 2 * index + 1)])
    jobs.append([(normed_a, d_qkv, 0), (normed_a, d_qkv, 1)])
    jobs.append([(normed_a, d_qkv, 2), (d_early, mix_a, None)])
    jobs.append([(normed_b, d_query_b, None), (d_mid, mix_b, None)])
    orders = [reduce_orders[index % 4] for index in range(8)]
    slots = [pair_gradient(orders[index], job) for index, job in enumerate(jobs)]
    slots.append(memory_gradient(orders[7]))

    shrink = 1.0 / math.sqrt(group_count * replicas)
    if staged:
        reduced = [reduce_slots(block, order) for block, order in zip(slots, orders)]
    else:
        reduced = []
        for block in slots:
            whole = block.reshape(dp_slots, tensor_slots, 2, 64, 128).transpose(2, 0, 3, 1, 4)
            whole = whole.reshape(2, width, width)
            whole = lax.psum_scatter(whole, "dp", scatter_dimension=1, tiled=True)
            reduced.append(lax.psum_scatter(whole, "tensor", scatter_dimension=2, tiled=True))
    reduced = [block.astype(wide) * shrink for block in reduced]

    def merge(pieces):
        blocks = jnp.concatenate(pieces, 0)
        count, high, across = blocks.shape
        return blocks.transpose(1, 0, 2).reshape(high, count * across)

    grad_in = jnp.stack(
        [
            reduced[4][0],
            reduced[4][1],
            reduced[5][0],
            reduced[6][0],
            reduced[7][0],
            reduced[7][1],
        ],
        0,
    )
    grad_out = jnp.stack([reduced[5][1].T, reduced[6][1].T], 0)
    grad_up = merge(reduced[:2])
    grad_down = merge(reduced[2:4]).T

    gain_start = me_tensor * gain_width
    gain_shard = lax.dynamic_slice_in_dim(gains, gain_start, gain_width, 1)
    gain_grad = lax.dynamic_slice_in_dim(gain_total, gain_start, gain_width, 1) * shrink
    bias_grad = (
        lax.dynamic_slice_in_dim(bias_total, me_tensor * heads_local, heads_local, 1) * shrink
    )
    velocity_in, averaged_in, updated_in = stepper(
        weights_in, grad_in, momentum_in, average_in, matrix_rate
    )
    velocity_out, averaged_out, updated_out = stepper(
        weights_out, grad_out, momentum_out, average_out, output_rate
    )
    velocity_up, averaged_up, updated_up = stepper(
        weights_up, grad_up, momentum_up, average_up, matrix_rate
    )
    velocity_down, averaged_down, updated_down = stepper(
        weights_down, grad_down, momentum_down, average_down, matrix_rate
    )
    velocity_gain, averaged_gain, updated_gain = stepper(
        gain_shard, gain_grad, momentum_gain, average_gain, small_rate
    )
    velocity_bias, averaged_bias, updated_bias = stepper(
        position_bias, bias_grad, momentum_bias, average_bias, small_rate
    )
    return (
        output,
        tokens_grad,
        memory_grad,
        example_norms,
        velocity_in,
        averaged_in,
        updated_in,
        velocity_out,
        averaged_out,
        updated_out,
        velocity_up,
        averaged_up,
        updated_up,
        velocity_down,
        averaged_down,
        updated_down,
        velocity_gain,
        averaged_gain,
        updated_gain,
        velocity_bias,
        averaged_bias,
        updated_bias,
    )


def solution(mesh):
    return jax.shard_map(
        on_device,
        mesh=mesh,
        in_specs=(
            P("dp", "tensor", None),
            P("dp", "tensor", None),
            P("dp", "tensor", None),
            P("dp", None, None),
            P("dp", None, None),
            P("dp"),
            P(None, "dp", "tensor"),
            P(None, "tensor", "dp"),
            P("dp", "tensor"),
            P("tensor", "dp"),
            P(),
            P(None, "tensor"),
            P(None, "dp", "tensor"),
            P(None, "dp", "tensor"),
            P(None, "tensor", "dp"),
            P(None, "tensor", "dp"),
            P("dp", "tensor"),
            P("dp", "tensor"),
            P("tensor", "dp"),
            P("tensor", "dp"),
            P(None, "tensor"),
            P(None, "tensor"),
            P(None, "tensor"),
            P(None, "tensor"),
        ),
        out_specs=(
            P("dp", "tensor", None),
            P("dp", "tensor", None),
            P("dp", "tensor", None),
            P("dp"),
            P(None, "dp", "tensor"),
            P(None, "dp", "tensor"),
            P(None, "dp", "tensor"),
            P(None, "tensor", "dp"),
            P(None, "tensor", "dp"),
            P(None, "tensor", "dp"),
            P("dp", "tensor"),
            P("dp", "tensor"),
            P("dp", "tensor"),
            P("tensor", "dp"),
            P("tensor", "dp"),
            P("tensor", "dp"),
            P(None, "tensor"),
            P(None, "tensor"),
            P(None, "tensor"),
            P(None, "tensor"),
            P(None, "tensor"),
            P(None, "tensor"),
        ),
        check_vma=False,
    )
```

```python
import functools
import math

import jax
import jax.numpy as jnp
from jax import lax
from jax.experimental import pallas as pl
from jax.experimental.pallas import tpu as pltpu
from jax.sharding import PartitionSpec as P

epsilon = 1e-06
momentum_decay = 0.9
average_decay = 0.7
matrix_rate = 10.0
output_rate = 40.0
small_rate = 50.0
group_limits = (0.6, 0.85, 1.2, 1.7)
head_dim = 64
quad = 4
quad_width = quad * head_dim
dp_slots = 8
tensor_slots = 4
wide = jnp.float32
narrow = jnp.bfloat16
vmem_bytes = 58 * 2**20
cost_scale = 1.0

core = ("tensor", 1)
row = ("tensor", 2)
side = ("dp", 1)
near = ("dp", 2)
far = ("dp", 4)
gather_order = (far, near, row, side, core)
reduce_orders = (
    (core, side, row, near, far),
    (core, row, near, far, side),
    (core, row, side, near, far),
    (core, near, far, side, row),
)
reduce_counts = (5, 3, 3, 5)


def dot_nn(left, right):
    return lax.dot_general(left, right, (((1,), (0,)), ((), ())), preferred_element_type=wide)


def dot_nt(left, right):
    return lax.dot_general(left, right, (((1,), (1,)), ((), ())), preferred_element_type=wide)


def dot_tn(left, right):
    return lax.dot_general(left, right, (((0,), (0,)), ((), ())), preferred_element_type=wide)


def head_masks(dtype):
    lanes = lax.broadcasted_iota(jnp.int32, (1, quad_width), 1) // head_dim
    return [(lanes == head).astype(wide).astype(dtype) for head in range(quad)]


def stack_heads(block, masks):
    return jnp.concatenate([block * mask for mask in masks], 0)


def unstack_heads(block, masks):
    rows = block.shape[0] // quad
    total = block[:rows] * masks[0]
    for head in range(1, quad):
        total = total + block[head * rows : (head + 1) * rows] * masks[head]
    return total


def norm_scale(rows):
    return lax.rsqrt(jnp.mean(rows * rows, -1, keepdims=True) + epsilon)


def norm_back(rows, gain, d_normed):
    scaling = norm_scale(rows)
    weighted = d_normed * gain
    cubed = scaling * scaling * scaling
    d_rows = scaling * weighted - rows * cubed * jnp.mean(rows * weighted, -1, keepdims=True)
    return d_rows, d_normed * rows * scaling


def softmax_keys(scores):
    peak = jnp.max(scores, 0, keepdims=True)
    weights = jnp.exp(scores - peak)
    return weights * (1.0 / jnp.sum(weights, 0, keepdims=True))


def gram_squares(left, right_grams):
    return jnp.sum(dot_nt(left, left) * right_grams, 0, keepdims=True)


def fold_lanes(row_sums):
    width = row_sums.shape[1]
    total = row_sums[:, :128]
    for start in range(128, width, 128):
        total = total + row_sums[:, start : start + 128]
    return total


def slot_places(order, first_is_high):
    places = []
    count = len(order)
    for slot in range(1 << count):
        index = {"dp": 0, "tensor": 0}
        for stage, (axis, bit) in enumerate(order):
            place = count - 1 - stage if first_is_high else stage
            if (slot >> place) & 1:
                index[axis] |= bit
        places.append((index["dp"], index["tensor"]))
    return places


def start_weights(info, pieces, plans, held, sems):
    for piece, (first, count, places, relative), sem in zip(pieces, plans, sems):
        for slot, (dp_index, tensor_index) in enumerate(places):
            if relative:
                high = pl.multiple_of((dp_index ^ info[0]) * 64, 64)
                left = pl.multiple_of((tensor_index ^ info[1]) * 128, 128)
            else:
                high, left = dp_index * 64, tensor_index * 128
            pltpu.make_async_copy(
                piece.at[slot],
                held.at[pl.ds(first, count), pl.ds(high, 64), pl.ds(left, 128)],
                sem,
            ).start()


def wait_weights(plans, held, sems):
    for (first, count, places, relative), sem in zip(plans, sems):
        share = 512 * len(places) // (dp_slots * tensor_slots)
        whole = held.at[pl.ds(first, count), pl.ds(0, share)]
        pltpu.make_async_copy(whole, whole, sem).wait()


def place_rows(info, parts, held, first=0):
    rows = held.shape[1] // len(parts)
    for index, part in enumerate(parts):
        start = pl.multiple_of((info[2] ^ index) * rows, rows)
        held[:, pl.ds(start, rows), :] = part[:, first : first + rows, :]


def split_rows(info, held, parts, first=0):
    rows = held.shape[1] // len(parts)
    for index, part in enumerate(parts):
        start = pl.multiple_of((info[2] ^ index) * rows, rows)
        part[:, first : first + rows, :] = held[:, pl.ds(start, rows), :].astype(part.dtype)


def self_forward_kernel(shards, plans, heads_local, *refs):
    refs = list(refs)

    def take(count):
        taken = refs[:count]
        del refs[:count]
        return taken

    (info,) = take(1)
    parts = take(shards)
    buckets, key_mask, gains, table = take(4)
    pieces = take(len(plans))
    normed_out, rows_out, qkv_out, weights_out, mix_out, mid_out = take(6)
    held, sems, rows_held, mix_held = take(4)
    sem_list = [sems.at[index] for index in range(len(plans))]

    @pl.when(pl.program_id(0) == 0)
    def _():
        start_weights(info, pieces, plans, held, sem_list)
        wait_weights(plans, held, sem_list)

    masks = head_masks(narrow)
    masks_wide = head_masks(wide)
    place_rows(info, parts, rows_held)
    rows_out[...] = rows_held[...]
    bundle, seq, width = rows_held.shape
    flat = rows_held[...].reshape(bundle * seq, width).astype(wide)
    normed = (flat * norm_scale(flat) * gains[0:1, :]).astype(narrow)
    normed_out[...] = normed.reshape(bundle, seq, width)
    for index in range(3):
        value = dot_nn(normed, held[index]).astype(narrow)
        qkv_out[index] = value.reshape(bundle, seq, width)
    for example in range(bundle):
        code = jnp.where(key_mask[example] > 0, buckets[example], -1).T
        safe = jnp.maximum(code, 0)
        code_all = jnp.concatenate([code] * quad, 1)
        for group in range(width // quad_width):
            columns = slice(group * quad_width, (group + 1) * quad_width)
            bias = []
            for head in range(group * quad, (group + 1) * quad):
                spot = ((head // heads_local) ^ info[2]) * heads_local + head % heads_local
                line = jnp.broadcast_to(table[pl.ds(spot, 1), :], (seq, 128))
                bias.append(jnp.take_along_axis(line, safe, axis=1))
            queries = stack_heads(qkv_out[0, example, :, columns], masks)
            scores = dot_nt(qkv_out[1, example, :, columns], queries) * (
                1.0 / math.sqrt(head_dim)
            ) + jnp.concatenate(bias, 1)
            weights = softmax_keys(jnp.where(code_all >= 0, scores, -1000000000.0))
            weights_out[example, group] = weights
            mixture = dot_tn(weights.astype(narrow), qkv_out[2, example, :, columns])
            mix_held[example, :, columns] = unstack_heads(mixture, masks_wide).astype(narrow)
    mix_out[...] = mix_held[...]
    mix = mix_held[...].reshape(bundle * seq, width)
    mid_out[...] = (flat + dot_nt(mix, held[3])).reshape(bundle, seq, width)


def cross_kernel(shards, plans, aliased, *refs):
    refs = list(refs)

    def take(count):
        taken = refs[:count]
        del refs[:count]
        return taken

    (info,) = take(1)
    memory_parts = take(shards)
    mid_in, gains = take(2)
    pieces = take(len(plans))
    take(aliased)
    own_output, own_grad = take(2)
    sent_parts = take(shards - 1)
    (
        early_out,
        normed_b_out,
        d_query_out,
        d_pair_out,
        mix_out,
        d_mid_out,
        normed_c_out,
        d_hidden_out,
        active_out,
        d_top_out,
        d_gain_b_out,
        d_gain_c_out,
        squares_out,
    ) = take(13)
    d_keys_out, d_values_out = d_pair_out.at[0], d_pair_out.at[1]
    held, sems, memory_held, keys_held, values_held, weights_held, rows_held, query_held = take(8)
    sem_list = [sems.at[index] for index in range(len(plans))]

    @pl.when(pl.program_id(0) == 0)
    def _():
        start_weights(info, pieces, plans, held, sem_list)
        wait_weights(plans, held, sem_list)

    masks = head_masks(narrow)
    masks_wide = head_masks(wide)
    scaling = 1.0 / math.sqrt(head_dim)
    bundle, seq, width = mid_in.shape
    memory_len = memory_held.shape[1]
    memory_rows = memory_len // shards
    groups = width // quad_width

    def flatten(block):
        return block.reshape(block.shape[0] * block.shape[1], block.shape[2])

    def unflatten(block):
        return block.reshape(bundle, block.shape[0] // bundle, block.shape[1])

    for index, part in enumerate(memory_parts):
        memory_held[:, index * memory_rows : (index + 1) * memory_rows, :] = part[
            :, :memory_rows, :
        ]
    place_rows(info, memory_parts, d_top_out, memory_rows)
    mid = flatten(mid_in[...])
    rows_b = mid.astype(narrow).astype(wide)
    normed_b = (rows_b * norm_scale(rows_b) * gains[1:2, :]).astype(narrow)
    normed_b_out[...] = unflatten(normed_b)
    query_held[...] = unflatten(dot_nn(normed_b, held[0]).astype(narrow))
    memory_flat = flatten(memory_held[...])
    keys_held[...] = unflatten(dot_nn(memory_flat, held[1]).astype(narrow))
    values_held[...] = unflatten(dot_nn(memory_flat, held[2]).astype(narrow))
    for example in range(bundle):
        for group in range(groups):
            columns = slice(group * quad_width, (group + 1) * quad_width)
            queries = stack_heads(query_held[example, :, columns], masks)
            scores = dot_nt(keys_held[example, :, columns], queries) * scaling
            weights = softmax_keys(scores)
            weights_held[example, group] = weights
            mixture = dot_tn(weights.astype(narrow), values_held[example, :, columns])
            mix_out[example, :, columns] = unstack_heads(mixture, masks_wide).astype(narrow)
    late = mid + dot_nt(flatten(mix_out[...]), held[3])
    rows_c = late.astype(narrow).astype(wide)
    normed_c = (rows_c * norm_scale(rows_c) * gains[2:3, :]).astype(narrow)
    normed_c_out[...] = unflatten(normed_c)
    d_top = flatten(d_top_out[...])
    total = late
    d_normed = jnp.zeros((bundle * seq, width), wide)
    up_grams = [jnp.zeros((seq, seq), wide) for _ in range(bundle)]
    down_grams = [jnp.zeros((seq, seq), wide) for _ in range(bundle)]
    slope = math.sqrt(2.0 / math.pi)
    for index in range(4):
        hidden = dot_nn(normed_c, held[4 + index])
        square = hidden * hidden
        bend = jnp.tanh(slope * hidden * (1.0 + 0.044715 * square))
        half = 0.5 * (1.0 + bend)
        active = (hidden * half).astype(narrow)
        steep = half + 0.5 * hidden * (1.0 - bend * bend) * (
            slope * (1.0 + (3.0 * 0.044715) * square)
        )
        total = total + dot_nt(active, held[8 + index])
        d_hidden = (dot_nn(d_top, held[8 + index]) * steep).astype(narrow)
        d_normed = d_normed + dot_nt(d_hidden, held[4 + index])
        active_out[index] = unflatten(active)
        d_hidden_out[index] = unflatten(d_hidden)
        for example in range(bundle):
            span = slice(example * seq, (example + 1) * seq)
            up_grams[example] += dot_nt(d_hidden[span], d_hidden[span])
            down_grams[example] += dot_nt(active[span], active[span])
    rows_held[...] = unflatten(total)
    for index in range(shards):
        start = pl.multiple_of((info[2] ^ index) * (seq // shards), seq // shards)
        block = rows_held[:, pl.ds(start, seq // shards), :].astype(narrow)
        if index:
            sent_parts[index - 1][:, memory_rows:, :] = block
        else:
            own_output[...] = block
    d_rows, d_gain_rows = norm_back(rows_c, gains[2:3, :], d_normed)
    d_gain_c = jnp.sum(unflatten(d_gain_rows), 1, keepdims=True)
    d_gain_c_out[...] = d_gain_c
    d_mid = d_top.astype(wide) + d_rows
    d_mid_low = d_mid.astype(narrow)
    d_mid_out[...] = unflatten(d_mid_low)
    d_mix = dot_nn(d_mid_low, held[3]).astype(narrow)
    squares = []
    for example in range(bundle):
        span = slice(example * seq, (example + 1) * seq)
        for group in range(groups):
            columns = slice(group * quad_width, (group + 1) * quad_width)
            keys = keys_held[example, :, columns]
            queries = stack_heads(query_held[example, :, columns], masks)
            d_mixes = stack_heads(d_mix[span, columns], masks)
            weights = weights_held[example, group]
            d_weights = dot_nt(values_held[example, :, columns], d_mixes)
            inner = jnp.sum(weights * d_weights, 0, keepdims=True)
            d_scores = (weights * (d_weights - inner)).astype(narrow)
            d_query_out[example, :, columns] = (
                unstack_heads(dot_tn(d_scores, keys), masks_wide) * scaling
            ).astype(narrow)
            d_keys_out[example, :, columns] = (dot_nn(d_scores, queries) * scaling).astype(narrow)
            d_values_out[example, :, columns] = dot_nn(weights.astype(narrow), d_mixes).astype(
                narrow
            )
        memory_grad = dot_nt(d_keys_out[example], held[1]) + dot_nt(d_values_out[example], held[2])
        own_grad[example] = memory_grad[:memory_rows]
        for index, part in enumerate(sent_parts):
            part[example, :memory_rows, :] = memory_grad[
                (index + 1) * memory_rows : (index + 2) * memory_rows
            ].astype(narrow)
        d_query = d_query_out[example]
        mix = mix_out[example]
        square_sum = gram_squares(normed_b[span], dot_nt(d_query, d_query))
        square_sum += gram_squares(mix, dot_nt(d_mid_low[span], d_mid_low[span]))
        square_sum += gram_squares(normed_c[span], up_grams[example])
        square_sum += gram_squares(d_top[span], down_grams[example])
        for block in (d_keys_out, d_values_out):
            product = dot_tn(memory_held[example], block[example])
            square_sum += fold_lanes(jnp.sum(product * product, 0, keepdims=True))
        square_sum += fold_lanes(d_gain_c[example] * d_gain_c[example])
        squares.append(square_sum)
    d_normed_b = dot_nt(flatten(d_query_out[...]), held[0])
    d_rows_b, d_gain_rows = norm_back(rows_b, gains[1:2, :], d_normed_b)
    d_gain_b = jnp.sum(unflatten(d_gain_rows), 1, keepdims=True)
    d_gain_b_out[...] = d_gain_b
    for example in range(bundle):
        squares_out[example] = squares[example] + fold_lanes(
            d_gain_b[example] * d_gain_b[example]
        )
    early_out[...] = unflatten(d_mid + d_rows_b)


def self_backward_kernel(shards, plans, *refs):
    refs = list(refs)

    def take(count):
        taken = refs[:count]
        del refs[:count]
        return taken

    info, early_in, rows_in, normed_in, qkv_in, weights_in, mix_in = take(7)
    squares_in, d_gain_b, d_gain_c, buckets, gains = take(5)
    pieces = take(len(plans))
    tokens_grads = take(shards)
    d_qkv_out, d_early_out, small_out, norms_out = take(4)
    held, sems, rows_held, bias_held = take(4)
    sem_list = [sems.at[index] for index in range(len(plans))]

    @pl.when(pl.program_id(0) == 0)
    def _():
        start_weights(info, pieces, plans, held, sem_list)
        wait_weights(plans, held, sem_list)

    masks = head_masks(narrow)
    masks_wide = head_masks(wide)
    scaling = 1.0 / math.sqrt(head_dim)
    bundle, seq, width = early_in.shape
    groups = width // quad_width
    bucket_count = bias_held.shape[0] // (groups * quad)

    def flatten(block):
        return block.reshape(block.shape[0] * block.shape[1], block.shape[2])

    def unflatten(block):
        return block.reshape(bundle, block.shape[0] // bundle, block.shape[1])

    early = flatten(early_in[...])
    d_early = early.astype(narrow)
    d_early_out[...] = unflatten(d_early)
    d_mix = dot_nn(d_early, held[3]).astype(narrow)
    squares = []
    for example in range(bundle):
        span = slice(example * seq, (example + 1) * seq)
        code = buckets[example].T
        for group in range(groups):
            columns = slice(group * quad_width, (group + 1) * quad_width)
            keys = qkv_in[1, example, :, columns]
            queries = stack_heads(qkv_in[0, example, :, columns], masks)
            d_mixes = stack_heads(d_mix[span, columns], masks)
            weights = weights_in[example, group]
            d_weights = dot_nt(qkv_in[2, example, :, columns], d_mixes)
            inner = jnp.sum(weights * d_weights, 0, keepdims=True)
            d_scores = (weights * (d_weights - inner)).astype(narrow)
            d_qkv_out[0, example, :, columns] = (
                unstack_heads(dot_tn(d_scores, keys), masks_wide) * scaling
            ).astype(narrow)
            d_qkv_out[1, example, :, columns] = (dot_nn(d_scores, queries) * scaling).astype(
                narrow
            )
            d_qkv_out[2, example, :, columns] = dot_nn(weights.astype(narrow), d_mixes).astype(
                narrow
            )
            d_wide = d_scores.astype(wide)
            for bucket in range(bucket_count):
                chosen = code == bucket
                for head in range(quad):
                    picked = jnp.where(chosen, d_wide[:, head * seq : (head + 1) * seq], 0.0)
                    spot = (group * quad + head) * bucket_count + bucket
                    bias_held[spot : spot + 1, :] = jnp.sum(picked, 0, keepdims=True)
        d_bias = lax.dot_general(
            jnp.ones((8, 128), wide),
            bias_held[...],
            (((1,), (1,)), ((), ())),
            precision=lax.Precision.HIGHEST,
            preferred_element_type=wide,
        )[:1]
        small_out[example, :, 3 * width :] = d_bias
        grams = jnp.zeros((seq, seq), wide)
        for index in range(3):
            block = d_qkv_out[index, example]
            grams = grams + dot_nt(block, block)
        square_sum = gram_squares(normed_in[example], grams)
        square_sum += gram_squares(mix_in[example], dot_nt(d_early[span], d_early[span]))
        square_sum += fold_lanes(d_bias * d_bias)
        squares.append(square_sum)
    d_normed = dot_nt(flatten(d_qkv_out[0]), held[0])
    d_normed = d_normed + dot_nt(flatten(d_qkv_out[1]), held[1])
    d_normed = d_normed + dot_nt(flatten(d_qkv_out[2]), held[2])
    d_rows, d_gain_rows = norm_back(flatten(rows_in[...]).astype(wide), gains[0:1, :], d_normed)
    d_gain = jnp.sum(unflatten(d_gain_rows), 1, keepdims=True)
    small_out[:, :, :width] = d_gain
    small_out[:, :, width : 2 * width] = d_gain_b[...]
    small_out[:, :, 2 * width : 3 * width] = d_gain_c[...]
    for example in range(bundle):
        square_sum = (
            squares[example]
            + squares_in[example]
            + fold_lanes(d_gain[example] * d_gain[example])
        )
        total = jnp.sum(square_sum, -1, keepdims=True) + epsilon
        norms_out[example] = jnp.broadcast_to(jnp.sqrt(total), (1, 128))
    rows_held[...] = unflatten(early + d_rows)
    split_rows(info, rows_held, tokens_grads)


class Gradients:
    def __init__(self, info, clip, loads, load_sems, scaled, tile, held, store_sems):
        self.info, self.clip, self.scaled = info, clip, scaled
        self.tile, self.held, self.store_sems = tile, held, store_sems
        self.copies = [
            pltpu.make_async_copy(source, target, load_sems.at[index])
            for index, (source, target) in enumerate(loads)
        ]
        self.targets = [target for source, target in loads]
        self.stores = []
        for copy in self.copies:
            copy.start()

    def read(self, index):
        self.copies[index].wait()
        return self.targets[index]

    def scale(self, index):
        block = self.read(index)
        count, rows, width = block.shape
        for example in range(count):
            self.scaled[example * rows : (example + 1) * rows, :] = (
                block[example].astype(wide) * self.clip[example]
            ).astype(narrow)

    def product(self, index):
        block = self.read(index)
        return dot_tn(self.scaled[...], block[...].reshape(self.scaled.shape[0], block.shape[-1]))

    def write(self, value, outs, unit, places):
        number = len(self.stores) // 2
        tile = self.tile.at[number % 2]
        tile[...] = value.astype(narrow)
        halves = self.held.at[number]
        count = len(places) // 2
        for slot, (dp_index, tensor_index) in enumerate(places):
            high = pl.multiple_of((dp_index ^ self.info[0]) * 64, 64)
            left = pl.multiple_of((tensor_index ^ self.info[1]) * 128, 128)
            halves[slot // count, slot % count] = tile[pl.ds(high, 64), pl.ds(left, 128)]
        for half, out in enumerate(outs):
            copy = pltpu.make_async_copy(
                halves.at[half], out.at[:, unit], self.store_sems.at[len(self.stores)]
            )
            copy.start()
            self.stores.append(copy)

    def finish(self):
        for copy in self.stores:
            copy.wait()


def inner_gradient_kernel(places, info, clip, normed, d_hidden, d_top, active, *refs):
    outs = (refs[:2], refs[2:4])
    rows_held, blocks_held, load_sems, scaled, tile, held, store_sems = refs[4:]
    loads = []
    for piece, (left, right) in enumerate(((normed, d_hidden), (d_top, active))):
        loads.append((left, rows_held.at[piece]))
        loads += [(right.at[unit], blocks_held.at[4 * piece + unit]) for unit in range(4)]
    work = Gradients(info, clip, loads, load_sems, scaled, tile, held, store_sems)
    for piece in range(2):
        work.scale(5 * piece)
        for unit in range(4):
            spot = 4 * piece + unit
            out = int(spot >= reduce_counts[0])
            spot -= out * reduce_counts[0]
            work.write(work.product(5 * piece + 1 + unit), outs[out], spot, places[out])
    work.finish()


def attention_gradient_kernel(shards, chunks, places, info, clip, *refs):
    normed_a, d_qkv, d_early, mix_a, normed_b, d_query, d_mid, mix_b = refs[:8]
    parts = refs[8 : 8 + shards * chunks]
    refs = refs[8 + shards * chunks :]
    d_pair = refs[0]
    self_out, cross_out = refs[1:3], refs[3:5]
    rows_held, parts_held, pairs_held, memory_held = refs[5:9]
    load_sems, scaled, tile, held, store_sems = refs[9:]
    count, memory_len = d_pair.shape[1:3]
    part_len = memory_len // shards
    group = count // chunks
    sources = [normed_a, d_qkv.at[0], d_qkv.at[1], d_qkv.at[2], d_early, mix_a]
    sources += [normed_b, d_query, d_mid, mix_b]
    loads = [(source, rows_held.at[index]) for index, source in enumerate(sources)]
    first = len(loads)
    for chunk in range(chunks):
        for index in range(shards):
            place = chunk * shards + index
            loads.append((parts[place].at[:, pl.ds(0, part_len)], parts_held.at[place]))
        for unit in range(2):
            loads.append(
                (d_pair.at[unit, pl.ds(chunk * group, group)], pairs_held.at[2 * chunk + unit])
            )
    work = Gradients(info, clip, loads, load_sems, scaled, tile, held, store_sems)
    work.scale(0)
    for unit in range(3):
        work.write(work.product(1 + unit), self_out, unit, places[0])
    work.scale(4)
    work.write(work.product(5), cross_out, 0, places[1])
    work.scale(6)
    work.write(work.product(7), cross_out, 1, places[1])
    work.scale(8)
    work.write(work.product(9), cross_out, 2, places[1])
    totals = [None, None]
    for chunk in range(chunks):
        start = first + chunk * (shards + 2)
        for index in range(shards):
            block = work.read(start + index)
            for example in range(group):
                top = (example * shards + index) * part_len
                memory_held[chunk, top : top + part_len, :] = (
                    block[example].astype(wide) * clip[chunk * group + example]
                ).astype(narrow)
        for unit in range(2):
            pair = work.read(start + shards + unit)
            product = dot_tn(
                memory_held[chunk], pair[...].reshape(group * memory_len, pair.shape[-1])
            )
            totals[unit] = product if chunk == 0 else totals[unit] + product
    for unit in range(2):
        work.write(totals[unit], cross_out, 3 + unit, places[1])
    work.finish()


def stepper(parameter, gradient, momentum, average, step_rate):
    velocity = momentum_decay * momentum + gradient
    updated = parameter - step_rate * (gradient + momentum_decay * velocity)
    averaged = average_decay * average + (1.0 - average_decay) * updated
    return (velocity, averaged, updated)


def update_kernel(shrink, *refs):
    sums = refs[:8]
    params, outs = refs[8:20], refs[20:]

    def gradient(piece, unit):
        total = sums[2 * piece][unit].astype(wide) + sums[2 * piece + 1][unit].astype(wide)
        return total * shrink

    def step(group, spot, value, rate):
        weight, momentum, average = params[3 * group : 3 * group + 3]
        stepped = stepper(weight[spot], value, momentum[spot], average[spot], rate)
        for out, block in zip(outs[3 * group : 3 * group + 3], stepped):
            out[spot] = block

    inside = ((2, 0), (2, 1), (2, 2), (3, 1), (3, 3), (3, 4))
    for index, (piece, unit) in enumerate(inside):
        step(0, index, gradient(piece, unit), matrix_rate)
    for index, unit in enumerate((0, 2)):
        step(1, index, gradient(3, unit), output_rate)
    for index in range(4):
        spot = (slice(None), slice(128 * index, 128 * (index + 1)))
        step(2, spot, gradient(0, index), matrix_rate)
        piece, unit = (1, index - 1) if index else (0, 4)
        step(3, spot, gradient(piece, unit), matrix_rate)


def assemble_kernel(shards, chunks, *refs):
    refs = list(refs[1:])

    def take(count):
        taken = refs[:count]
        del refs[:count]
        return taken

    arrived = [take(shards - 1) for _ in range(chunks)]
    tokens_parts = take(shards - 1)
    take(3)
    output, tokens_grad, memory_grad = refs
    rows = memory_grad.shape[1]
    for index in range(shards - 1):
        for chunk in range(chunks):

            @pl.when((pl.program_id(0) == index) & (pl.program_id(1) == chunk))
            def _(index=index, chunk=chunk):
                tokens_grad[...] = tokens_parts[index][...].astype(wide)
                block = arrived[chunk][index]
                output[...] = block[:, rows:, :]
                memory_grad[...] = block[:, :rows, :].astype(wide)


def swap(value, axis, bit):
    size = lax.axis_size(axis)
    return lax.ppermute(value, axis, [(index, index ^ bit) for index in range(size)])


def after(value, *earlier):
    return lax.optimization_barrier((value,) + earlier)[0]


def gather_slots(shard):
    gathered = shard[None]
    for axis, bit in gather_order[:3]:
        gathered = jnp.concatenate([gathered, swap(gathered, axis, bit)], 0)
    beside = swap(gathered, *gather_order[3])
    pieces = [gathered, beside, swap(gathered, *gather_order[4]), swap(beside, *gather_order[4])]
    places = slot_places(gather_order, False)
    count = len(places) // 4
    return [
        (piece, places[index * count : (index + 1) * count]) for index, piece in enumerate(pieces)
    ]


def add_stage(kept, arrived):
    half = kept.shape[0] // 2

    def added(start, stop):
        total = kept[start:stop].astype(wide) + arrived[start:stop].astype(wide)
        return total.astype(narrow)

    if not half:
        return added(0, 1)[0], None
    return added(0, half), added(half, 2 * half)


def on_device(
    tokens,
    memory,
    cotangent,
    buckets,
    key_mask,
    task_groups,
    weights_in,
    weights_out,
    weights_up,
    weights_down,
    gains,
    position_bias,
    momentum_in,
    average_in,
    momentum_out,
    average_out,
    momentum_up,
    average_up,
    momentum_down,
    average_down,
    momentum_gain,
    average_gain,
    momentum_bias,
    average_bias,
):
    shards = lax.axis_size("tensor")
    replicas = lax.axis_size("dp")
    me_tensor = lax.axis_index("tensor")
    me_dp = lax.axis_index("dp")
    width = tokens.shape[2]
    seq = buckets.shape[1]
    seq_rows = tokens.shape[1]
    memory_rows = memory.shape[1]
    memory_len = memory_rows * shards
    group_count = tokens.shape[0]
    local = group_count // shards
    chunks = 2 if local % 2 == 0 else 1
    per_chunk = local // chunks
    bundle = 2 if per_chunk % 2 == 0 else 1
    steps = per_chunk // bundle
    bucket_count, heads_local = position_bias.shape
    heads = heads_local * shards
    gain_width = momentum_gain.shape[1]
    staged = shards == tensor_slots and replicas == dp_slots

    slot_base = [me_dp, me_tensor] if staged else [0 * me_dp, 0 * me_tensor]
    kernel_info = jnp.stack(slot_base + [me_tensor]).astype(jnp.int32)

    def square_shards():
        high, across = weights_in.shape[1], weights_in.shape[2]
        split = lambda block: block.reshape(high, -1, across).transpose(1, 0, 2)
        return (
            weights_in.astype(narrow),
            weights_out.astype(narrow).transpose(0, 2, 1),
            split(weights_up.astype(narrow)),
            split(weights_down.astype(narrow).T),
        )

    shard_in, shard_out, shard_up, shard_down = square_shards()
    slot_count = dp_slots * tensor_slots
    plain_places = [(slot // tensor_slots, slot % tensor_slots) for slot in range(slot_count)]

    def gather_late(blocks):
        count = blocks.shape[0]
        if staged:
            whole = lax.all_gather(blocks, ("dp", "tensor"), axis=0)
        else:
            whole = lax.all_gather(blocks, "dp", axis=1, tiled=True)
            whole = lax.all_gather(whole, "tensor", axis=2, tiled=True)
            whole = whole.reshape(count, dp_slots, 64, tensor_slots, 128).transpose(1, 3, 0, 2, 4)
            whole = whole.reshape(slot_count, count, 64, 128)
        return [whole], [(0, count, plain_places, False)]

    def gather_soon(blocks):
        if not staged:
            return gather_late(blocks)
        pieces, plans = [], []
        for piece, places in gather_slots(blocks):
            pieces.append(piece)
            plans.append((0, blocks.shape[0], places, True))
        return pieces, plans

    def exchange(values, start, count):
        found = []
        for index in range(shards):
            first = (me_tensor ^ index) * local + start
            blocks = [lax.dynamic_slice_in_dim(value, first, count, 0) for value in values]
            block = jnp.concatenate(blocks, 1) if len(blocks) > 1 else blocks[0]
            found.append(swap(block, "tensor", index) if index else block)
        return found

    late_pieces, late_plans = gather_late(
        jnp.concatenate([shard_in[3:6], shard_out[1:2], shard_up, shard_down], 0)
    )
    token_parts = exchange([tokens], 0, local)
    self_pieces, self_plans = gather_soon(jnp.concatenate([shard_in[:3], shard_out[:1]], 0))
    table = jnp.pad(position_bias.T, ((0, 0), (0, 128 - bucket_count)))
    table_all = jnp.concatenate(
        [swap(table, "tensor", index) if index else table for index in range(shards)], 0
    )
    memory_parts = []
    earlier = token_parts
    for chunk in range(chunks):
        source, _ = lax.optimization_barrier((memory, earlier[-1]))
        earlier = exchange([source, cotangent], chunk * per_chunk, per_chunk)
        memory_parts.append(earlier)
    bucket_mine = lax.dynamic_slice_in_dim(buckets, me_tensor * local, local, 0)
    mask_mine = lax.dynamic_slice_in_dim(key_mask, me_tensor * local, local, 0)
    groups_mine = lax.dynamic_slice_in_dim(task_groups, me_tensor * local, local, 0)

    smem = pl.BlockSpec(memory_space=pltpu.SMEM)
    anywhere = pl.BlockSpec(memory_space=pl.ANY)
    params = pltpu.CompilerParams(
        vmem_limit_bytes=vmem_bytes, dimension_semantics=("arbitrary",)
    )

    def part_spec(shape, offset=0, lead=None):
        zeros = (0,) * len(shape)
        if lead is None:
            return pl.BlockSpec(
                (bundle,) + tuple(shape), lambda step, *_: (step + offset,) + zeros
            )
        return pl.BlockSpec(
            (lead, bundle) + tuple(shape), lambda step, *_: (0, step + offset) + zeros
        )

    def own_spec(shape, offset=0):
        zeros = (0,) * len(shape)
        return pl.BlockSpec(
            (bundle,) + tuple(shape),
            lambda step, info: (info[2] * (local // bundle) + step + offset,) + zeros,
        )

    def whole_spec(shape):
        return pl.BlockSpec(tuple(shape), lambda step, *_: (0,) * len(shape))

    def shaped(shape, dtype, lead=None, count=local):
        front = (count,) if lead is None else (lead, count)
        return jax.ShapeDtypeStruct(front + tuple(shape), dtype)

    def cost(flops, moved):
        return pl.CostEstimate(
            flops=int(flops * cost_scale), bytes_accessed=int(moved * cost_scale), transcendentals=0
        )

    groups = width // quad_width
    row_block = (seq, width)
    part_rows = memory_rows + seq_rows

    normed_a, rows_a, qkv_a, weights_a, mix_a, mid = pl.pallas_call(
        functools.partial(self_forward_kernel, shards, self_plans, heads_local),
        grid=(local // bundle,),
        in_specs=[smem]
        + [part_spec((seq_rows, width))] * shards
        + [part_spec((seq, seq))] * 2
        + [whole_spec(gains.shape), whole_spec(table_all.shape)]
        + [anywhere] * len(self_pieces),
        out_specs=[
            part_spec(row_block),
            part_spec(row_block),
            part_spec(row_block, lead=3),
            part_spec((groups, seq, quad * seq)),
            part_spec(row_block),
            part_spec(row_block),
        ],
        out_shape=[
            shaped(row_block, narrow),
            shaped(row_block, narrow),
            shaped(row_block, narrow, 3),
            shaped((groups, seq, quad * seq), wide),
            shaped(row_block, narrow),
            shaped(row_block, wide),
        ],
        scratch_shapes=[
            pltpu.VMEM((4, width, width), narrow),
            pltpu.SemaphoreType.DMA((len(self_pieces),)),
            pltpu.VMEM((bundle,) + row_block, narrow),
            pltpu.VMEM((bundle,) + row_block, narrow),
        ],
        compiler_params=params,
        name="self_forward",
        cost_estimate=cost(local * 2e9, local * 2e6),
    )(
        kernel_info,
        *token_parts,
        bucket_mine,
        mask_mine,
        gains,
        table_all,
        *self_pieces,
    )

    def cross(chunk, filled):
        offset = chunk * steps
        gain_block = (1, width)
        kept_specs = [
            part_spec(row_block, offset),
            part_spec(row_block, offset),
            part_spec(row_block, offset),
            part_spec((memory_len, width), offset, 2),
            part_spec(row_block, offset),
            part_spec(row_block, offset),
            part_spec(row_block, offset),
            part_spec(row_block, offset, 4),
            part_spec(row_block, offset, 4),
            part_spec(row_block, offset),
            part_spec(gain_block, offset),
            part_spec(gain_block, offset),
            part_spec((1, 128), offset),
        ]
        kept_shapes = [
            shaped(row_block, wide),
            shaped(row_block, narrow),
            shaped(row_block, narrow),
            shaped((memory_len, width), narrow, 2),
            shaped(row_block, narrow),
            shaped(row_block, narrow),
            shaped(row_block, narrow),
            shaped(row_block, narrow, 4),
            shaped(row_block, narrow, 4),
            shaped(row_block, narrow),
            shaped(gain_block, wide),
            shaped(gain_block, wide),
            shaped((1, 128), wide),
        ]
        own_specs = [own_spec((seq_rows, width), offset), own_spec((memory_rows, width), offset)]
        own_shapes = [
            shaped((seq_rows, width), narrow, count=group_count),
            shaped((memory_rows, width), wide, count=group_count),
        ]
        operands = [kernel_info, *memory_parts[chunk], mid, gains, *late_pieces]
        aliases = {}
        for index, block in enumerate(filled):
            aliases[len(operands) + index] = index if index < 2 else index + shards - 1
        return pl.pallas_call(
            functools.partial(cross_kernel, shards, late_plans, len(filled)),
            grid_spec=pltpu.PrefetchScalarGridSpec(
                num_scalar_prefetch=1,
                grid=(steps,),
                in_specs=[part_spec((part_rows, width))] * shards
                + [part_spec(row_block, offset), whole_spec(gains.shape)]
                + [anywhere] * (len(late_pieces) + len(filled)),
                out_specs=own_specs + [part_spec((part_rows, width))] * (shards - 1) + kept_specs,
                scratch_shapes=[
                    pltpu.VMEM((12, width, width), narrow),
                    pltpu.SemaphoreType.DMA((len(late_pieces),)),
                    pltpu.VMEM((bundle, memory_len, width), narrow),
                    pltpu.VMEM((bundle, memory_len, width), narrow),
                    pltpu.VMEM((bundle, memory_len, width), narrow),
                    pltpu.VMEM((bundle, groups, memory_len, quad * seq), wide),
                    pltpu.VMEM((bundle,) + row_block, wide),
                    pltpu.VMEM((bundle,) + row_block, narrow),
                ],
            ),
            out_shape=own_shapes
            + [shaped((part_rows, width), narrow, count=per_chunk)] * (shards - 1)
            + kept_shapes,
            input_output_aliases=aliases,
            compiler_params=params,
            name="cross",
            cost_estimate=cost(per_chunk * 8e9, per_chunk * 6e6),
        )(*operands, *filled)

    filled, sent = [], []
    for chunk in range(chunks):
        found = cross(chunk, filled)
        sent.append(found[2 : shards + 1])
        filled = list(found[:2]) + list(found[shards + 1 :])
    own_output, own_memory = filled[:2]
    (
        early,
        normed_b,
        d_query_b,
        d_pair,
        mix_b,
        d_mid,
        normed_c,
        d_hidden,
        active,
        d_top,
        d_gain_b,
        d_gain_c,
        squares,
    ) = filled[2:]
    arrived = [
        [swap(block, "tensor", index + 1) for index, block in enumerate(blocks)] for blocks in sent
    ]
    soon = [block for blocks in arrived[:-1] for block in blocks]

    found = pl.pallas_call(
        functools.partial(self_backward_kernel, shards, self_plans),
        grid_spec=pltpu.PrefetchScalarGridSpec(
            num_scalar_prefetch=1,
            grid=(local // bundle,),
            in_specs=[
            part_spec(row_block),
            part_spec(row_block),
            part_spec(row_block),
            part_spec(row_block, lead=3),
            part_spec((groups, seq, quad * seq)),
            part_spec(row_block),
            part_spec((1, 128)),
            part_spec((1, width)),
            part_spec((1, width)),
            part_spec((seq, seq)),
            whole_spec(gains.shape),
        ]
        + [anywhere] * len(self_pieces),
        out_specs=[own_spec((seq_rows, width))]
        + [part_spec((seq_rows, width))] * (shards - 1)
        + [
            part_spec(row_block, lead=3),
            part_spec(row_block),
            part_spec((1, 3 * width + heads * bucket_count)),
            part_spec((1, 128)),
        ],
        scratch_shapes=[
            pltpu.VMEM((4, width, width), narrow),
            pltpu.SemaphoreType.DMA((len(self_pieces),)),
            pltpu.VMEM((bundle,) + row_block, wide),
            pltpu.VMEM((heads * bucket_count, 128), wide),
        ],
        ),
        out_shape=[shaped((seq_rows, width), wide, count=group_count)]
        + [shaped((seq_rows, width), narrow)] * (shards - 1)
        + [
            shaped(row_block, narrow, 3),
            shaped(row_block, narrow),
            shaped((1, 3 * width + heads * bucket_count), wide),
            shaped((1, 128), wide),
        ],
        compiler_params=params,
        name="self_backward",
        cost_estimate=cost(local * 3e9, local * 3e6),
    )(
        after(kernel_info, *soon),
        early,
        rows_a,
        normed_a,
        qkv_a,
        weights_a,
        mix_a,
        squares,
        d_gain_b,
        d_gain_c,
        bucket_mine,
        gains,
        *self_pieces,
    )
    own_tokens, tokens_sent = found[0], found[1:shards]
    d_qkv, d_early, small, norms = found[shards:]

    norms = after(norms.reshape(local, 128), *arrived[-1])
    norm_slots = norms
    bit = 1
    while bit < shards:
        norm_slots = jnp.concatenate([norm_slots, swap(norm_slots, "tensor", bit)], 0)
        bit *= 2
    total = jnp.broadcast_to(jnp.sum(norm_slots, 0, keepdims=True), (8, 128))
    bit = 1
    while bit < replicas:
        total = total + swap(total, "dp", bit)
        bit *= 2
    order = jnp.arange(shards, dtype=jnp.int32) ^ me_tensor
    example_norms = norm_slots[:, 0].reshape(shards, local)[order].reshape(group_count)
    mean_norm = total[0, 0] / (group_count * replicas)
    limits = jnp.sum(
        (groups_mine[:, None] == jnp.arange(len(group_limits), dtype=jnp.int32))
        * jnp.asarray(group_limits, wide),
        1,
    )
    clip_weights = jnp.minimum(1.0 / mean_norm, limits / norms[:, 0])
    small = jnp.sum(clip_weights[:, None, None] * small, 0).reshape(-1, 128)

    def places_of(index):
        return slot_places(reduce_orders[index], True) if staged else plain_places

    out_shapes = [
        jax.ShapeDtypeStruct((slot_count // 2, count, 64, 128), narrow) for count in reduce_counts
    ]

    def gradient_call(kernel, clip, operands, outs, loads, extra, name, work):
        return pl.pallas_call(
            kernel,
            in_specs=[smem, smem] + [anywhere] * len(operands),
            out_specs=[anywhere] * 4,
            out_shape=[shape for shape in outs for _ in range(2)],
            scratch_shapes=extra
            + [
                pltpu.SemaphoreType.DMA((loads,)),
                pltpu.VMEM((local * seq, width), narrow),
                pltpu.VMEM((2, width, width), narrow),
                pltpu.VMEM((8, 2, slot_count // 2, 64, 128), narrow),
                pltpu.SemaphoreType.DMA((16,)),
            ],
            compiler_params=pltpu.CompilerParams(vmem_limit_bytes=vmem_bytes),
            name=name,
            cost_estimate=work,
        )(kernel_info, clip, *operands)

    def inner_gradients(clip):
        kernel = functools.partial(inner_gradient_kernel, (places_of(0), places_of(1)))
        extra = [
            pltpu.VMEM((2, local, seq, width), narrow),
            pltpu.VMEM((8, local, seq, width), narrow),
        ]
        operands = [normed_c, d_hidden, d_top, active]
        return gradient_call(
            kernel, clip, operands, out_shapes[:2], 10, extra, "inner_gradients", cost(9e9, 14e6)
        )

    def attention_gradients(clip):
        kernel = functools.partial(
            attention_gradient_kernel, shards, chunks, (places_of(2), places_of(3))
        )
        extra = [
            pltpu.VMEM((10, local, seq, width), narrow),
            pltpu.VMEM((chunks * shards, per_chunk, memory_rows, width), narrow),
            pltpu.VMEM((2 * chunks, per_chunk, memory_len, width), narrow),
            pltpu.VMEM((chunks, per_chunk * memory_len, width), narrow),
        ]
        operands = [normed_a, d_qkv, d_early, mix_a, normed_b, d_query_b, d_mid, mix_b]
        operands += [block for blocks in memory_parts for block in blocks] + [d_pair]
        return gradient_call(
            kernel,
            clip,
            operands,
            out_shapes[2:],
            10 + chunks * (shards + 2),
            extra,
            "attention_gradients",
            cost(14e9, 30e6),
        )

    tokens_arrived = [swap(block, "tensor", index + 1) for index, block in enumerate(tokens_sent)]

    def by_place(shape, index, chunk=None):
        def spot(place, step, info):
            if chunk is not None:
                return (0, 0, 0)
            return (jnp.where(place == index, step, jnp.where(place < index, 0, chunks - 1)), 0, 0)

        return pl.BlockSpec((per_chunk,) + shape, spot)

    def to_place(shape):
        return pl.BlockSpec(
            (per_chunk,) + shape,
            lambda place, step, info: ((info[2] ^ (place + 1)) * chunks + step, 0, 0),
        )

    small_rows, large_rows = (seq_rows, width), (memory_rows, width)
    operands = [block for blocks in arrived for block in blocks] + tokens_arrived
    assemble = pl.pallas_call(
        functools.partial(assemble_kernel, shards, chunks),
        grid_spec=pltpu.PrefetchScalarGridSpec(
            num_scalar_prefetch=1,
            grid=(shards - 1, chunks),
            in_specs=[
                by_place((part_rows, width), index, chunk)
                for chunk in range(chunks)
                for index in range(shards - 1)
            ]
            + [by_place(small_rows, index) for index in range(shards - 1)]
            + [anywhere] * 3,
            out_specs=[to_place(small_rows), to_place(small_rows), to_place(large_rows)],
        ),
        out_shape=[
            jax.ShapeDtypeStruct((group_count,) + small_rows, narrow),
            jax.ShapeDtypeStruct((group_count,) + small_rows, wide),
            jax.ShapeDtypeStruct((group_count,) + large_rows, wide),
        ],
        input_output_aliases={len(operands) + 1 + index: index for index in range(3)},
        compiler_params=pltpu.CompilerParams(
            vmem_limit_bytes=vmem_bytes, dimension_semantics=("arbitrary", "arbitrary")
        ),
        name="assemble",
        cost_estimate=cost(1e6, 20e6),
    )
    returned = operands + [own_output, own_tokens, own_memory]

    pairs = [None] * 4

    def travel(index, stage):
        kept, sent = pairs[index]
        pairs[index] = add_stage(kept, swap(sent, *reduce_orders[index][stage]))

    last_stage = len(reduce_orders[0]) - 1
    done = [0] * 4

    def travel(*indices):
        for index in indices:
            if staged and done[index] <= last_stage:
                kept, sent = pairs[index]
                order = reduce_orders[index][done[index]]
                pairs[index] = add_stage(kept, swap(sent, *order))
                done[index] += 1

    def there(*indices):
        return [block for index in indices for block in pairs[index] if block is not None]

    found = inner_gradients(clip_weights)
    pairs[:2] = [tuple(found[:2]), tuple(found[2:])]
    found = attention_gradients(after(clip_weights, *there(0, 1), *tokens_arrived))
    pairs[2:] = [tuple(found[:2]), tuple(found[2:])]
    travel(0, 1)
    travel(2, 3)
    travel(0, 1, 2, 3)
    output, tokens_grad, memory_grad = assemble(after(kernel_info, *there(0)), *returned)

    def together(*extra):
        held = lax.optimization_barrier((pairs, extra))
        pairs[:] = held[0]
        return held[1]

    shrink = 1.0 / math.sqrt(group_count * replicas)
    if staged:
        small = small + swap(small, *core)
        small = after(small, *there(2, 3))
        small = small + swap(small, *side)
        small, output = together(small, output)
        small = small + swap(small, *row)
        travel(0, 1, 2, 3)
        (small,) = together(small)
        small = small + swap(small, *near)
        travel(0, 1, 2, 3)
        (small,) = together(small)
        small = small + swap(small, *far)
        last = [swap(sent, *order[-1]) for (kept, sent), order in zip(pairs, reduce_orders)]
        last = [block[0] for pair, came in zip(pairs, last) for block in (pair[0], came)]
    else:
        reduced = []
        for kept, sent in pairs:
            whole = jnp.concatenate([kept, sent], 0)
            count = whole.shape[1]
            whole = whole.reshape(dp_slots, tensor_slots, count, 64, 128).transpose(2, 0, 3, 1, 4)
            whole = whole.reshape(count, width, width)
            whole = lax.psum_scatter(whole, "dp", scatter_dimension=1, tiled=True)
            reduced.append(lax.psum_scatter(whole, "tensor", scatter_dimension=2, tiled=True))
        small = lax.psum(small, ("dp", "tensor"))
    small = small.reshape(-1)
    gain_total = small[: 3 * width].reshape(3, width)
    bias_total = small[3 * width :].reshape(heads, bucket_count).T

    large = [
        (weights_in, momentum_in, average_in, matrix_rate),
        (weights_out, momentum_out, average_out, output_rate),
        (weights_up, momentum_up, average_up, matrix_rate),
        (weights_down, momentum_down, average_down, matrix_rate),
    ]
    if staged:
        turns = ((0, 1, 2), (0, 2, 1), (0, 1), (1, 0))
        turned = [
            block.transpose(turn) for group, turn in zip(large, turns) for block in group[:3]
        ]
        operands = last + turned
        stepped = pl.pallas_call(
            functools.partial(update_kernel, shrink),
            out_shape=[
                jax.ShapeDtypeStruct(block.shape, wide) for block in turned
            ],
            compiler_params=pltpu.CompilerParams(vmem_limit_bytes=vmem_bytes),
            name="update",
            cost_estimate=cost(1e6, 4e6),
        )(*operands)
        stepped = [block.transpose(turns[index // 3]) for index, block in enumerate(stepped)]
    else:
        reduced = [block.astype(wide) * shrink for block in reduced]

        def merge(blocks):
            count, high, across = blocks.shape
            return blocks.transpose(1, 0, 2).reshape(high, count * across)

        inside = jnp.concatenate([reduced[2], reduced[3][1:2], reduced[3][3:]], 0)
        outward = jnp.stack([reduced[3][0].T, reduced[3][2].T], 0)
        down = jnp.concatenate([reduced[0][4:], reduced[1]], 0)
        gradients = [inside, outward, merge(reduced[0][:4]), merge(down).T]
        stepped = []
        for (weight, momentum, average, rate), gradient in zip(large, gradients):
            stepped += stepper(weight, gradient, momentum, average, rate)
    (
        velocity_in,
        averaged_in,
        updated_in,
        velocity_out,
        averaged_out,
        updated_out,
        velocity_up,
        averaged_up,
        updated_up,
        velocity_down,
        averaged_down,
        updated_down,
    ) = stepped

    gain_start = me_tensor * gain_width
    gain_shard = lax.dynamic_slice_in_dim(gains, gain_start, gain_width, 1)
    gain_grad = lax.dynamic_slice_in_dim(gain_total, gain_start, gain_width, 1) * shrink
    bias_grad = (
        lax.dynamic_slice_in_dim(bias_total, me_tensor * heads_local, heads_local, 1) * shrink
    )
    velocity_gain, averaged_gain, updated_gain = stepper(
        gain_shard, gain_grad, momentum_gain, average_gain, small_rate
    )
    velocity_bias, averaged_bias, updated_bias = stepper(
        position_bias, bias_grad, momentum_bias, average_bias, small_rate
    )
    return (
        output,
        tokens_grad,
        memory_grad,
        example_norms,
        velocity_in,
        averaged_in,
        updated_in,
        velocity_out,
        averaged_out,
        updated_out,
        velocity_up,
        averaged_up,
        updated_up,
        velocity_down,
        averaged_down,
        updated_down,
        velocity_gain,
        averaged_gain,
        updated_gain,
        velocity_bias,
        averaged_bias,
        updated_bias,
    )


def solution(mesh):
    return jax.shard_map(
        on_device,
        mesh=mesh,
        in_specs=(
            P("dp", "tensor", None),
            P("dp", "tensor", None),
            P("dp", "tensor", None),
            P("dp", None, None),
            P("dp", None, None),
            P("dp"),
            P(None, "dp", "tensor"),
            P(None, "tensor", "dp"),
            P("dp", "tensor"),
            P("tensor", "dp"),
            P(),
            P(None, "tensor"),
            P(None, "dp", "tensor"),
            P(None, "dp", "tensor"),
            P(None, "tensor", "dp"),
            P(None, "tensor", "dp"),
            P("dp", "tensor"),
            P("dp", "tensor"),
            P("tensor", "dp"),
            P("tensor", "dp"),
            P(None, "tensor"),
            P(None, "tensor"),
            P(None, "tensor"),
            P(None, "tensor"),
        ),
        out_specs=(
            P("dp", "tensor", None),
            P("dp", "tensor", None),
            P("dp", "tensor", None),
            P("dp"),
            P(None, "dp", "tensor"),
            P(None, "dp", "tensor"),
            P(None, "dp", "tensor"),
            P(None, "tensor", "dp"),
            P(None, "tensor", "dp"),
            P(None, "tensor", "dp"),
            P("dp", "tensor"),
            P("dp", "tensor"),
            P("dp", "tensor"),
            P("tensor", "dp"),
            P("tensor", "dp"),
            P("tensor", "dp"),
            P(None, "tensor"),
            P(None, "tensor"),
            P(None, "tensor"),
            P(None, "tensor"),
            P(None, "tensor"),
            P(None, "tensor"),
        ),
        check_vma=False,
    )
```

```python
import functools
import math

import jax
import jax.numpy as jnp
from jax import lax
from jax.experimental import pallas as pl
from jax.experimental.pallas import tpu as pltpu
from jax.sharding import PartitionSpec as P

epsilon = 1e-06
momentum_decay = 0.9
average_decay = 0.7
matrix_rate = 10.0
output_rate = 40.0
small_rate = 50.0
group_limits = (0.6, 0.85, 1.2, 1.7)
head_dim = 64
quad = 4
quad_width = quad * head_dim
dp_slots = 8
tensor_slots = 4
wide = jnp.float32
narrow = jnp.bfloat16
vmem_bytes = 58 * 2**20
cost_scale = 1.0

core = ("tensor", 1)
row = ("tensor", 2)
side = ("dp", 1)
near = ("dp", 2)
far = ("dp", 4)
gather_order = (far, near, row, side, core)
reduce_orders = (
    (core, side, row, near, far),
    (core, row, near, far, side),
    (core, row, side, near, far),
    (core, near, far, side, row),
)
reduce_counts = (5, 3, 3, 5)


def dot_nn(left, right):
    return lax.dot_general(left, right, (((1,), (0,)), ((), ())), preferred_element_type=wide)


def dot_nt(left, right):
    return lax.dot_general(left, right, (((1,), (1,)), ((), ())), preferred_element_type=wide)


def dot_tn(left, right):
    return lax.dot_general(left, right, (((0,), (0,)), ((), ())), preferred_element_type=wide)


def head_masks(dtype):
    lanes = lax.broadcasted_iota(jnp.int32, (1, quad_width), 1) // head_dim
    return [(lanes == head).astype(wide).astype(dtype) for head in range(quad)]


def stack_heads(block, masks):
    return jnp.concatenate([block * mask for mask in masks], 0)


def unstack_heads(block, masks):
    rows = block.shape[0] // quad
    total = block[:rows] * masks[0]
    for head in range(1, quad):
        total = total + block[head * rows : (head + 1) * rows] * masks[head]
    return total


def norm_scale(rows):
    return lax.rsqrt(jnp.mean(rows * rows, -1, keepdims=True) + epsilon)


def norm_back(rows, gain, d_normed):
    scaling = norm_scale(rows)
    weighted = d_normed * gain
    cubed = scaling * scaling * scaling
    d_rows = scaling * weighted - rows * cubed * jnp.mean(rows * weighted, -1, keepdims=True)
    return d_rows, d_normed * rows * scaling


def softmax_keys(scores):
    peak = jnp.max(scores, 0, keepdims=True)
    weights = jnp.exp(scores - peak)
    return weights * (1.0 / jnp.sum(weights, 0, keepdims=True))


def gram_squares(left, right_grams):
    return jnp.sum(dot_nt(left, left) * right_grams, 0, keepdims=True)


def fold_causal(block):
    size = block.shape[0]
    lanes = lax.broadcasted_iota(jnp.int32, (8, size), 1)
    rows = [block[:8], block[size // 2 : size // 2 + 8]]
    for start in range(8, size // 2, 8):
        other = pltpu.roll(block[size - start : size - start + 8], start, 1)
        rows.append(jnp.where(lanes >= start, block[start : start + 8], other))
    return jnp.concatenate(rows, 0)


def fold_lanes(row_sums):
    width = row_sums.shape[1]
    total = row_sums[:, :128]
    for start in range(128, width, 128):
        total = total + row_sums[:, start : start + 128]
    return total


def slot_places(order, first_is_high):
    places = []
    count = len(order)
    for slot in range(1 << count):
        index = {"dp": 0, "tensor": 0}
        for stage, (axis, bit) in enumerate(order):
            place = count - 1 - stage if first_is_high else stage
            if (slot >> place) & 1:
                index[axis] |= bit
        places.append((index["dp"], index["tensor"]))
    return places


def start_weights(info, pieces, plans, held, sems):
    for piece, (first, count, places, relative), sem in zip(pieces, plans, sems):
        for slot, (dp_index, tensor_index) in enumerate(places):
            if relative:
                high = pl.multiple_of((dp_index ^ info[0]) * 64, 64)
                left = pl.multiple_of((tensor_index ^ info[1]) * 128, 128)
            else:
                high, left = dp_index * 64, tensor_index * 128
            pltpu.make_async_copy(
                piece.at[slot],
                held.at[pl.ds(first, count), pl.ds(high, 64), pl.ds(left, 128)],
                sem,
            ).start()


def wait_weights(plans, held, sems):
    for (first, count, places, relative), sem in zip(plans, sems):
        share = 512 * len(places) // (dp_slots * tensor_slots)
        whole = held.at[pl.ds(first, count), pl.ds(0, share)]
        pltpu.make_async_copy(whole, whole, sem).wait()


def place_rows(info, parts, held, first=0):
    rows = held.shape[1] // len(parts)
    for index, part in enumerate(parts):
        start = pl.multiple_of((info[2] ^ index) * rows, rows)
        held[:, pl.ds(start, rows), :] = part[:, first : first + rows, :]


def split_rows(info, held, parts, first=0):
    rows = held.shape[1] // len(parts)
    for index, part in enumerate(parts):
        start = pl.multiple_of((info[2] ^ index) * rows, rows)
        part[:, first : first + rows, :] = held[:, pl.ds(start, rows), :].astype(part.dtype)


def self_forward_kernel(shards, plans, heads_local, *refs):
    refs = list(refs)

    def take(count):
        taken = refs[:count]
        del refs[:count]
        return taken

    (info,) = take(1)
    parts = take(shards)
    buckets, key_mask, gains, table = take(4)
    pieces = take(len(plans))
    normed_out, rows_out, qkv_out, weights_out, mix_out, mid_out = take(6)
    held, sems, rows_held, mix_held = take(4)
    sem_list = [sems.at[index] for index in range(len(plans))]

    @pl.when(pl.program_id(0) == 0)
    def _():
        start_weights(info, pieces, plans, held, sem_list)
        wait_weights(plans, held, sem_list)

    masks = head_masks(narrow)
    masks_wide = head_masks(wide)
    place_rows(info, parts, rows_held)
    rows_out[...] = rows_held[...]
    bundle, seq, width = rows_held.shape
    flat = rows_held[...].reshape(bundle * seq, width).astype(wide)
    normed = (flat * norm_scale(flat) * gains[0:1, :]).astype(narrow)
    normed_out[...] = normed.reshape(bundle, seq, width)
    for index in range(3):
        value = dot_nn(normed, held[index]).astype(narrow)
        qkv_out[index] = value.reshape(bundle, seq, width)
    for example in range(bundle):
        code = jnp.where(key_mask[example] > 0, buckets[example], -1).T
        safe = jnp.maximum(code, 0)
        code_all = jnp.concatenate([code] * quad, 1)
        for group in range(width // quad_width):
            columns = slice(group * quad_width, (group + 1) * quad_width)
            bias = []
            for head in range(group * quad, (group + 1) * quad):
                spot = ((head // heads_local) ^ info[2]) * heads_local + head % heads_local
                line = jnp.broadcast_to(table[pl.ds(spot, 1), :], (seq, 128))
                bias.append(jnp.take_along_axis(line, safe, axis=1))
            queries = stack_heads(qkv_out[0, example, :, columns], masks)
            scores = dot_nt(qkv_out[1, example, :, columns], queries) * (
                1.0 / math.sqrt(head_dim)
            ) + jnp.concatenate(bias, 1)
            weights = softmax_keys(jnp.where(code_all >= 0, scores, -1000000000.0))
            weights_out[example, group] = weights
            mixture = dot_tn(weights.astype(narrow), qkv_out[2, example, :, columns])
            mix_held[example, :, columns] = unstack_heads(mixture, masks_wide).astype(narrow)
    mix_out[...] = mix_held[...]
    mix = mix_held[...].reshape(bundle * seq, width)
    mid_out[...] = (flat + dot_nt(mix, held[3])).reshape(bundle, seq, width)


def cross_kernel(shards, plans, soon, aliased, *refs):
    refs = list(refs)

    def take(count):
        taken = refs[:count]
        del refs[:count]
        return taken

    (info,) = take(1)
    memory_parts = take(shards)
    mid_in, gains = take(2)
    pieces = take(len(plans))
    take(aliased)
    own_output, own_grad = take(2)
    sent_parts = take(shards - 1)
    (
        early_out,
        normed_b_out,
        d_query_out,
        d_pair_out,
        mix_out,
        d_mid_out,
        normed_c_out,
        d_hidden_out,
        active_out,
        d_top_out,
        d_gain_b_out,
        d_gain_c_out,
        squares_out,
    ) = take(13)
    d_keys_out, d_values_out = d_pair_out.at[0], d_pair_out.at[1]
    held, sems, memory_held, keys_held, values_held, weights_held, rows_held, query_held = take(8)
    sem_list = [sems.at[index] for index in range(len(plans))]

    @pl.when(pl.program_id(0) == 0)
    def _():
        start_weights(info, pieces, plans, held, sem_list)
        wait_weights(plans[:soon], held, sem_list[:soon])

    masks = head_masks(narrow)
    masks_wide = head_masks(wide)
    scaling = 1.0 / math.sqrt(head_dim)
    bundle, seq, width = mid_in.shape
    memory_len = memory_held.shape[1]
    memory_rows = memory_len // shards
    groups = width // quad_width

    def flatten(block):
        return block.reshape(block.shape[0] * block.shape[1], block.shape[2])

    def unflatten(block):
        return block.reshape(bundle, block.shape[0] // bundle, block.shape[1])

    for index, part in enumerate(memory_parts):
        memory_held[:, index * memory_rows : (index + 1) * memory_rows, :] = part[
            :, :memory_rows, :
        ]
    place_rows(info, memory_parts, d_top_out, memory_rows)
    mid = flatten(mid_in[...])
    rows_b = mid.astype(narrow).astype(wide)
    normed_b = (rows_b * norm_scale(rows_b) * gains[1:2, :]).astype(narrow)
    normed_b_out[...] = unflatten(normed_b)
    query_held[...] = unflatten(dot_nn(normed_b, held[0]).astype(narrow))
    memory_flat = flatten(memory_held[...])
    keys_held[...] = unflatten(dot_nn(memory_flat, held[1]).astype(narrow))
    values_held[...] = unflatten(dot_nn(memory_flat, held[2]).astype(narrow))
    for example in range(bundle):
        for group in range(groups):
            columns = slice(group * quad_width, (group + 1) * quad_width)
            queries = stack_heads(query_held[example, :, columns], masks)
            scores = dot_nt(keys_held[example, :, columns], queries) * scaling
            weights = softmax_keys(scores)
            weights_held[example, group] = weights
            mixture = dot_tn(weights.astype(narrow), values_held[example, :, columns])
            mix_out[example, :, columns] = unstack_heads(mixture, masks_wide).astype(narrow)
    late = mid + dot_nt(flatten(mix_out[...]), held[3])

    @pl.when(pl.program_id(0) == 0)
    def _():
        wait_weights(plans[soon:], held, sem_list[soon:])

    rows_c = late.astype(narrow).astype(wide)
    normed_c = (rows_c * norm_scale(rows_c) * gains[2:3, :]).astype(narrow)
    normed_c_out[...] = unflatten(normed_c)
    d_top = flatten(d_top_out[...])
    total = late
    d_normed = jnp.zeros((bundle * seq, width), wide)
    up_grams = [jnp.zeros((seq, seq), wide) for _ in range(bundle)]
    down_grams = [jnp.zeros((seq, seq), wide) for _ in range(bundle)]
    slope = math.sqrt(2.0 / math.pi)
    for index in range(4):
        hidden = dot_nn(normed_c, held[4 + index])
        square = hidden * hidden
        bend = jnp.tanh(slope * hidden * (1.0 + 0.044715 * square))
        half = 0.5 * (1.0 + bend)
        active = (hidden * half).astype(narrow)
        steep = half + 0.5 * hidden * (1.0 - bend * bend) * (
            slope * (1.0 + (3.0 * 0.044715) * square)
        )
        total = total + dot_nt(active, held[8 + index])
        d_hidden = (dot_nn(d_top, held[8 + index]) * steep).astype(narrow)
        d_normed = d_normed + dot_nt(d_hidden, held[4 + index])
        active_out[index] = unflatten(active)
        d_hidden_out[index] = unflatten(d_hidden)
        for example in range(bundle):
            span = slice(example * seq, (example + 1) * seq)
            up_grams[example] += dot_nt(d_hidden[span], d_hidden[span])
            down_grams[example] += dot_nt(active[span], active[span])
    rows_held[...] = unflatten(total)
    for index in range(shards):
        start = pl.multiple_of((info[2] ^ index) * (seq // shards), seq // shards)
        block = rows_held[:, pl.ds(start, seq // shards), :].astype(narrow)
        if index:
            sent_parts[index - 1][:, memory_rows:, :] = block
        else:
            own_output[...] = block
    d_rows, d_gain_rows = norm_back(rows_c, gains[2:3, :], d_normed)
    d_gain_c = jnp.sum(unflatten(d_gain_rows), 1, keepdims=True)
    d_gain_c_out[...] = d_gain_c
    d_mid = d_top.astype(wide) + d_rows
    d_mid_low = d_mid.astype(narrow)
    d_mid_out[...] = unflatten(d_mid_low)
    d_mix = dot_nn(d_mid_low, held[3]).astype(narrow)
    squares = []
    for example in range(bundle):
        span = slice(example * seq, (example + 1) * seq)
        for group in range(groups):
            columns = slice(group * quad_width, (group + 1) * quad_width)
            keys = keys_held[example, :, columns]
            queries = stack_heads(query_held[example, :, columns], masks)
            d_mixes = stack_heads(d_mix[span, columns], masks)
            weights = weights_held[example, group]
            d_weights = dot_nt(values_held[example, :, columns], d_mixes)
            inner = jnp.sum(weights * d_weights, 0, keepdims=True)
            d_scores = (weights * (d_weights - inner)).astype(narrow)
            d_query_out[example, :, columns] = (
                unstack_heads(dot_tn(d_scores, keys), masks_wide) * scaling
            ).astype(narrow)
            d_keys_out[example, :, columns] = (dot_nn(d_scores, queries) * scaling).astype(narrow)
            d_values_out[example, :, columns] = dot_nn(weights.astype(narrow), d_mixes).astype(
                narrow
            )
        memory_grad = dot_nt(d_keys_out[example], held[1]) + dot_nt(d_values_out[example], held[2])
        own_grad[example] = memory_grad[:memory_rows]
        for index, part in enumerate(sent_parts):
            part[example, :memory_rows, :] = memory_grad[
                (index + 1) * memory_rows : (index + 2) * memory_rows
            ].astype(narrow)
        d_query = d_query_out[example]
        mix = mix_out[example]
        square_sum = gram_squares(normed_b[span], dot_nt(d_query, d_query))
        square_sum += gram_squares(mix, dot_nt(d_mid_low[span], d_mid_low[span]))
        square_sum += gram_squares(normed_c[span], up_grams[example])
        square_sum += gram_squares(d_top[span], down_grams[example])
        for block in (d_keys_out, d_values_out):
            product = dot_tn(memory_held[example], block[example])
            square_sum += fold_lanes(jnp.sum(product * product, 0, keepdims=True))
        square_sum += fold_lanes(d_gain_c[example] * d_gain_c[example])
        squares.append(square_sum)
    d_normed_b = dot_nt(flatten(d_query_out[...]), held[0])
    d_rows_b, d_gain_rows = norm_back(rows_b, gains[1:2, :], d_normed_b)
    d_gain_b = jnp.sum(unflatten(d_gain_rows), 1, keepdims=True)
    d_gain_b_out[...] = d_gain_b
    for example in range(bundle):
        squares_out[example] = squares[example] + fold_lanes(
            d_gain_b[example] * d_gain_b[example]
        )
    early_out[...] = unflatten(d_mid + d_rows_b)


def self_backward_kernel(shards, plans, *refs):
    refs = list(refs)

    def take(count):
        taken = refs[:count]
        del refs[:count]
        return taken

    info, early_in, rows_in, normed_in, qkv_in, weights_in, mix_in = take(7)
    squares_in, d_gain_b, d_gain_c, buckets, gains = take(5)
    pieces = take(len(plans))
    tokens_grads = take(shards)
    d_qkv_out, d_early_out, small_out, norms_out = take(4)
    held, sems, rows_held, bias_held, folded_held = take(5)
    sem_list = [sems.at[index] for index in range(len(plans))]

    @pl.when(pl.program_id(0) == 0)
    def _():
        start_weights(info, pieces, plans, held, sem_list)
        wait_weights(plans, held, sem_list)

    masks = head_masks(narrow)
    masks_wide = head_masks(wide)
    scaling = 1.0 / math.sqrt(head_dim)
    bundle, seq, width = early_in.shape
    groups = width // quad_width
    bucket_count = bias_held.shape[0] // (groups * quad)

    def flatten(block):
        return block.reshape(block.shape[0] * block.shape[1], block.shape[2])

    def unflatten(block):
        return block.reshape(bundle, block.shape[0] // bundle, block.shape[1])

    early = flatten(early_in[...])
    d_early = early.astype(narrow)
    d_early_out[...] = unflatten(d_early)
    d_mix = dot_nn(d_early, held[3]).astype(narrow)
    squares = []
    for example in range(bundle):
        span = slice(example * seq, (example + 1) * seq)
        code = buckets[example].T
        for group in range(groups):
            columns = slice(group * quad_width, (group + 1) * quad_width)
            keys = qkv_in[1, example, :, columns]
            queries = stack_heads(qkv_in[0, example, :, columns], masks)
            d_mixes = stack_heads(d_mix[span, columns], masks)
            weights = weights_in[example, group]
            d_weights = dot_nt(qkv_in[2, example, :, columns], d_mixes)
            inner = jnp.sum(weights * d_weights, 0, keepdims=True)
            d_scores = (weights * (d_weights - inner)).astype(narrow)
            d_qkv_out[0, example, :, columns] = (
                unstack_heads(dot_tn(d_scores, keys), masks_wide) * scaling
            ).astype(narrow)
            d_qkv_out[1, example, :, columns] = (dot_nn(d_scores, queries) * scaling).astype(
                narrow
            )
            d_qkv_out[2, example, :, columns] = dot_nn(weights.astype(narrow), d_mixes).astype(
                narrow
            )
            d_wide = d_scores.astype(wide)
            for head in range(quad):
                folded_held[group * quad + head] = fold_causal(
                    d_wide[:, head * seq : (head + 1) * seq]
                )
        code = fold_causal(code)
        for bucket in range(bucket_count):
            chosen = code == bucket
            for head in range(groups * quad):
                picked = jnp.where(chosen, folded_held[head], 0.0)
                spot = head * bucket_count + bucket
                bias_held[spot : spot + 1, :] = jnp.sum(picked, 0, keepdims=True)
        d_bias = lax.dot_general(
            jnp.ones((8, 128), wide),
            bias_held[...],
            (((1,), (1,)), ((), ())),
            precision=lax.Precision.HIGHEST,
            preferred_element_type=wide,
        )[:1]
        small_out[example, :, 3 * width :] = d_bias
        grams = jnp.zeros((seq, seq), wide)
        for index in range(3):
            block = d_qkv_out[index, example]
            grams = grams + dot_nt(block, block)
        square_sum = gram_squares(normed_in[example], grams)
        square_sum += gram_squares(mix_in[example], dot_nt(d_early[span], d_early[span]))
        square_sum += fold_lanes(d_bias * d_bias)
        squares.append(square_sum)
    d_normed = dot_nt(flatten(d_qkv_out[0]), held[0])
    d_normed = d_normed + dot_nt(flatten(d_qkv_out[1]), held[1])
    d_normed = d_normed + dot_nt(flatten(d_qkv_out[2]), held[2])
    d_rows, d_gain_rows = norm_back(flatten(rows_in[...]).astype(wide), gains[0:1, :], d_normed)
    d_gain = jnp.sum(unflatten(d_gain_rows), 1, keepdims=True)
    small_out[:, :, :width] = d_gain
    small_out[:, :, width : 2 * width] = d_gain_b[...]
    small_out[:, :, 2 * width : 3 * width] = d_gain_c[...]
    for example in range(bundle):
        square_sum = (
            squares[example]
            + squares_in[example]
            + fold_lanes(d_gain[example] * d_gain[example])
        )
        total = jnp.sum(square_sum, -1, keepdims=True) + epsilon
        norms_out[example] = jnp.broadcast_to(jnp.sqrt(total), (1, 128))
    rows_held[...] = unflatten(early + d_rows)
    split_rows(info, rows_held, tokens_grads)


class Gradients:
    def __init__(self, info, clip, loads, load_sems, scaled, tile, held, store_sems):
        self.info, self.clip, self.scaled = info, clip, scaled
        self.tile, self.held, self.store_sems = tile, held, store_sems
        self.copies = [
            pltpu.make_async_copy(source, target, load_sems.at[index])
            for index, (source, target) in enumerate(loads)
        ]
        self.targets = [target for source, target in loads]
        self.stores = []
        for copy in self.copies:
            copy.start()

    def read(self, index):
        self.copies[index].wait()
        return self.targets[index]

    def scale(self, index):
        block = self.read(index)
        count, rows, width = block.shape
        for example in range(count):
            self.scaled[example * rows : (example + 1) * rows, :] = (
                block[example].astype(wide) * self.clip[example]
            ).astype(narrow)

    def product(self, index):
        block = self.read(index)
        return dot_tn(self.scaled[...], block[...].reshape(self.scaled.shape[0], block.shape[-1]))

    def write(self, value, outs, unit, places):
        number = len(self.stores) // 2
        tile = self.tile.at[number % 2]
        tile[...] = value.astype(narrow)
        halves = self.held.at[number]
        count = len(places) // 2
        for slot, (dp_index, tensor_index) in enumerate(places):
            high = pl.multiple_of((dp_index ^ self.info[0]) * 64, 64)
            left = pl.multiple_of((tensor_index ^ self.info[1]) * 128, 128)
            halves[slot // count, slot % count] = tile[pl.ds(high, 64), pl.ds(left, 128)]
        for half, out in enumerate(outs):
            copy = pltpu.make_async_copy(
                halves.at[half], out.at[:, unit], self.store_sems.at[len(self.stores)]
            )
            copy.start()
            self.stores.append(copy)

    def finish(self):
        for copy in self.stores:
            copy.wait()


def inner_gradient_kernel(places, info, clip, normed, d_hidden, d_top, active, *refs):
    outs = (refs[:2], refs[2:4])
    rows_held, blocks_held, load_sems, scaled, tile, held, store_sems = refs[4:]
    loads = []
    for piece, (left, right) in enumerate(((normed, d_hidden), (d_top, active))):
        loads.append((left, rows_held.at[piece]))
        loads += [(right.at[unit], blocks_held.at[4 * piece + unit]) for unit in range(4)]
    work = Gradients(info, clip, loads, load_sems, scaled, tile, held, store_sems)
    for piece in range(2):
        work.scale(5 * piece)
        for unit in range(4):
            spot = 4 * piece + unit
            out = int(spot >= reduce_counts[0])
            spot -= out * reduce_counts[0]
            work.write(work.product(5 * piece + 1 + unit), outs[out], spot, places[out])
    work.finish()


def attention_gradient_kernel(shards, chunks, places, info, clip, *refs):
    normed_a, d_qkv, d_early, mix_a, normed_b, d_query, d_mid, mix_b = refs[:8]
    parts = refs[8 : 8 + shards * chunks]
    refs = refs[8 + shards * chunks :]
    d_pair = refs[0]
    self_out, cross_out = refs[1:3], refs[3:5]
    rows_held, parts_held, pairs_held, memory_held = refs[5:9]
    load_sems, scaled, tile, held, store_sems = refs[9:]
    count, memory_len = d_pair.shape[1:3]
    part_len = memory_len // shards
    group = count // chunks
    sources = [normed_a, d_qkv.at[0], d_qkv.at[1], d_qkv.at[2], d_early, mix_a]
    sources += [normed_b, d_query, d_mid, mix_b]
    loads = [(source, rows_held.at[index]) for index, source in enumerate(sources)]
    first = len(loads)
    for chunk in range(chunks):
        for index in range(shards):
            place = chunk * shards + index
            loads.append((parts[place].at[:, pl.ds(0, part_len)], parts_held.at[place]))
        for unit in range(2):
            loads.append(
                (d_pair.at[unit, pl.ds(chunk * group, group)], pairs_held.at[2 * chunk + unit])
            )
    work = Gradients(info, clip, loads, load_sems, scaled, tile, held, store_sems)
    work.scale(0)
    for unit in range(3):
        work.write(work.product(1 + unit), self_out, unit, places[0])
    work.scale(4)
    work.write(work.product(5), cross_out, 0, places[1])
    work.scale(6)
    work.write(work.product(7), cross_out, 1, places[1])
    work.scale(8)
    work.write(work.product(9), cross_out, 2, places[1])
    totals = [None, None]
    for chunk in range(chunks):
        start = first + chunk * (shards + 2)
        for index in range(shards):
            block = work.read(start + index)
            for example in range(group):
                top = (example * shards + index) * part_len
                memory_held[chunk, top : top + part_len, :] = (
                    block[example].astype(wide) * clip[chunk * group + example]
                ).astype(narrow)
        for unit in range(2):
            pair = work.read(start + shards + unit)
            product = dot_tn(
                memory_held[chunk], pair[...].reshape(group * memory_len, pair.shape[-1])
            )
            totals[unit] = product if chunk == 0 else totals[unit] + product
    for unit in range(2):
        work.write(totals[unit], cross_out, 3 + unit, places[1])
    work.finish()


def stepper(parameter, gradient, momentum, average, step_rate):
    velocity = momentum_decay * momentum + gradient
    updated = parameter - step_rate * (gradient + momentum_decay * velocity)
    averaged = average_decay * average + (1.0 - average_decay) * updated
    return (velocity, averaged, updated)


def update_kernel(shrink, *refs):
    sums = refs[:8]
    params, outs = refs[8:20], refs[20:]

    def gradient(piece, unit):
        total = sums[2 * piece][unit].astype(wide) + sums[2 * piece + 1][unit].astype(wide)
        return total * shrink

    def step(group, spot, value, rate):
        weight, momentum, average = params[3 * group : 3 * group + 3]
        stepped = stepper(weight[spot], value, momentum[spot], average[spot], rate)
        for out, block in zip(outs[3 * group : 3 * group + 3], stepped):
            out[spot] = block

    inside = ((2, 0), (2, 1), (2, 2), (3, 1), (3, 3), (3, 4))
    for index, (piece, unit) in enumerate(inside):
        step(0, index, gradient(piece, unit), matrix_rate)
    for index, unit in enumerate((0, 2)):
        step(1, index, gradient(3, unit), output_rate)
    for index in range(4):
        spot = (slice(None), slice(128 * index, 128 * (index + 1)))
        step(2, spot, gradient(0, index), matrix_rate)
        piece, unit = (1, index - 1) if index else (0, 4)
        step(3, spot, gradient(piece, unit), matrix_rate)


def assemble_kernel(shards, chunks, *refs):
    refs = list(refs[1:])

    def take(count):
        taken = refs[:count]
        del refs[:count]
        return taken

    arrived = [take(shards - 1) for _ in range(chunks)]
    tokens_parts = take(shards - 1)
    take(3)
    output, tokens_grad, memory_grad = refs
    rows = memory_grad.shape[1]
    for index in range(shards - 1):
        for chunk in range(chunks):

            @pl.when((pl.program_id(0) == index) & (pl.program_id(1) == chunk))
            def _(index=index, chunk=chunk):
                tokens_grad[...] = tokens_parts[index][...].astype(wide)
                block = arrived[chunk][index]
                output[...] = block[:, rows:, :]
                memory_grad[...] = block[:, :rows, :].astype(wide)


def swap(value, axis, bit):
    size = lax.axis_size(axis)
    return lax.ppermute(value, axis, [(index, index ^ bit) for index in range(size)])


def after(value, *earlier):
    return lax.optimization_barrier((value,) + earlier)[0]


def gather_slots(shard):
    gathered = shard[None]
    for axis, bit in gather_order[:3]:
        gathered = jnp.concatenate([gathered, swap(gathered, axis, bit)], 0)
    beside = swap(gathered, *gather_order[3])
    pieces = [gathered, beside, swap(gathered, *gather_order[4]), swap(beside, *gather_order[4])]
    places = slot_places(gather_order, False)
    count = len(places) // 4
    return [
        (piece, places[index * count : (index + 1) * count]) for index, piece in enumerate(pieces)
    ]


def add_stage(kept, arrived):
    half = kept.shape[0] // 2

    def added(start, stop):
        total = kept[start:stop].astype(wide) + arrived[start:stop].astype(wide)
        return total.astype(narrow)

    if not half:
        return added(0, 1)[0], None
    return added(0, half), added(half, 2 * half)


def on_device(
    tokens,
    memory,
    cotangent,
    buckets,
    key_mask,
    task_groups,
    weights_in,
    weights_out,
    weights_up,
    weights_down,
    gains,
    position_bias,
    momentum_in,
    average_in,
    momentum_out,
    average_out,
    momentum_up,
    average_up,
    momentum_down,
    average_down,
    momentum_gain,
    average_gain,
    momentum_bias,
    average_bias,
):
    shards = lax.axis_size("tensor")
    replicas = lax.axis_size("dp")
    me_tensor = lax.axis_index("tensor")
    me_dp = lax.axis_index("dp")
    width = tokens.shape[2]
    seq = buckets.shape[1]
    seq_rows = tokens.shape[1]
    memory_rows = memory.shape[1]
    memory_len = memory_rows * shards
    group_count = tokens.shape[0]
    local = group_count // shards
    chunks = 2 if local % 2 == 0 else 1
    per_chunk = local // chunks
    bundle = 2 if per_chunk % 2 == 0 else 1
    steps = per_chunk // bundle
    bucket_count, heads_local = position_bias.shape
    heads = heads_local * shards
    gain_width = momentum_gain.shape[1]
    staged = shards == tensor_slots and replicas == dp_slots

    slot_base = [me_dp, me_tensor] if staged else [0 * me_dp, 0 * me_tensor]
    kernel_info = jnp.stack(slot_base + [me_tensor]).astype(jnp.int32)

    def square_shards():
        high, across = weights_in.shape[1], weights_in.shape[2]
        split = lambda block: block.reshape(high, -1, across).transpose(1, 0, 2)
        return (
            weights_in.astype(narrow),
            weights_out.astype(narrow).transpose(0, 2, 1),
            split(weights_up.astype(narrow)),
            split(weights_down.astype(narrow).T),
        )

    shard_in, shard_out, shard_up, shard_down = square_shards()
    slot_count = dp_slots * tensor_slots
    plain_places = [(slot // tensor_slots, slot % tensor_slots) for slot in range(slot_count)]

    def gather_late(blocks):
        count = blocks.shape[0]
        if staged:
            whole = lax.all_gather(blocks, ("dp", "tensor"), axis=0)
        else:
            whole = lax.all_gather(blocks, "dp", axis=1, tiled=True)
            whole = lax.all_gather(whole, "tensor", axis=2, tiled=True)
            whole = whole.reshape(count, dp_slots, 64, tensor_slots, 128).transpose(1, 3, 0, 2, 4)
            whole = whole.reshape(slot_count, count, 64, 128)
        return [whole], [(0, count, plain_places, False)]

    def gather_soon(blocks):
        if not staged:
            return gather_late(blocks)
        pieces, plans = [], []
        for piece, places in gather_slots(blocks):
            pieces.append(piece)
            plans.append((0, blocks.shape[0], places, True))
        return pieces, plans

    def exchange(values, start, count):
        found = []
        for index in range(shards):
            first = (me_tensor ^ index) * local + start
            blocks = [lax.dynamic_slice_in_dim(value, first, count, 0) for value in values]
            block = jnp.concatenate(blocks, 1) if len(blocks) > 1 else blocks[0]
            found.append(swap(block, "tensor", index) if index else block)
        return found

    late_pieces, late_plans = gather_late(jnp.concatenate([shard_up, shard_down], 0))
    token_parts = exchange([tokens], 0, local)
    self_pieces, self_plans = gather_soon(jnp.concatenate([shard_in[:3], shard_out[:1]], 0))
    cross_pieces, cross_plans = gather_soon(jnp.concatenate([shard_in[3:6], shard_out[1:2]], 0))
    late_plans = cross_plans + [(4,) + plan[1:] for plan in late_plans]
    late_pieces = cross_pieces + late_pieces
    soon_count = len(cross_pieces)
    table = jnp.pad(position_bias.T, ((0, 0), (0, 128 - bucket_count)))
    table_all = jnp.concatenate(
        [swap(table, "tensor", index) if index else table for index in range(shards)], 0
    )
    memory_parts = []
    earlier = token_parts
    for chunk in range(chunks):
        source, _ = lax.optimization_barrier((memory, earlier[-1]))
        earlier = exchange([source, cotangent], chunk * per_chunk, per_chunk)
        memory_parts.append(earlier)
    bucket_mine = lax.dynamic_slice_in_dim(buckets, me_tensor * local, local, 0)
    mask_mine = lax.dynamic_slice_in_dim(key_mask, me_tensor * local, local, 0)
    groups_mine = lax.dynamic_slice_in_dim(task_groups, me_tensor * local, local, 0)

    smem = pl.BlockSpec(memory_space=pltpu.SMEM)
    anywhere = pl.BlockSpec(memory_space=pl.ANY)
    params = pltpu.CompilerParams(
        vmem_limit_bytes=vmem_bytes, dimension_semantics=("arbitrary",)
    )

    def part_spec(shape, offset=0, lead=None):
        zeros = (0,) * len(shape)
        if lead is None:
            return pl.BlockSpec(
                (bundle,) + tuple(shape), lambda step, *_: (step + offset,) + zeros
            )
        return pl.BlockSpec(
            (lead, bundle) + tuple(shape), lambda step, *_: (0, step + offset) + zeros
        )

    def own_spec(shape, offset=0):
        zeros = (0,) * len(shape)
        return pl.BlockSpec(
            (bundle,) + tuple(shape),
            lambda step, info: (info[2] * (local // bundle) + step + offset,) + zeros,
        )

    def whole_spec(shape):
        return pl.BlockSpec(tuple(shape), lambda step, *_: (0,) * len(shape))

    def shaped(shape, dtype, lead=None, count=local):
        front = (count,) if lead is None else (lead, count)
        return jax.ShapeDtypeStruct(front + tuple(shape), dtype)

    def cost(flops, moved):
        return pl.CostEstimate(
            flops=int(flops * cost_scale), bytes_accessed=int(moved * cost_scale), transcendentals=0
        )

    groups = width // quad_width
    row_block = (seq, width)
    part_rows = memory_rows + seq_rows

    normed_a, rows_a, qkv_a, weights_a, mix_a, mid = pl.pallas_call(
        functools.partial(self_forward_kernel, shards, self_plans, heads_local),
        grid=(local // bundle,),
        in_specs=[smem]
        + [part_spec((seq_rows, width))] * shards
        + [part_spec((seq, seq))] * 2
        + [whole_spec(gains.shape), whole_spec(table_all.shape)]
        + [anywhere] * len(self_pieces),
        out_specs=[
            part_spec(row_block),
            part_spec(row_block),
            part_spec(row_block, lead=3),
            part_spec((groups, seq, quad * seq)),
            part_spec(row_block),
            part_spec(row_block),
        ],
        out_shape=[
            shaped(row_block, narrow),
            shaped(row_block, narrow),
            shaped(row_block, narrow, 3),
            shaped((groups, seq, quad * seq), wide),
            shaped(row_block, narrow),
            shaped(row_block, wide),
        ],
        scratch_shapes=[
            pltpu.VMEM((4, width, width), narrow),
            pltpu.SemaphoreType.DMA((len(self_pieces),)),
            pltpu.VMEM((bundle,) + row_block, narrow),
            pltpu.VMEM((bundle,) + row_block, narrow),
        ],
        compiler_params=params,
        name="self_forward",
        cost_estimate=cost(local * 2e9, local * 2e6),
    )(
        kernel_info,
        *token_parts,
        bucket_mine,
        mask_mine,
        gains,
        table_all,
        *self_pieces,
    )

    def cross(chunk, filled):
        offset = chunk * steps
        gain_block = (1, width)
        kept_specs = [
            part_spec(row_block, offset),
            part_spec(row_block, offset),
            part_spec(row_block, offset),
            part_spec((memory_len, width), offset, 2),
            part_spec(row_block, offset),
            part_spec(row_block, offset),
            part_spec(row_block, offset),
            part_spec(row_block, offset, 4),
            part_spec(row_block, offset, 4),
            part_spec(row_block, offset),
            part_spec(gain_block, offset),
            part_spec(gain_block, offset),
            part_spec((1, 128), offset),
        ]
        kept_shapes = [
            shaped(row_block, wide),
            shaped(row_block, narrow),
            shaped(row_block, narrow),
            shaped((memory_len, width), narrow, 2),
            shaped(row_block, narrow),
            shaped(row_block, narrow),
            shaped(row_block, narrow),
            shaped(row_block, narrow, 4),
            shaped(row_block, narrow, 4),
            shaped(row_block, narrow),
            shaped(gain_block, wide),
            shaped(gain_block, wide),
            shaped((1, 128), wide),
        ]
        own_specs = [own_spec((seq_rows, width), offset), own_spec((memory_rows, width), offset)]
        own_shapes = [
            shaped((seq_rows, width), narrow, count=group_count),
            shaped((memory_rows, width), wide, count=group_count),
        ]
        operands = [kernel_info, *memory_parts[chunk], mid, gains, *late_pieces]
        aliases = {}
        for index, block in enumerate(filled):
            aliases[len(operands) + index] = index if index < 2 else index + shards - 1
        return pl.pallas_call(
            functools.partial(cross_kernel, shards, late_plans, soon_count, len(filled)),
            grid_spec=pltpu.PrefetchScalarGridSpec(
                num_scalar_prefetch=1,
                grid=(steps,),
                in_specs=[part_spec((part_rows, width))] * shards
                + [part_spec(row_block, offset), whole_spec(gains.shape)]
                + [anywhere] * (len(late_pieces) + len(filled)),
                out_specs=own_specs + [part_spec((part_rows, width))] * (shards - 1) + kept_specs,
                scratch_shapes=[
                    pltpu.VMEM((12, width, width), narrow),
                    pltpu.SemaphoreType.DMA((len(late_pieces),)),
                    pltpu.VMEM((bundle, memory_len, width), narrow),
                    pltpu.VMEM((bundle, memory_len, width), narrow),
                    pltpu.VMEM((bundle, memory_len, width), narrow),
                    pltpu.VMEM((bundle, groups, memory_len, quad * seq), wide),
                    pltpu.VMEM((bundle,) + row_block, wide),
                    pltpu.VMEM((bundle,) + row_block, narrow),
                ],
            ),
            out_shape=own_shapes
            + [shaped((part_rows, width), narrow, count=per_chunk)] * (shards - 1)
            + kept_shapes,
            input_output_aliases=aliases,
            compiler_params=params,
            name="cross",
            cost_estimate=cost(per_chunk * 8e9, per_chunk * 6e6),
        )(*operands, *filled)

    filled, sent = [], []
    for chunk in range(chunks):
        found = cross(chunk, filled)
        sent.append(found[2 : shards + 1])
        filled = list(found[:2]) + list(found[shards + 1 :])
    own_output, own_memory = filled[:2]
    (
        early,
        normed_b,
        d_query_b,
        d_pair,
        mix_b,
        d_mid,
        normed_c,
        d_hidden,
        active,
        d_top,
        d_gain_b,
        d_gain_c,
        squares,
    ) = filled[2:]
    arrived = [
        [swap(block, "tensor", index + 1) for index, block in enumerate(blocks)] for blocks in sent
    ]
    soon = [block for blocks in arrived[:-1] for block in blocks]

    found = pl.pallas_call(
        functools.partial(self_backward_kernel, shards, self_plans),
        grid_spec=pltpu.PrefetchScalarGridSpec(
            num_scalar_prefetch=1,
            grid=(local // bundle,),
            in_specs=[
            part_spec(row_block),
            part_spec(row_block),
            part_spec(row_block),
            part_spec(row_block, lead=3),
            part_spec((groups, seq, quad * seq)),
            part_spec(row_block),
            part_spec((1, 128)),
            part_spec((1, width)),
            part_spec((1, width)),
            part_spec((seq, seq)),
            whole_spec(gains.shape),
        ]
        + [anywhere] * len(self_pieces),
        out_specs=[own_spec((seq_rows, width))]
        + [part_spec((seq_rows, width))] * (shards - 1)
        + [
            part_spec(row_block, lead=3),
            part_spec(row_block),
            part_spec((1, 3 * width + heads * bucket_count)),
            part_spec((1, 128)),
        ],
        scratch_shapes=[
            pltpu.VMEM((4, width, width), narrow),
            pltpu.SemaphoreType.DMA((len(self_pieces),)),
            pltpu.VMEM((bundle,) + row_block, wide),
            pltpu.VMEM((heads * bucket_count, 128), wide),
            pltpu.VMEM((heads, seq // 2 + 8, seq), wide),
        ],
        ),
        out_shape=[shaped((seq_rows, width), wide, count=group_count)]
        + [shaped((seq_rows, width), narrow)] * (shards - 1)
        + [
            shaped(row_block, narrow, 3),
            shaped(row_block, narrow),
            shaped((1, 3 * width + heads * bucket_count), wide),
            shaped((1, 128), wide),
        ],
        compiler_params=params,
        name="self_backward",
        cost_estimate=cost(local * 3e9, local * 3e6),
    )(
        after(kernel_info, *soon),
        early,
        rows_a,
        normed_a,
        qkv_a,
        weights_a,
        mix_a,
        squares,
        d_gain_b,
        d_gain_c,
        bucket_mine,
        gains,
        *self_pieces,
    )
    own_tokens, tokens_sent = found[0], found[1:shards]
    d_qkv, d_early, small, norms = found[shards:]

    norms = after(norms.reshape(local, 128), *arrived[-1])
    norm_slots = norms
    bit = 1
    while bit < shards:
        norm_slots = jnp.concatenate([norm_slots, swap(norm_slots, "tensor", bit)], 0)
        bit *= 2
    total = jnp.broadcast_to(jnp.sum(norm_slots, 0, keepdims=True), (8, 128))
    bit = 1
    while bit < replicas:
        total = total + swap(total, "dp", bit)
        bit *= 2
    order = jnp.arange(shards, dtype=jnp.int32) ^ me_tensor
    example_norms = norm_slots[:, 0].reshape(shards, local)[order].reshape(group_count)
    mean_norm = total[0, 0] / (group_count * replicas)
    limits = jnp.sum(
        (groups_mine[:, None] == jnp.arange(len(group_limits), dtype=jnp.int32))
        * jnp.asarray(group_limits, wide),
        1,
    )
    clip_weights = jnp.minimum(1.0 / mean_norm, limits / norms[:, 0])
    small = jnp.sum(clip_weights[:, None, None] * small, 0).reshape(-1, 128)

    def places_of(index):
        return slot_places(reduce_orders[index], True) if staged else plain_places

    out_shapes = [
        jax.ShapeDtypeStruct((slot_count // 2, count, 64, 128), narrow) for count in reduce_counts
    ]

    def gradient_call(kernel, clip, operands, outs, loads, extra, name, work):
        return pl.pallas_call(
            kernel,
            in_specs=[smem, smem] + [anywhere] * len(operands),
            out_specs=[anywhere] * 4,
            out_shape=[shape for shape in outs for _ in range(2)],
            scratch_shapes=extra
            + [
                pltpu.SemaphoreType.DMA((loads,)),
                pltpu.VMEM((local * seq, width), narrow),
                pltpu.VMEM((2, width, width), narrow),
                pltpu.VMEM((8, 2, slot_count // 2, 64, 128), narrow),
                pltpu.SemaphoreType.DMA((16,)),
            ],
            compiler_params=pltpu.CompilerParams(vmem_limit_bytes=vmem_bytes),
            name=name,
            cost_estimate=work,
        )(kernel_info, clip, *operands)

    def inner_gradients(clip):
        kernel = functools.partial(inner_gradient_kernel, (places_of(0), places_of(1)))
        extra = [
            pltpu.VMEM((2, local, seq, width), narrow),
            pltpu.VMEM((8, local, seq, width), narrow),
        ]
        operands = [normed_c, d_hidden, d_top, active]
        return gradient_call(
            kernel, clip, operands, out_shapes[:2], 10, extra, "inner_gradients", cost(9e9, 14e6)
        )

    def attention_gradients(clip):
        kernel = functools.partial(
            attention_gradient_kernel, shards, chunks, (places_of(2), places_of(3))
        )
        extra = [
            pltpu.VMEM((10, local, seq, width), narrow),
            pltpu.VMEM((chunks * shards, per_chunk, memory_rows, width), narrow),
            pltpu.VMEM((2 * chunks, per_chunk, memory_len, width), narrow),
            pltpu.VMEM((chunks, per_chunk * memory_len, width), narrow),
        ]
        operands = [normed_a, d_qkv, d_early, mix_a, normed_b, d_query_b, d_mid, mix_b]
        operands += [block for blocks in memory_parts for block in blocks] + [d_pair]
        return gradient_call(
            kernel,
            clip,
            operands,
            out_shapes[2:],
            10 + chunks * (shards + 2),
            extra,
            "attention_gradients",
            cost(14e9, 30e6),
        )

    tokens_arrived = [swap(block, "tensor", index + 1) for index, block in enumerate(tokens_sent)]

    def by_place(shape, index, chunk=None):
        def spot(place, step, info):
            if chunk is not None:
                return (0, 0, 0)
            return (jnp.where(place == index, step, jnp.where(place < index, 0, chunks - 1)), 0, 0)

        return pl.BlockSpec((per_chunk,) + shape, spot)

    def to_place(shape):
        return pl.BlockSpec(
            (per_chunk,) + shape,
            lambda place, step, info: ((info[2] ^ (place + 1)) * chunks + step, 0, 0),
        )

    small_rows, large_rows = (seq_rows, width), (memory_rows, width)
    operands = [block for blocks in arrived for block in blocks] + tokens_arrived
    assemble = pl.pallas_call(
        functools.partial(assemble_kernel, shards, chunks),
        grid_spec=pltpu.PrefetchScalarGridSpec(
            num_scalar_prefetch=1,
            grid=(shards - 1, chunks),
            in_specs=[
                by_place((part_rows, width), index, chunk)
                for chunk in range(chunks)
                for index in range(shards - 1)
            ]
            + [by_place(small_rows, index) for index in range(shards - 1)]
            + [anywhere] * 3,
            out_specs=[to_place(small_rows), to_place(small_rows), to_place(large_rows)],
        ),
        out_shape=[
            jax.ShapeDtypeStruct((group_count,) + small_rows, narrow),
            jax.ShapeDtypeStruct((group_count,) + small_rows, wide),
            jax.ShapeDtypeStruct((group_count,) + large_rows, wide),
        ],
        input_output_aliases={len(operands) + 1 + index: index for index in range(3)},
        compiler_params=pltpu.CompilerParams(
            vmem_limit_bytes=vmem_bytes, dimension_semantics=("arbitrary", "arbitrary")
        ),
        name="assemble",
        cost_estimate=cost(1e6, 20e6),
    )
    returned = operands + [own_output, own_tokens, own_memory]

    pairs = [None] * 4

    def travel(index, stage):
        kept, sent = pairs[index]
        pairs[index] = add_stage(kept, swap(sent, *reduce_orders[index][stage]))

    last_stage = len(reduce_orders[0]) - 1
    done = [0] * 4

    def travel(*indices):
        for index in indices:
            if staged and done[index] <= last_stage:
                kept, sent = pairs[index]
                order = reduce_orders[index][done[index]]
                pairs[index] = add_stage(kept, swap(sent, *order))
                done[index] += 1

    def there(*indices):
        return [block for index in indices for block in pairs[index] if block is not None]

    found = inner_gradients(clip_weights)
    pairs[:2] = [tuple(found[:2]), tuple(found[2:])]
    found = attention_gradients(after(clip_weights, *there(0, 1), *tokens_arrived))
    pairs[2:] = [tuple(found[:2]), tuple(found[2:])]
    travel(0, 1)
    travel(2, 3)
    travel(0, 1, 2, 3)
    output, tokens_grad, memory_grad = assemble(after(kernel_info, *there(0)), *returned)

    def together(*extra):
        held = lax.optimization_barrier((pairs, extra))
        pairs[:] = held[0]
        return held[1]

    shrink = 1.0 / math.sqrt(group_count * replicas)
    if staged:
        small = small + swap(small, *core)
        small = after(small, *there(2, 3))
        small = small + swap(small, *side)
        small, output = together(small, output)
        small = small + swap(small, *row)
        travel(0, 1, 2, 3)
        (small,) = together(small)
        small = small + swap(small, *near)
        travel(0, 1, 2, 3)
        (small,) = together(small)
        small = small + swap(small, *far)
        last = [swap(sent, *order[-1]) for (kept, sent), order in zip(pairs, reduce_orders)]
        last = [block[0] for pair, came in zip(pairs, last) for block in (pair[0], came)]
    else:
        reduced = []
        for kept, sent in pairs:
            whole = jnp.concatenate([kept, sent], 0)
            count = whole.shape[1]
            whole = whole.reshape(dp_slots, tensor_slots, count, 64, 128).transpose(2, 0, 3, 1, 4)
            whole = whole.reshape(count, width, width)
            whole = lax.psum_scatter(whole, "dp", scatter_dimension=1, tiled=True)
            reduced.append(lax.psum_scatter(whole, "tensor", scatter_dimension=2, tiled=True))
        small = lax.psum(small, ("dp", "tensor"))
    small = small.reshape(-1)
    gain_total = small[: 3 * width].reshape(3, width)
    bias_total = small[3 * width :].reshape(heads, bucket_count).T

    large = [
        (weights_in, momentum_in, average_in, matrix_rate),
        (weights_out, momentum_out, average_out, output_rate),
        (weights_up, momentum_up, average_up, matrix_rate),
        (weights_down, momentum_down, average_down, matrix_rate),
    ]
    if staged:
        turns = ((0, 1, 2), (0, 2, 1), (0, 1), (1, 0))
        turned = [
            block.transpose(turn) for group, turn in zip(large, turns) for block in group[:3]
        ]
        operands = last + turned
        stepped = pl.pallas_call(
            functools.partial(update_kernel, shrink),
            out_shape=[
                jax.ShapeDtypeStruct(block.shape, wide) for block in turned
            ],
            compiler_params=pltpu.CompilerParams(vmem_limit_bytes=vmem_bytes),
            name="update",
            cost_estimate=cost(1e6, 4e6),
        )(*operands)
        stepped = [block.transpose(turns[index // 3]) for index, block in enumerate(stepped)]
    else:
        reduced = [block.astype(wide) * shrink for block in reduced]

        def merge(blocks):
            count, high, across = blocks.shape
            return blocks.transpose(1, 0, 2).reshape(high, count * across)

        inside = jnp.concatenate([reduced[2], reduced[3][1:2], reduced[3][3:]], 0)
        outward = jnp.stack([reduced[3][0].T, reduced[3][2].T], 0)
        down = jnp.concatenate([reduced[0][4:], reduced[1]], 0)
        gradients = [inside, outward, merge(reduced[0][:4]), merge(down).T]
        stepped = []
        for (weight, momentum, average, rate), gradient in zip(large, gradients):
            stepped += stepper(weight, gradient, momentum, average, rate)
    (
        velocity_in,
        averaged_in,
        updated_in,
        velocity_out,
        averaged_out,
        updated_out,
        velocity_up,
        averaged_up,
        updated_up,
        velocity_down,
        averaged_down,
        updated_down,
    ) = stepped

    gain_start = me_tensor * gain_width
    gain_shard = lax.dynamic_slice_in_dim(gains, gain_start, gain_width, 1)
    gain_grad = lax.dynamic_slice_in_dim(gain_total, gain_start, gain_width, 1) * shrink
    bias_grad = (
        lax.dynamic_slice_in_dim(bias_total, me_tensor * heads_local, heads_local, 1) * shrink
    )
    velocity_gain, averaged_gain, updated_gain = stepper(
        gain_shard, gain_grad, momentum_gain, average_gain, small_rate
    )
    velocity_bias, averaged_bias, updated_bias = stepper(
        position_bias, bias_grad, momentum_bias, average_bias, small_rate
    )
    return (
        output,
        tokens_grad,
        memory_grad,
        example_norms,
        velocity_in,
        averaged_in,
        updated_in,
        velocity_out,
        averaged_out,
        updated_out,
        velocity_up,
        averaged_up,
        updated_up,
        velocity_down,
        averaged_down,
        updated_down,
        velocity_gain,
        averaged_gain,
        updated_gain,
        velocity_bias,
        averaged_bias,
        updated_bias,
    )


def solution(mesh):
    return jax.shard_map(
        on_device,
        mesh=mesh,
        in_specs=(
            P("dp", "tensor", None),
            P("dp", "tensor", None),
            P("dp", "tensor", None),
            P("dp", None, None),
            P("dp", None, None),
            P("dp"),
            P(None, "dp", "tensor"),
            P(None, "tensor", "dp"),
            P("dp", "tensor"),
            P("tensor", "dp"),
            P(),
            P(None, "tensor"),
            P(None, "dp", "tensor"),
            P(None, "dp", "tensor"),
            P(None, "tensor", "dp"),
            P(None, "tensor", "dp"),
            P("dp", "tensor"),
            P("dp", "tensor"),
            P("tensor", "dp"),
            P("tensor", "dp"),
            P(None, "tensor"),
            P(None, "tensor"),
            P(None, "tensor"),
            P(None, "tensor"),
        ),
        out_specs=(
            P("dp", "tensor", None),
            P("dp", "tensor", None),
            P("dp", "tensor", None),
            P("dp"),
            P(None, "dp", "tensor"),
            P(None, "dp", "tensor"),
            P(None, "dp", "tensor"),
            P(None, "tensor", "dp"),
            P(None, "tensor", "dp"),
            P(None, "tensor", "dp"),
            P("dp", "tensor"),
            P("dp", "tensor"),
            P("dp", "tensor"),
            P("tensor", "dp"),
            P("tensor", "dp"),
            P("tensor", "dp"),
            P(None, "tensor"),
            P(None, "tensor"),
            P(None, "tensor"),
            P(None, "tensor"),
            P(None, "tensor"),
            P(None, "tensor"),
        ),
        check_vma=False,
    )
```

```python
import functools
import math

import jax
import jax.numpy as jnp
from jax import lax
from jax.experimental import pallas as pl
from jax.experimental.pallas import tpu as pltpu
from jax.sharding import PartitionSpec as P

epsilon = 1e-06
momentum_decay = 0.9
average_decay = 0.7
matrix_rate = 10.0
output_rate = 40.0
small_rate = 50.0
group_limits = (0.6, 0.85, 1.2, 1.7)
head_dim = 64
quad = 4
quad_width = quad * head_dim
dp_slots = 8
tensor_slots = 4
wide = jnp.float32
narrow = jnp.bfloat16
vmem_bytes = 58 * 2**20
cost_scale = 1.0

core = ("tensor", 1)
row = ("tensor", 2)
side = ("dp", 1)
near = ("dp", 2)
far = ("dp", 4)
gather_order = (far, near, row, side, core)
reduce_orders = (
    (core, side, near, row, far),
    (core, row, near, side, far),
    (core, row, near, far, side),
    (core, side, row, near, far),
)


def dot_nn(left, right):
    return lax.dot_general(left, right, (((1,), (0,)), ((), ())), preferred_element_type=wide)


def dot_nt(left, right):
    return lax.dot_general(left, right, (((1,), (1,)), ((), ())), preferred_element_type=wide)


def dot_tn(left, right):
    return lax.dot_general(left, right, (((0,), (0,)), ((), ())), preferred_element_type=wide)


def head_masks(dtype):
    lanes = lax.broadcasted_iota(jnp.int32, (1, quad_width), 1) // head_dim
    return [(lanes == head).astype(wide).astype(dtype) for head in range(quad)]


def stack_heads(block, masks):
    return jnp.concatenate([block * mask for mask in masks], 0)


def unstack_heads(block, masks):
    rows = block.shape[0] // quad
    total = block[:rows] * masks[0]
    for head in range(1, quad):
        total = total + block[head * rows : (head + 1) * rows] * masks[head]
    return total


def norm_scale(rows):
    return lax.rsqrt(jnp.mean(rows * rows, -1, keepdims=True) + epsilon)


def norm_back(rows, gain, d_normed):
    scaling = norm_scale(rows)
    weighted = d_normed * gain
    cubed = scaling * scaling * scaling
    d_rows = scaling * weighted - rows * cubed * jnp.mean(rows * weighted, -1, keepdims=True)
    return d_rows, d_normed * rows * scaling


def softmax_keys(scores):
    peak = jnp.max(scores, 0, keepdims=True)
    weights = jnp.exp(scores - peak)
    return weights * (1.0 / jnp.sum(weights, 0, keepdims=True))


def gram_squares(left, right_grams):
    return jnp.sum(dot_nt(left, left) * right_grams, 0, keepdims=True)


def fold_causal(block):
    size = block.shape[0]
    lanes = lax.broadcasted_iota(jnp.int32, (8, size), 1)
    rows = [block[:8], block[size // 2 : size // 2 + 8]]
    for start in range(8, size // 2, 8):
        other = pltpu.roll(block[size - start : size - start + 8], start, 1)
        rows.append(jnp.where(lanes >= start, block[start : start + 8], other))
    return jnp.concatenate(rows, 0)


def fold_lanes(row_sums):
    width = row_sums.shape[1]
    total = row_sums[:, :128]
    for start in range(128, width, 128):
        total = total + row_sums[:, start : start + 128]
    return total


def slot_places(order, first_is_high):
    places = []
    count = len(order)
    for slot in range(1 << count):
        index = {"dp": 0, "tensor": 0}
        for stage, (axis, bit) in enumerate(order):
            place = count - 1 - stage if first_is_high else stage
            if (slot >> place) & 1:
                index[axis] |= bit
        places.append((index["dp"], index["tensor"]))
    return places


def start_weights(info, pieces, plans, held, sems):
    for piece, (first, count, places, relative), sem in zip(pieces, plans, sems):
        for slot, (dp_index, tensor_index) in enumerate(places):
            if relative:
                high = pl.multiple_of((dp_index ^ info[0]) * 64, 64)
                left = pl.multiple_of((tensor_index ^ info[1]) * 128, 128)
            else:
                high, left = dp_index * 64, tensor_index * 128
            pltpu.make_async_copy(
                piece.at[slot],
                held.at[pl.ds(first, count), pl.ds(high, 64), pl.ds(left, 128)],
                sem,
            ).start()


def wait_weights(plans, held, sems):
    for (first, count, places, relative), sem in zip(plans, sems):
        share = 512 * len(places) // (dp_slots * tensor_slots)
        whole = held.at[pl.ds(first, count), pl.ds(0, share)]
        pltpu.make_async_copy(whole, whole, sem).wait()


def place_rows(info, parts, held, first=0):
    rows = held.shape[1] // len(parts)
    for index, part in enumerate(parts):
        start = pl.multiple_of((info[2] ^ index) * rows, rows)
        held[:, pl.ds(start, rows), :] = part[:, first : first + rows, :]


def split_rows(info, held, parts, first=0):
    rows = held.shape[1] // len(parts)
    for index, part in enumerate(parts):
        start = pl.multiple_of((info[2] ^ index) * rows, rows)
        part[:, first : first + rows, :] = held[:, pl.ds(start, rows), :].astype(part.dtype)


def self_forward_kernel(shards, plans, heads_local, *refs):
    refs = list(refs)

    def take(count):
        taken = refs[:count]
        del refs[:count]
        return taken

    (info,) = take(1)
    parts = take(shards)
    buckets, key_mask, gains, table = take(4)
    pieces = take(len(plans))
    normed_out, rows_out, qkv_out, weights_out, mix_out, mid_out = take(6)
    held, sems, rows_held, mix_held = take(4)
    sem_list = [sems.at[index] for index in range(len(plans))]

    @pl.when(pl.program_id(0) == 0)
    def _():
        start_weights(info, pieces, plans, held, sem_list)
        wait_weights(plans, held, sem_list)

    masks = head_masks(narrow)
    masks_wide = head_masks(wide)
    place_rows(info, parts, rows_held)
    rows_out[...] = rows_held[...]
    bundle, seq, width = rows_held.shape
    flat = rows_held[...].reshape(bundle * seq, width).astype(wide)
    normed = (flat * norm_scale(flat) * gains[0:1, :]).astype(narrow)
    normed_out[...] = normed.reshape(bundle, seq, width)
    for index in range(3):
        value = dot_nn(normed, held[index]).astype(narrow)
        qkv_out[index] = value.reshape(bundle, seq, width)
    for example in range(bundle):
        code = jnp.where(key_mask[example] > 0, buckets[example], -1).T
        safe = jnp.maximum(code, 0)
        code_all = jnp.concatenate([code] * quad, 1)
        for group in range(width // quad_width):
            columns = slice(group * quad_width, (group + 1) * quad_width)
            bias = []
            for head in range(group * quad, (group + 1) * quad):
                spot = ((head // heads_local) ^ info[2]) * heads_local + head % heads_local
                line = jnp.broadcast_to(table[pl.ds(spot, 1), :], (seq, 128))
                bias.append(jnp.take_along_axis(line, safe, axis=1))
            queries = stack_heads(qkv_out[0, example, :, columns], masks)
            scores = dot_nt(qkv_out[1, example, :, columns], queries) * (
                1.0 / math.sqrt(head_dim)
            ) + jnp.concatenate(bias, 1)
            weights = softmax_keys(jnp.where(code_all >= 0, scores, -1000000000.0))
            weights_out[example, group] = weights
            mixture = dot_tn(weights.astype(narrow), qkv_out[2, example, :, columns])
            mix_held[example, :, columns] = unstack_heads(mixture, masks_wide).astype(narrow)
    mix_out[...] = mix_held[...]
    mix = mix_held[...].reshape(bundle * seq, width)
    mid_out[...] = (flat + dot_nt(mix, held[3])).reshape(bundle, seq, width)


def cross_kernel(shards, plans, soon, aliased, *refs):
    refs = list(refs)

    def take(count):
        taken = refs[:count]
        del refs[:count]
        return taken

    (info,) = take(1)
    memory_parts = take(shards)
    mid_in, gains = take(2)
    pieces = take(len(plans))
    take(aliased)
    own_output, own_grad = take(2)
    sent_parts = take(shards - 1)
    (
        early_out,
        normed_b_out,
        d_query_out,
        d_pair_out,
        mix_out,
        d_mid_out,
        normed_c_out,
        d_hidden_out,
        active_out,
        d_top_out,
        d_gain_b_out,
        d_gain_c_out,
        squares_out,
    ) = take(13)
    d_keys_out, d_values_out = d_pair_out.at[0], d_pair_out.at[1]
    held, sems, memory_held, keys_held, values_held, weights_held, rows_held, query_held = take(8)
    sem_list = [sems.at[index] for index in range(len(plans))]

    @pl.when(pl.program_id(0) == 0)
    def _():
        start_weights(info, pieces, plans, held, sem_list)
        wait_weights(plans[:soon], held, sem_list[:soon])

    masks = head_masks(narrow)
    masks_wide = head_masks(wide)
    scaling = 1.0 / math.sqrt(head_dim)
    bundle, seq, width = mid_in.shape
    memory_len = memory_held.shape[1]
    memory_rows = memory_len // shards
    groups = width // quad_width

    def flatten(block):
        return block.reshape(block.shape[0] * block.shape[1], block.shape[2])

    def unflatten(block):
        return block.reshape(bundle, block.shape[0] // bundle, block.shape[1])

    for index, part in enumerate(memory_parts):
        memory_held[:, index * memory_rows : (index + 1) * memory_rows, :] = part[
            :, :memory_rows, :
        ]
    place_rows(info, memory_parts, d_top_out, memory_rows)
    mid = flatten(mid_in[...])
    rows_b = mid.astype(narrow).astype(wide)
    normed_b = (rows_b * norm_scale(rows_b) * gains[1:2, :]).astype(narrow)
    normed_b_out[...] = unflatten(normed_b)
    query_held[...] = unflatten(dot_nn(normed_b, held[0]).astype(narrow))
    memory_flat = flatten(memory_held[...])
    keys_held[...] = unflatten(dot_nn(memory_flat, held[1]).astype(narrow))
    values_held[...] = unflatten(dot_nn(memory_flat, held[2]).astype(narrow))
    for example in range(bundle):
        for group in range(groups):
            columns = slice(group * quad_width, (group + 1) * quad_width)
            queries = stack_heads(query_held[example, :, columns], masks)
            scores = dot_nt(keys_held[example, :, columns], queries) * scaling
            weights = softmax_keys(scores)
            weights_held[example, group] = weights
            mixture = dot_tn(weights.astype(narrow), values_held[example, :, columns])
            mix_out[example, :, columns] = unstack_heads(mixture, masks_wide).astype(narrow)
    late = mid + dot_nt(flatten(mix_out[...]), held[3])

    @pl.when(pl.program_id(0) == 0)
    def _():
        wait_weights(plans[soon:], held, sem_list[soon:])

    rows_c = late.astype(narrow).astype(wide)
    normed_c = (rows_c * norm_scale(rows_c) * gains[2:3, :]).astype(narrow)
    normed_c_out[...] = unflatten(normed_c)
    d_top = flatten(d_top_out[...])
    total = late
    d_normed = jnp.zeros((bundle * seq, width), wide)
    up_grams = [jnp.zeros((seq, seq), wide) for _ in range(bundle)]
    down_grams = [jnp.zeros((seq, seq), wide) for _ in range(bundle)]
    slope = math.sqrt(2.0 / math.pi)
    for index in range(4):
        hidden = dot_nn(normed_c, held[4 + index])
        square = hidden * hidden
        bend = jnp.tanh(slope * hidden * (1.0 + 0.044715 * square))
        half = 0.5 * (1.0 + bend)
        active = (hidden * half).astype(narrow)
        steep = half + 0.5 * hidden * (1.0 - bend * bend) * (
            slope * (1.0 + (3.0 * 0.044715) * square)
        )
        total = total + dot_nt(active, held[8 + index])
        d_hidden = (dot_nn(d_top, held[8 + index]) * steep).astype(narrow)
        d_normed = d_normed + dot_nt(d_hidden, held[4 + index])
        active_out[index] = unflatten(active)
        d_hidden_out[index] = unflatten(d_hidden)
        for example in range(bundle):
            span = slice(example * seq, (example + 1) * seq)
            up_grams[example] += dot_nt(d_hidden[span], d_hidden[span])
            down_grams[example] += dot_nt(active[span], active[span])
    rows_held[...] = unflatten(total)
    for index in range(shards):
        start = pl.multiple_of((info[2] ^ index) * (seq // shards), seq // shards)
        block = rows_held[:, pl.ds(start, seq // shards), :].astype(narrow)
        if index:
            sent_parts[index - 1][:, memory_rows:, :] = block
        else:
            own_output[...] = block
    d_rows, d_gain_rows = norm_back(rows_c, gains[2:3, :], d_normed)
    d_gain_c = jnp.sum(unflatten(d_gain_rows), 1, keepdims=True)
    d_gain_c_out[...] = d_gain_c
    d_mid = d_top.astype(wide) + d_rows
    d_mid_low = d_mid.astype(narrow)
    d_mid_out[...] = unflatten(d_mid_low)
    d_mix = dot_nn(d_mid_low, held[3]).astype(narrow)
    squares = []
    for example in range(bundle):
        span = slice(example * seq, (example + 1) * seq)
        for group in range(groups):
            columns = slice(group * quad_width, (group + 1) * quad_width)
            keys = keys_held[example, :, columns]
            queries = stack_heads(query_held[example, :, columns], masks)
            d_mixes = stack_heads(d_mix[span, columns], masks)
            weights = weights_held[example, group]
            d_weights = dot_nt(values_held[example, :, columns], d_mixes)
            inner = jnp.sum(weights * d_weights, 0, keepdims=True)
            d_scores = (weights * (d_weights - inner)).astype(narrow)
            d_query_out[example, :, columns] = (
                unstack_heads(dot_tn(d_scores, keys), masks_wide) * scaling
            ).astype(narrow)
            d_keys_out[example, :, columns] = (dot_nn(d_scores, queries) * scaling).astype(narrow)
            d_values_out[example, :, columns] = dot_nn(weights.astype(narrow), d_mixes).astype(
                narrow
            )
        memory_grad = dot_nt(d_keys_out[example], held[1]) + dot_nt(d_values_out[example], held[2])
        own_grad[example] = memory_grad[:memory_rows]
        for index, part in enumerate(sent_parts):
            part[example, :memory_rows, :] = memory_grad[
                (index + 1) * memory_rows : (index + 2) * memory_rows
            ].astype(narrow)
        d_query = d_query_out[example]
        mix = mix_out[example]
        square_sum = gram_squares(normed_b[span], dot_nt(d_query, d_query))
        square_sum += gram_squares(mix, dot_nt(d_mid_low[span], d_mid_low[span]))
        square_sum += gram_squares(normed_c[span], up_grams[example])
        square_sum += gram_squares(d_top[span], down_grams[example])
        for block in (d_keys_out, d_values_out):
            product = dot_tn(memory_held[example], block[example])
            square_sum += fold_lanes(jnp.sum(product * product, 0, keepdims=True))
        square_sum += fold_lanes(d_gain_c[example] * d_gain_c[example])
        squares.append(square_sum)
    d_normed_b = dot_nt(flatten(d_query_out[...]), held[0])
    d_rows_b, d_gain_rows = norm_back(rows_b, gains[1:2, :], d_normed_b)
    d_gain_b = jnp.sum(unflatten(d_gain_rows), 1, keepdims=True)
    d_gain_b_out[...] = d_gain_b
    for example in range(bundle):
        squares_out[example] = squares[example] + fold_lanes(
            d_gain_b[example] * d_gain_b[example]
        )
    early_out[...] = unflatten(d_mid + d_rows_b)


def self_backward_kernel(shards, plans, *refs):
    refs = list(refs)

    def take(count):
        taken = refs[:count]
        del refs[:count]
        return taken

    info, early_in, rows_in, normed_in, qkv_in, weights_in, mix_in = take(7)
    squares_in, d_gain_b, d_gain_c, buckets, gains = take(5)
    pieces = take(len(plans))
    tokens_grads = take(shards)
    d_qkv_out, d_early_out, small_out, norms_out = take(4)
    held, sems, rows_held, bias_held, folded_held = take(5)
    sem_list = [sems.at[index] for index in range(len(plans))]

    @pl.when(pl.program_id(0) == 0)
    def _():
        start_weights(info, pieces, plans, held, sem_list)
        wait_weights(plans, held, sem_list)

    masks = head_masks(narrow)
    masks_wide = head_masks(wide)
    scaling = 1.0 / math.sqrt(head_dim)
    bundle, seq, width = early_in.shape
    groups = width // quad_width
    bucket_count = bias_held.shape[0] // (groups * quad)

    def flatten(block):
        return block.reshape(block.shape[0] * block.shape[1], block.shape[2])

    def unflatten(block):
        return block.reshape(bundle, block.shape[0] // bundle, block.shape[1])

    early = flatten(early_in[...])
    d_early = early.astype(narrow)
    d_early_out[...] = unflatten(d_early)
    d_mix = dot_nn(d_early, held[3]).astype(narrow)
    squares = []
    for example in range(bundle):
        span = slice(example * seq, (example + 1) * seq)
        code = buckets[example].T
        for group in range(groups):
            columns = slice(group * quad_width, (group + 1) * quad_width)
            keys = qkv_in[1, example, :, columns]
            queries = stack_heads(qkv_in[0, example, :, columns], masks)
            d_mixes = stack_heads(d_mix[span, columns], masks)
            weights = weights_in[example, group]
            d_weights = dot_nt(qkv_in[2, example, :, columns], d_mixes)
            inner = jnp.sum(weights * d_weights, 0, keepdims=True)
            d_scores = (weights * (d_weights - inner)).astype(narrow)
            d_qkv_out[0, example, :, columns] = (
                unstack_heads(dot_tn(d_scores, keys), masks_wide) * scaling
            ).astype(narrow)
            d_qkv_out[1, example, :, columns] = (dot_nn(d_scores, queries) * scaling).astype(
                narrow
            )
            d_qkv_out[2, example, :, columns] = dot_nn(weights.astype(narrow), d_mixes).astype(
                narrow
            )
            d_wide = d_scores.astype(wide)
            for head in range(quad):
                folded_held[group * quad + head] = fold_causal(
                    d_wide[:, head * seq : (head + 1) * seq]
                )
        code = fold_causal(code)
        for bucket in range(bucket_count):
            chosen = code == bucket
            for head in range(groups * quad):
                picked = jnp.where(chosen, folded_held[head], 0.0)
                spot = head * bucket_count + bucket
                bias_held[spot : spot + 1, :] = jnp.sum(picked, 0, keepdims=True)
        d_bias = lax.dot_general(
            jnp.ones((8, 128), wide),
            bias_held[...],
            (((1,), (1,)), ((), ())),
            precision=lax.Precision.HIGHEST,
            preferred_element_type=wide,
        )[:1]
        small_out[example, :, 3 * width :] = d_bias
        grams = jnp.zeros((seq, seq), wide)
        for index in range(3):
            block = d_qkv_out[index, example]
            grams = grams + dot_nt(block, block)
        square_sum = gram_squares(normed_in[example], grams)
        square_sum += gram_squares(mix_in[example], dot_nt(d_early[span], d_early[span]))
        square_sum += fold_lanes(d_bias * d_bias)
        squares.append(square_sum)
    d_normed = dot_nt(flatten(d_qkv_out[0]), held[0])
    d_normed = d_normed + dot_nt(flatten(d_qkv_out[1]), held[1])
    d_normed = d_normed + dot_nt(flatten(d_qkv_out[2]), held[2])
    d_rows, d_gain_rows = norm_back(flatten(rows_in[...]).astype(wide), gains[0:1, :], d_normed)
    d_gain = jnp.sum(unflatten(d_gain_rows), 1, keepdims=True)
    small_out[:, :, :width] = d_gain
    small_out[:, :, width : 2 * width] = d_gain_b[...]
    small_out[:, :, 2 * width : 3 * width] = d_gain_c[...]
    for example in range(bundle):
        square_sum = (
            squares[example]
            + squares_in[example]
            + fold_lanes(d_gain[example] * d_gain[example])
        )
        total = jnp.sum(square_sum, -1, keepdims=True) + epsilon
        norms_out[example] = jnp.broadcast_to(jnp.sqrt(total), (1, 128))
    rows_held[...] = unflatten(early + d_rows)
    split_rows(info, rows_held, tokens_grads)


class Gradients:
    def __init__(self, info, clip, loads, load_sems, scaled, tile, held, store_sems):
        self.info, self.clip, self.scaled = info, clip, scaled
        self.tile, self.held, self.store_sems = tile, held, store_sems
        self.copies = [
            pltpu.make_async_copy(source, target, load_sems.at[index])
            for index, (source, target) in enumerate(loads)
        ]
        self.targets = [target for source, target in loads]
        self.stores = []
        for copy in self.copies:
            copy.start()

    def read(self, index):
        self.copies[index].wait()
        return self.targets[index]

    def scale(self, index):
        block = self.read(index)
        count, rows, width = block.shape
        for example in range(count):
            self.scaled[example * rows : (example + 1) * rows, :] = (
                block[example].astype(wide) * self.clip[example]
            ).astype(narrow)

    def product(self, index):
        block = self.read(index)
        return dot_tn(self.scaled[...], block[...].reshape(self.scaled.shape[0], block.shape[-1]))

    def write(self, value, outs, unit, places):
        number = len(self.stores) // 2
        tile = self.tile.at[number % 2]
        tile[...] = value.astype(narrow)
        halves = self.held.at[number]
        count = len(places) // 2
        for slot, (dp_index, tensor_index) in enumerate(places):
            high = pl.multiple_of((dp_index ^ self.info[0]) * 64, 64)
            left = pl.multiple_of((tensor_index ^ self.info[1]) * 128, 128)
            halves[slot // count, slot % count] = tile[pl.ds(high, 64), pl.ds(left, 128)]
        for half, out in enumerate(outs):
            copy = pltpu.make_async_copy(
                halves.at[half], out.at[:, unit], self.store_sems.at[len(self.stores)]
            )
            copy.start()
            self.stores.append(copy)

    def finish(self):
        for copy in self.stores:
            copy.wait()


class Carry:
    def __init__(self, info, count, first, parts, cuts, outs, low, sems):
        self.low, self.sems, self.cuts, self.outs = low, sems, cuts, outs
        self.spots = [
            (info[2] ^ (index + 1)) * count + first for index in range(len(parts))
        ]
        self.loads = [
            pltpu.make_async_copy(part, low.at[index], sems.at[index])
            for index, part in enumerate(parts)
        ]
        for load in self.loads:
            load.start()

    def pass_on(self, helds):
        stores = []
        size = self.low.shape[1]
        for index, (load, spot) in enumerate(zip(self.loads, self.spots)):
            load.wait()
            for (start, stop), out, held in zip(self.cuts, self.outs, helds):
                held[index] = self.low[index, :, start:stop, :].astype(held.dtype)
                sem = self.sems.at[len(self.loads) + len(stores)]
                store = pltpu.make_async_copy(held.at[index], out.at[pl.ds(spot, size)], sem)
                store.start()
                stores.append(store)
        return stores


def inner_gradient_kernel(places, shards, local, first, info, clip, left, right, *refs):
    parts, refs = refs[: shards - 1], refs[shards + 1 :]
    outs, carried = refs[:2], refs[2:4]
    rows_held, low_held, output_held, grad_held, carry_sems = refs[4:9]
    load_sems, scaled, tile, held, store_sems = refs[9:]
    loads = [(left, rows_held.at[0])]
    loads += [(right.at[unit], rows_held.at[1 + unit]) for unit in range(4)]
    work = Gradients(info, clip, loads, load_sems, scaled, tile, held, store_sems)
    rows = grad_held.shape[2]
    cuts = ((rows, low_held.shape[2]), (0, rows))
    carry = Carry(info, local, first, parts, cuts, carried, low_held, carry_sems)
    work.scale(0)
    for unit in range(4):
        work.write(work.product(1 + unit), outs, unit, places)
    stores = carry.pass_on((output_held, grad_held))
    work.finish()
    for store in stores:
        store.wait()


def self_gradient_kernel(places, shards, local, info, clip, normed, d_qkv, d_early, mix, *refs):
    parts, refs = refs[: shards - 1], refs[shards:]
    outs, carried = refs[:2], refs[2:3]
    rows_held, low_held, grad_held, carry_sems = refs[3:7]
    load_sems, scaled, tile, held, store_sems = refs[7:]
    sources = [normed, d_qkv.at[0], d_qkv.at[1], d_qkv.at[2], d_early, mix]
    loads = [(source, rows_held.at[index]) for index, source in enumerate(sources)]
    work = Gradients(info, clip, loads, load_sems, scaled, tile, held, store_sems)
    cuts = ((0, low_held.shape[2]),)
    carry = Carry(info, local, 0, parts, cuts, carried, low_held, carry_sems)
    work.scale(0)
    for unit in range(3):
        work.write(work.product(1 + unit), outs, unit, places)
    work.scale(4)
    work.write(work.product(5), outs, 3, places)
    stores = carry.pass_on((grad_held,))
    work.finish()
    for store in stores:
        store.wait()


def cross_gradient_kernel(shards, chunks, places, info, clip, *refs):
    normed, d_query, d_mid, mix = refs[:4]
    parts = refs[4 : 4 + shards * chunks]
    refs = refs[4 + shards * chunks :]
    d_pair = refs[0]
    outs = refs[1:3]
    rows_held, parts_held, pairs_held, memory_held = refs[3:7]
    load_sems, scaled, tile, held, store_sems = refs[7:]
    count, memory_len = d_pair.shape[1:3]
    part_len = memory_len // shards
    group = count // chunks
    sources = [normed, d_query, d_mid, mix]
    loads = [(source, rows_held.at[index]) for index, source in enumerate(sources)]
    first = len(loads)
    for chunk in range(chunks):
        for index in range(shards):
            place = chunk * shards + index
            loads.append((parts[place].at[:, pl.ds(0, part_len)], parts_held.at[place]))
        for unit in range(2):
            loads.append(
                (d_pair.at[unit, pl.ds(chunk * group, group)], pairs_held.at[2 * chunk + unit])
            )
    work = Gradients(info, clip, loads, load_sems, scaled, tile, held, store_sems)
    work.scale(0)
    work.write(work.product(1), outs, 0, places)
    work.scale(2)
    work.write(work.product(3), outs, 1, places)
    totals = [None, None]
    for chunk in range(chunks):
        start = first + chunk * (shards + 2)
        for index in range(shards):
            block = work.read(start + index)
            for example in range(group):
                top = (example * shards + index) * part_len
                memory_held[chunk, top : top + part_len, :] = (
                    block[example].astype(wide) * clip[chunk * group + example]
                ).astype(narrow)
        for unit in range(2):
            pair = work.read(start + shards + unit)
            product = dot_tn(
                memory_held[chunk], pair[...].reshape(group * memory_len, pair.shape[-1])
            )
            totals[unit] = product if chunk == 0 else totals[unit] + product
    for unit in range(2):
        work.write(totals[unit], outs, 2 + unit, places)
    work.finish()


def stepper(parameter, gradient, momentum, average, step_rate):
    velocity = momentum_decay * momentum + gradient
    updated = parameter - step_rate * (gradient + momentum_decay * velocity)
    averaged = average_decay * average + (1.0 - average_decay) * updated
    return (velocity, averaged, updated)


def update_kernel(shrink, *refs):
    sums = refs[:8]
    params, outs = refs[8:20], refs[20:]

    def gradient(piece, unit):
        total = sums[2 * piece][unit].astype(wide) + sums[2 * piece + 1][unit].astype(wide)
        return total * shrink

    def step(group, spot, value, rate):
        weight, momentum, average = params[3 * group : 3 * group + 3]
        stepped = stepper(weight[spot], value, momentum[spot], average[spot], rate)
        for out, block in zip(outs[3 * group : 3 * group + 3], stepped):
            out[spot] = block

    inside = ((2, 0), (2, 1), (2, 2), (3, 0), (3, 2), (3, 3))
    for index, (piece, unit) in enumerate(inside):
        step(0, index, gradient(piece, unit), matrix_rate)
    for index, (piece, unit) in enumerate(((2, 3), (3, 1))):
        step(1, index, gradient(piece, unit), output_rate)
    for index in range(4):
        spot = (slice(None), slice(128 * index, 128 * (index + 1)))
        step(2, spot, gradient(0, index), matrix_rate)
        step(3, spot, gradient(1, index), matrix_rate)


def swap(value, axis, bit):
    size = lax.axis_size(axis)
    return lax.ppermute(value, axis, [(index, index ^ bit) for index in range(size)])


def after(value, *earlier):
    return lax.optimization_barrier((value,) + earlier)[0]


def gather_slots(shard):
    gathered = shard[None]
    for axis, bit in gather_order[:3]:
        gathered = jnp.concatenate([gathered, swap(gathered, axis, bit)], 0)
    beside = swap(gathered, *gather_order[3])
    pieces = [gathered, beside, swap(gathered, *gather_order[4]), swap(beside, *gather_order[4])]
    places = slot_places(gather_order, False)
    count = len(places) // 4
    return [
        (piece, places[index * count : (index + 1) * count]) for index, piece in enumerate(pieces)
    ]


def add_stage(kept, arrived):
    half = kept.shape[0] // 2

    def added(start, stop):
        total = kept[start:stop].astype(wide) + arrived[start:stop].astype(wide)
        return total.astype(narrow)

    if not half:
        return added(0, 1)[0], None
    return added(0, half), added(half, 2 * half)


def on_device(
    tokens,
    memory,
    cotangent,
    buckets,
    key_mask,
    task_groups,
    weights_in,
    weights_out,
    weights_up,
    weights_down,
    gains,
    position_bias,
    momentum_in,
    average_in,
    momentum_out,
    average_out,
    momentum_up,
    average_up,
    momentum_down,
    average_down,
    momentum_gain,
    average_gain,
    momentum_bias,
    average_bias,
):
    shards = lax.axis_size("tensor")
    replicas = lax.axis_size("dp")
    me_tensor = lax.axis_index("tensor")
    me_dp = lax.axis_index("dp")
    width = tokens.shape[2]
    seq = buckets.shape[1]
    seq_rows = tokens.shape[1]
    memory_rows = memory.shape[1]
    memory_len = memory_rows * shards
    group_count = tokens.shape[0]
    local = group_count // shards
    chunks = 2
    per_chunk = local // chunks
    bundle = 2 if per_chunk % 2 == 0 else 1
    steps = per_chunk // bundle
    bucket_count, heads_local = position_bias.shape
    heads = heads_local * shards
    gain_width = momentum_gain.shape[1]
    staged = shards == tensor_slots and replicas == dp_slots

    slot_base = [me_dp, me_tensor] if staged else [0 * me_dp, 0 * me_tensor]
    kernel_info = jnp.stack(slot_base + [me_tensor]).astype(jnp.int32)

    def square_shards():
        high, across = weights_in.shape[1], weights_in.shape[2]
        split = lambda block: block.reshape(high, -1, across).transpose(1, 0, 2)
        return (
            weights_in.astype(narrow),
            weights_out.astype(narrow).transpose(0, 2, 1),
            split(weights_up.astype(narrow)),
            split(weights_down.astype(narrow).T),
        )

    shard_in, shard_out, shard_up, shard_down = square_shards()
    slot_count = dp_slots * tensor_slots
    plain_places = [(slot // tensor_slots, slot % tensor_slots) for slot in range(slot_count)]

    def gather_late(blocks):
        count = blocks.shape[0]
        if staged:
            whole = lax.all_gather(blocks, ("dp", "tensor"), axis=0)
        else:
            whole = lax.all_gather(blocks, "dp", axis=1, tiled=True)
            whole = lax.all_gather(whole, "tensor", axis=2, tiled=True)
            whole = whole.reshape(count, dp_slots, 64, tensor_slots, 128).transpose(1, 3, 0, 2, 4)
            whole = whole.reshape(slot_count, count, 64, 128)
        return [whole], [(0, count, plain_places, False)]

    def gather_soon(blocks):
        if not staged:
            return gather_late(blocks)
        pieces, plans = [], []
        for piece, places in gather_slots(blocks):
            pieces.append(piece)
            plans.append((0, blocks.shape[0], places, True))
        return pieces, plans

    def exchange(values, start, count):
        found = []
        for index in range(shards):
            first = (me_tensor ^ index) * local + start
            blocks = [lax.dynamic_slice_in_dim(value, first, count, 0) for value in values]
            block = jnp.concatenate(blocks, 1) if len(blocks) > 1 else blocks[0]
            found.append(swap(block, "tensor", index) if index else block)
        return found

    late_pieces, late_plans = gather_late(jnp.concatenate([shard_up, shard_down], 0))
    token_parts = exchange([tokens], 0, local)
    self_pieces, self_plans = gather_soon(jnp.concatenate([shard_in[:3], shard_out[:1]], 0))
    cross_pieces, cross_plans = gather_soon(jnp.concatenate([shard_in[3:6], shard_out[1:2]], 0))
    late_plans = cross_plans + [(4,) + plan[1:] for plan in late_plans]
    late_pieces = cross_pieces + late_pieces
    soon_count = len(cross_pieces)
    table = jnp.pad(position_bias.T, ((0, 0), (0, 128 - bucket_count)))
    table_all = jnp.concatenate(
        [swap(table, "tensor", index) if index else table for index in range(shards)], 0
    )
    memory_parts = []
    earlier = token_parts
    for chunk in range(chunks):
        source, _ = lax.optimization_barrier((memory, earlier[-1]))
        earlier = exchange([source, cotangent], chunk * per_chunk, per_chunk)
        memory_parts.append(earlier)
    bucket_mine = lax.dynamic_slice_in_dim(buckets, me_tensor * local, local, 0)
    mask_mine = lax.dynamic_slice_in_dim(key_mask, me_tensor * local, local, 0)
    groups_mine = lax.dynamic_slice_in_dim(task_groups, me_tensor * local, local, 0)

    smem = pl.BlockSpec(memory_space=pltpu.SMEM)
    anywhere = pl.BlockSpec(memory_space=pl.ANY)
    params = pltpu.CompilerParams(
        vmem_limit_bytes=vmem_bytes, dimension_semantics=("arbitrary",)
    )

    def part_spec(shape, offset=0, lead=None):
        zeros = (0,) * len(shape)
        if lead is None:
            return pl.BlockSpec(
                (bundle,) + tuple(shape), lambda step, *_: (step + offset,) + zeros
            )
        return pl.BlockSpec(
            (lead, bundle) + tuple(shape), lambda step, *_: (0, step + offset) + zeros
        )

    def own_spec(shape, offset=0):
        zeros = (0,) * len(shape)
        return pl.BlockSpec(
            (bundle,) + tuple(shape),
            lambda step, info: (info[2] * (local // bundle) + step + offset,) + zeros,
        )

    def whole_spec(shape):
        return pl.BlockSpec(tuple(shape), lambda step, *_: (0,) * len(shape))

    def shaped(shape, dtype, lead=None, count=local):
        front = (count,) if lead is None else (lead, count)
        return jax.ShapeDtypeStruct(front + tuple(shape), dtype)

    def cost(flops, moved):
        return pl.CostEstimate(
            flops=int(flops * cost_scale), bytes_accessed=int(moved * cost_scale), transcendentals=0
        )

    groups = width // quad_width
    row_block = (seq, width)
    part_rows = memory_rows + seq_rows

    normed_a, rows_a, qkv_a, weights_a, mix_a, mid = pl.pallas_call(
        functools.partial(self_forward_kernel, shards, self_plans, heads_local),
        grid=(local // bundle,),
        in_specs=[smem]
        + [part_spec((seq_rows, width))] * shards
        + [part_spec((seq, seq))] * 2
        + [whole_spec(gains.shape), whole_spec(table_all.shape)]
        + [anywhere] * len(self_pieces),
        out_specs=[
            part_spec(row_block),
            part_spec(row_block),
            part_spec(row_block, lead=3),
            part_spec((groups, seq, quad * seq)),
            part_spec(row_block),
            part_spec(row_block),
        ],
        out_shape=[
            shaped(row_block, narrow),
            shaped(row_block, narrow),
            shaped(row_block, narrow, 3),
            shaped((groups, seq, quad * seq), wide),
            shaped(row_block, narrow),
            shaped(row_block, wide),
        ],
        scratch_shapes=[
            pltpu.VMEM((4, width, width), narrow),
            pltpu.SemaphoreType.DMA((len(self_pieces),)),
            pltpu.VMEM((bundle,) + row_block, narrow),
            pltpu.VMEM((bundle,) + row_block, narrow),
        ],
        compiler_params=params,
        name="self_forward",
        cost_estimate=cost(local * 2e9, local * 2e6),
    )(
        kernel_info,
        *token_parts,
        bucket_mine,
        mask_mine,
        gains,
        table_all,
        *self_pieces,
    )

    def cross(chunk, filled):
        offset = chunk * steps
        gain_block = (1, width)
        kept_specs = [
            part_spec(row_block, offset),
            part_spec(row_block, offset),
            part_spec(row_block, offset),
            part_spec((memory_len, width), offset, 2),
            part_spec(row_block, offset),
            part_spec(row_block, offset),
            part_spec(row_block, offset),
            part_spec(row_block, offset, 4),
            part_spec(row_block, offset, 4),
            part_spec(row_block, offset),
            part_spec(gain_block, offset),
            part_spec(gain_block, offset),
            part_spec((1, 128), offset),
        ]
        kept_shapes = [
            shaped(row_block, wide),
            shaped(row_block, narrow),
            shaped(row_block, narrow),
            shaped((memory_len, width), narrow, 2),
            shaped(row_block, narrow),
            shaped(row_block, narrow),
            shaped(row_block, narrow),
            shaped(row_block, narrow, 4),
            shaped(row_block, narrow, 4),
            shaped(row_block, narrow),
            shaped(gain_block, wide),
            shaped(gain_block, wide),
            shaped((1, 128), wide),
        ]
        own_specs = [own_spec((seq_rows, width), offset), own_spec((memory_rows, width), offset)]
        own_shapes = [
            shaped((seq_rows, width), narrow, count=group_count),
            shaped((memory_rows, width), wide, count=group_count),
        ]
        operands = [kernel_info, *memory_parts[chunk], mid, gains, *late_pieces]
        aliases = {}
        for index, block in enumerate(filled):
            aliases[len(operands) + index] = index if index < 2 else index + shards - 1
        return pl.pallas_call(
            functools.partial(cross_kernel, shards, late_plans, soon_count, len(filled)),
            grid_spec=pltpu.PrefetchScalarGridSpec(
                num_scalar_prefetch=1,
                grid=(steps,),
                in_specs=[part_spec((part_rows, width))] * shards
                + [part_spec(row_block, offset), whole_spec(gains.shape)]
                + [anywhere] * (len(late_pieces) + len(filled)),
                out_specs=own_specs + [part_spec((part_rows, width))] * (shards - 1) + kept_specs,
                scratch_shapes=[
                    pltpu.VMEM((12, width, width), narrow),
                    pltpu.SemaphoreType.DMA((len(late_pieces),)),
                    pltpu.VMEM((bundle, memory_len, width), narrow),
                    pltpu.VMEM((bundle, memory_len, width), narrow),
                    pltpu.VMEM((bundle, memory_len, width), narrow),
                    pltpu.VMEM((bundle, groups, memory_len, quad * seq), wide),
                    pltpu.VMEM((bundle,) + row_block, wide),
                    pltpu.VMEM((bundle,) + row_block, narrow),
                ],
            ),
            out_shape=own_shapes
            + [shaped((part_rows, width), narrow, count=per_chunk)] * (shards - 1)
            + kept_shapes,
            input_output_aliases=aliases,
            compiler_params=params,
            name="cross",
            cost_estimate=cost(per_chunk * 8e9, per_chunk * 6e6),
        )(*operands, *filled)

    filled, sent = [], []
    for chunk in range(chunks):
        found = cross(chunk, filled)
        sent.append(found[2 : shards + 1])
        filled = list(found[:2]) + list(found[shards + 1 :])
    own_output, own_memory = filled[:2]
    (
        early,
        normed_b,
        d_query_b,
        d_pair,
        mix_b,
        d_mid,
        normed_c,
        d_hidden,
        active,
        d_top,
        d_gain_b,
        d_gain_c,
        squares,
    ) = filled[2:]
    arrived = [
        [swap(block, "tensor", index + 1) for index, block in enumerate(blocks)] for blocks in sent
    ]
    soon = [block for blocks in arrived[:-1] for block in blocks]

    found = pl.pallas_call(
        functools.partial(self_backward_kernel, shards, self_plans),
        grid_spec=pltpu.PrefetchScalarGridSpec(
            num_scalar_prefetch=1,
            grid=(local // bundle,),
            in_specs=[
            part_spec(row_block),
            part_spec(row_block),
            part_spec(row_block),
            part_spec(row_block, lead=3),
            part_spec((groups, seq, quad * seq)),
            part_spec(row_block),
            part_spec((1, 128)),
            part_spec((1, width)),
            part_spec((1, width)),
            part_spec((seq, seq)),
            whole_spec(gains.shape),
        ]
        + [anywhere] * len(self_pieces),
        out_specs=[own_spec((seq_rows, width))]
        + [part_spec((seq_rows, width))] * (shards - 1)
        + [
            part_spec(row_block, lead=3),
            part_spec(row_block),
            part_spec((1, 3 * width + heads * bucket_count)),
            part_spec((1, 128)),
        ],
        scratch_shapes=[
            pltpu.VMEM((4, width, width), narrow),
            pltpu.SemaphoreType.DMA((len(self_pieces),)),
            pltpu.VMEM((bundle,) + row_block, wide),
            pltpu.VMEM((heads * bucket_count, 128), wide),
            pltpu.VMEM((heads, seq // 2 + 8, seq), wide),
        ],
        ),
        out_shape=[shaped((seq_rows, width), wide, count=group_count)]
        + [shaped((seq_rows, width), narrow)] * (shards - 1)
        + [
            shaped(row_block, narrow, 3),
            shaped(row_block, narrow),
            shaped((1, 3 * width + heads * bucket_count), wide),
            shaped((1, 128), wide),
        ],
        compiler_params=params,
        name="self_backward",
        cost_estimate=cost(local * 3e9, local * 3e6),
    )(
        after(kernel_info, *soon),
        early,
        rows_a,
        normed_a,
        qkv_a,
        weights_a,
        mix_a,
        squares,
        d_gain_b,
        d_gain_c,
        bucket_mine,
        gains,
        *self_pieces,
    )
    own_tokens, tokens_sent = found[0], found[1:shards]
    d_qkv, d_early, small, norms = found[shards:]

    norms = after(norms.reshape(local, 128), *arrived[-1])
    norm_slots = norms
    bit = 1
    while bit < shards:
        norm_slots = jnp.concatenate([norm_slots, swap(norm_slots, "tensor", bit)], 0)
        bit *= 2
    total = jnp.broadcast_to(jnp.sum(norm_slots, 0, keepdims=True), (8, 128))
    bit = 1
    while bit < replicas:
        total = total + swap(total, "dp", bit)
        bit *= 2
    order = jnp.arange(shards, dtype=jnp.int32) ^ me_tensor
    example_norms = norm_slots[:, 0].reshape(shards, local)[order].reshape(group_count)
    mean_norm = total[0, 0] / (group_count * replicas)
    limits = jnp.sum(
        (groups_mine[:, None] == jnp.arange(len(group_limits), dtype=jnp.int32))
        * jnp.asarray(group_limits, wide),
        1,
    )
    clip_weights = jnp.minimum(1.0 / mean_norm, limits / norms[:, 0])
    small = jnp.sum(clip_weights[:, None, None] * small, 0).reshape(-1, 128)

    def places_of(index):
        return slot_places(reduce_orders[index], True) if staged else plain_places

    out_shape = jax.ShapeDtypeStruct((slot_count // 2, 4, 64, 128), narrow)

    def gradient_call(kernel, clip, operands, loads, extra, name, work, carried=()):
        first = 2 + len(operands)
        return tuple(
            pl.pallas_call(
                kernel,
                in_specs=[smem, smem] + [anywhere] * (len(operands) + len(carried)),
                out_specs=[anywhere] * (2 + len(carried)),
                out_shape=[out_shape] * 2
                + [jax.ShapeDtypeStruct(block.shape, block.dtype) for block in carried],
                input_output_aliases={first + index: 2 + index for index in range(len(carried))},
                scratch_shapes=extra
                + [
                    pltpu.SemaphoreType.DMA((loads,)),
                    pltpu.VMEM((local * seq, width), narrow),
                    pltpu.VMEM((2, width, width), narrow),
                    pltpu.VMEM((4, 2, slot_count // 2, 64, 128), narrow),
                    pltpu.SemaphoreType.DMA((8,)),
                ],
                compiler_params=pltpu.CompilerParams(vmem_limit_bytes=vmem_bytes),
                name=name,
                cost_estimate=work,
            )(kernel_info, clip, *operands, *carried)
        )

    def inner_gradients(index, clip, left, right, parts, carried):
        kernel = functools.partial(
            inner_gradient_kernel, places_of(index), shards, local, index * per_chunk
        )
        extra = [
            pltpu.VMEM((5, local, seq, width), narrow),
            pltpu.VMEM((shards - 1, per_chunk, part_rows, width), narrow),
            pltpu.VMEM((shards - 1, per_chunk, seq_rows, width), narrow),
            pltpu.VMEM((shards - 1, per_chunk, memory_rows, width), wide),
            pltpu.SemaphoreType.DMA((3 * (shards - 1),)),
        ]
        return gradient_call(
            kernel,
            clip,
            [left, right, *parts],
            5,
            extra,
            "inner_gradients",
            cost(5e9, 7e6),
            carried,
        )

    def self_gradients(clip, parts, carried):
        kernel = functools.partial(self_gradient_kernel, places_of(2), shards, local)
        extra = [
            pltpu.VMEM((6, local, seq, width), narrow),
            pltpu.VMEM((shards - 1, local, seq_rows, width), narrow),
            pltpu.VMEM((shards - 1, local, seq_rows, width), wide),
            pltpu.SemaphoreType.DMA((2 * (shards - 1),)),
        ]
        operands = [normed_a, d_qkv, d_early, mix_a, *parts]
        return gradient_call(
            kernel, clip, operands, 6, extra, "self_gradients", cost(5e9, 8e6), carried
        )

    def cross_gradients(clip):
        kernel = functools.partial(cross_gradient_kernel, shards, chunks, places_of(3))
        extra = [
            pltpu.VMEM((4, local, seq, width), narrow),
            pltpu.VMEM((chunks * shards, per_chunk, memory_rows, width), narrow),
            pltpu.VMEM((2 * chunks, per_chunk, memory_len, width), narrow),
            pltpu.VMEM((chunks, per_chunk * memory_len, width), narrow),
        ]
        operands = [normed_b, d_query_b, d_mid, mix_b]
        operands += [block for blocks in memory_parts for block in blocks] + [d_pair]
        loads = 4 + chunks * (shards + 2)
        return gradient_call(
            kernel, clip, operands, loads, extra, "cross_gradients", cost(9e9, 20e6)
        )

    tokens_arrived = [swap(block, "tensor", index + 1) for index, block in enumerate(tokens_sent)]
    pairs = [None] * 4

    def travel(index, stage):
        kept, sent = pairs[index]
        pairs[index] = add_stage(kept, swap(sent, *reduce_orders[index][stage]))

    last_stage = len(reduce_orders[0]) - 1
    done = [0] * 4

    def travel(*indices):
        for index in indices:
            if staged and done[index] <= last_stage:
                kept, sent = pairs[index]
                order = reduce_orders[index][done[index]]
                pairs[index] = add_stage(kept, swap(sent, *order))
                done[index] += 1

    def there(*indices):
        return [block for index in indices for block in pairs[index] if block is not None]

    clip_weights = after(clip_weights, *tokens_arrived)
    carried = (own_output, own_memory)
    found = inner_gradients(0, clip_weights, normed_c, d_hidden, arrived[0], carried)
    pairs[0] = found[:2]
    clip = after(clip_weights, *there(0))
    found = inner_gradients(1, clip, d_top, active, arrived[1], found[2:])
    pairs[1] = found[:2]
    output, memory_grad = found[2:]
    travel(0)
    clip = after(clip_weights, *there(0, 1))
    found = self_gradients(clip, tokens_arrived, (own_tokens,))
    pairs[2] = found[:2]
    tokens_grad = found[2]
    travel(1)
    clip = after(clip_weights, *there(1, 2))
    pairs[3] = cross_gradients(clip)
    travel(0, 1)
    travel(2, 3)

    def together(*extra):
        held = lax.optimization_barrier((pairs, extra))
        pairs[:] = held[0]
        return held[1]

    shrink = 1.0 / math.sqrt(group_count * replicas)
    if staged:
        small = small + swap(small, *core)
        (small,) = together(small)
        small = small + swap(small, *side)
        travel(0, 1, 2, 3)
        (small,) = together(small)
        small = small + swap(small, *row)
        travel(0, 1, 2, 3)
        (small,) = together(small)
        small = small + swap(small, *near)
        last = [None] * 4
        for index in (0, 1):
            kept, sent = pairs[index]
            last[index] = (kept[0], swap(sent, *reduce_orders[index][-1])[0])
        travel(2, 3)
        small, last = lax.optimization_barrier((small, last))
        small = small + swap(small, *far)
        for index in (2, 3):
            kept, sent = pairs[index]
            last[index] = (kept[0], swap(sent, *reduce_orders[index][-1])[0])
        last = [block for pair in last for block in pair]
    else:
        reduced = []
        for kept, sent in pairs:
            whole = jnp.concatenate([kept, sent], 0)
            count = whole.shape[1]
            whole = whole.reshape(dp_slots, tensor_slots, count, 64, 128).transpose(2, 0, 3, 1, 4)
            whole = whole.reshape(count, width, width)
            whole = lax.psum_scatter(whole, "dp", scatter_dimension=1, tiled=True)
            reduced.append(lax.psum_scatter(whole, "tensor", scatter_dimension=2, tiled=True))
        small = lax.psum(small, ("dp", "tensor"))
    small = small.reshape(-1)
    gain_total = small[: 3 * width].reshape(3, width)
    bias_total = small[3 * width :].reshape(heads, bucket_count).T

    large = [
        (weights_in, momentum_in, average_in, matrix_rate),
        (weights_out, momentum_out, average_out, output_rate),
        (weights_up, momentum_up, average_up, matrix_rate),
        (weights_down, momentum_down, average_down, matrix_rate),
    ]
    if staged:
        turns = ((0, 1, 2), (0, 2, 1), (0, 1), (1, 0))
        turned = [
            block.transpose(turn) for group, turn in zip(large, turns) for block in group[:3]
        ]
        operands = last + turned
        stepped = pl.pallas_call(
            functools.partial(update_kernel, shrink),
            out_shape=[
                jax.ShapeDtypeStruct(block.shape, wide) for block in turned
            ],
            compiler_params=pltpu.CompilerParams(vmem_limit_bytes=vmem_bytes),
            name="update",
            cost_estimate=cost(1e6, 4e6),
        )(*operands)
        stepped = [block.transpose(turns[index // 3]) for index, block in enumerate(stepped)]
    else:
        reduced = [block.astype(wide) * shrink for block in reduced]

        def merge(blocks):
            count, high, across = blocks.shape
            return blocks.transpose(1, 0, 2).reshape(high, count * across)

        inside = jnp.concatenate([reduced[2][:3], reduced[3][:1], reduced[3][2:]], 0)
        outward = jnp.stack([reduced[2][3].T, reduced[3][1].T], 0)
        gradients = [inside, outward, merge(reduced[0]), merge(reduced[1]).T]
        stepped = []
        for (weight, momentum, average, rate), gradient in zip(large, gradients):
            stepped += stepper(weight, gradient, momentum, average, rate)
    (
        velocity_in,
        averaged_in,
        updated_in,
        velocity_out,
        averaged_out,
        updated_out,
        velocity_up,
        averaged_up,
        updated_up,
        velocity_down,
        averaged_down,
        updated_down,
    ) = stepped

    gain_start = me_tensor * gain_width
    gain_shard = lax.dynamic_slice_in_dim(gains, gain_start, gain_width, 1)
    gain_grad = lax.dynamic_slice_in_dim(gain_total, gain_start, gain_width, 1) * shrink
    bias_grad = (
        lax.dynamic_slice_in_dim(bias_total, me_tensor * heads_local, heads_local, 1) * shrink
    )
    velocity_gain, averaged_gain, updated_gain = stepper(
        gain_shard, gain_grad, momentum_gain, average_gain, small_rate
    )
    velocity_bias, averaged_bias, updated_bias = stepper(
        position_bias, bias_grad, momentum_bias, average_bias, small_rate
    )
    return (
        output,
        tokens_grad,
        memory_grad,
        example_norms,
        velocity_in,
        averaged_in,
        updated_in,
        velocity_out,
        averaged_out,
        updated_out,
        velocity_up,
        averaged_up,
        updated_up,
        velocity_down,
        averaged_down,
        updated_down,
        velocity_gain,
        averaged_gain,
        updated_gain,
        velocity_bias,
        averaged_bias,
        updated_bias,
    )


def solution(mesh):
    return jax.shard_map(
        on_device,
        mesh=mesh,
        in_specs=(
            P("dp", "tensor", None),
            P("dp", "tensor", None),
            P("dp", "tensor", None),
            P("dp", None, None),
            P("dp", None, None),
            P("dp"),
            P(None, "dp", "tensor"),
            P(None, "tensor", "dp"),
            P("dp", "tensor"),
            P("tensor", "dp"),
            P(),
            P(None, "tensor"),
            P(None, "dp", "tensor"),
            P(None, "dp", "tensor"),
            P(None, "tensor", "dp"),
            P(None, "tensor", "dp"),
            P("dp", "tensor"),
            P("dp", "tensor"),
            P("tensor", "dp"),
            P("tensor", "dp"),
            P(None, "tensor"),
            P(None, "tensor"),
            P(None, "tensor"),
            P(None, "tensor"),
        ),
        out_specs=(
            P("dp", "tensor", None),
            P("dp", "tensor", None),
            P("dp", "tensor", None),
            P("dp"),
            P(None, "dp", "tensor"),
            P(None, "dp", "tensor"),
            P(None, "dp", "tensor"),
            P(None, "tensor", "dp"),
            P(None, "tensor", "dp"),
            P(None, "tensor", "dp"),
            P("dp", "tensor"),
            P("dp", "tensor"),
            P("dp", "tensor"),
            P("tensor", "dp"),
            P("tensor", "dp"),
            P("tensor", "dp"),
            P(None, "tensor"),
            P(None, "tensor"),
            P(None, "tensor"),
            P(None, "tensor"),
            P(None, "tensor"),
            P(None, "tensor"),
        ),
        check_vma=False,
    )
```

```python
import functools
import math

import jax
import jax.numpy as jnp
from jax import lax
from jax.experimental import pallas as pl
from jax.experimental.pallas import tpu as pltpu
from jax.sharding import PartitionSpec as P

epsilon = 1e-06
momentum_decay = 0.9
average_decay = 0.7
matrix_rate = 10.0
output_rate = 40.0
small_rate = 50.0
group_limits = (0.6, 0.85, 1.2, 1.7)
head_dim = 64
quad = 4
quad_width = quad * head_dim
dp_slots = 8
tensor_slots = 4
wide = jnp.float32
narrow = jnp.bfloat16
vmem_bytes = 58 * 2**20
cost_scale = 1.0

core = ("tensor", 1)
row = ("tensor", 2)
side = ("dp", 1)
near = ("dp", 2)
far = ("dp", 4)
gather_order = (far, near, row, side, core)
reduce_orders = (
    (core, side, near, row, far),
    (core, row, near, side, far),
    (core, row, near, far, side),
    (core, side, row, near, far),
)


def dot_nn(left, right):
    return lax.dot_general(left, right, (((1,), (0,)), ((), ())), preferred_element_type=wide)


def dot_nt(left, right):
    return lax.dot_general(left, right, (((1,), (1,)), ((), ())), preferred_element_type=wide)


def dot_tn(left, right):
    return lax.dot_general(left, right, (((0,), (0,)), ((), ())), preferred_element_type=wide)


def head_masks(dtype):
    lanes = lax.broadcasted_iota(jnp.int32, (1, quad_width), 1) // head_dim
    return [(lanes == head).astype(wide).astype(dtype) for head in range(quad)]


def stack_heads(block, masks):
    return jnp.concatenate([block * mask for mask in masks], 0)


def unstack_heads(block, masks):
    rows = block.shape[0] // quad
    total = block[:rows] * masks[0]
    for head in range(1, quad):
        total = total + block[head * rows : (head + 1) * rows] * masks[head]
    return total


def norm_scale(rows):
    return lax.rsqrt(jnp.mean(rows * rows, -1, keepdims=True) + epsilon)


def norm_back(rows, gain, d_normed):
    scaling = norm_scale(rows)
    weighted = d_normed * gain
    cubed = scaling * scaling * scaling
    d_rows = scaling * weighted - rows * cubed * jnp.mean(rows * weighted, -1, keepdims=True)
    return d_rows, d_normed * rows * scaling


def softmax_keys(scores):
    peak = jnp.max(scores, 0, keepdims=True)
    weights = jnp.exp(scores - peak)
    return weights * (1.0 / jnp.sum(weights, 0, keepdims=True))


def gram_squares(left, right_grams):
    return jnp.sum(dot_nt(left, left) * right_grams, 0, keepdims=True)


def fold_causal(block):
    size = block.shape[0]
    lanes = lax.broadcasted_iota(jnp.int32, (8, size), 1)
    rows = [block[:8], block[size // 2 : size // 2 + 8]]
    for start in range(8, size // 2, 8):
        other = pltpu.roll(block[size - start : size - start + 8], start, 1)
        rows.append(jnp.where(lanes >= start, block[start : start + 8], other))
    return jnp.concatenate(rows, 0)


def fold_lanes(row_sums):
    width = row_sums.shape[1]
    total = row_sums[:, :128]
    for start in range(128, width, 128):
        total = total + row_sums[:, start : start + 128]
    return total


def slot_places(order, first_is_high):
    places = []
    count = len(order)
    for slot in range(1 << count):
        index = {"dp": 0, "tensor": 0}
        for stage, (axis, bit) in enumerate(order):
            place = count - 1 - stage if first_is_high else stage
            if (slot >> place) & 1:
                index[axis] |= bit
        places.append((index["dp"], index["tensor"]))
    return places


def start_weights(info, pieces, plans, held, sems):
    for piece, (first, count, places, relative), sem in zip(pieces, plans, sems):
        for slot, (dp_index, tensor_index) in enumerate(places):
            if relative:
                high = pl.multiple_of((dp_index ^ info[0]) * 64, 64)
                left = pl.multiple_of((tensor_index ^ info[1]) * 128, 128)
            else:
                high, left = dp_index * 64, tensor_index * 128
            pltpu.make_async_copy(
                piece.at[slot],
                held.at[pl.ds(first, count), pl.ds(high, 64), pl.ds(left, 128)],
                sem,
            ).start()


def wait_weights(plans, held, sems):
    for (first, count, places, relative), sem in zip(plans, sems):
        share = 512 * len(places) // (dp_slots * tensor_slots)
        whole = held.at[pl.ds(first, count), pl.ds(0, share)]
        pltpu.make_async_copy(whole, whole, sem).wait()


def place_rows(info, parts, held, first=0):
    rows = held.shape[1] // len(parts)
    for index, part in enumerate(parts):
        start = pl.multiple_of((info[2] ^ index) * rows, rows)
        held[:, pl.ds(start, rows), :] = part[:, first : first + rows, :]


def split_rows(info, held, parts, first=0):
    rows = held.shape[1] // len(parts)
    for index, part in enumerate(parts):
        start = pl.multiple_of((info[2] ^ index) * rows, rows)
        part[:, first : first + rows, :] = held[:, pl.ds(start, rows), :].astype(part.dtype)


def self_forward_kernel(shards, plans, heads_local, *refs):
    refs = list(refs)

    def take(count):
        taken = refs[:count]
        del refs[:count]
        return taken

    (info,) = take(1)
    parts = take(shards)
    buckets, key_mask, gains, table = take(4)
    pieces = take(len(plans))
    normed_out, rows_out, qkv_out, weights_out, mix_out, mid_out = take(6)
    held, sems, rows_held, mix_held = take(4)
    sem_list = [sems.at[index] for index in range(len(plans))]

    @pl.when(pl.program_id(0) == 0)
    def _():
        start_weights(info, pieces, plans, held, sem_list)
        wait_weights(plans, held, sem_list)

    masks = head_masks(narrow)
    masks_wide = head_masks(wide)
    place_rows(info, parts, rows_held)
    rows_out[...] = rows_held[...]
    bundle, seq, width = rows_held.shape
    flat = rows_held[...].reshape(bundle * seq, width).astype(wide)
    normed = (flat * norm_scale(flat) * gains[0:1, :]).astype(narrow)
    normed_out[...] = normed.reshape(bundle, seq, width)
    for index in range(3):
        value = dot_nn(normed, held[index]).astype(narrow)
        qkv_out[index] = value.reshape(bundle, seq, width)
    for example in range(bundle):
        code = jnp.where(key_mask[example] > 0, buckets[example], -1).T
        safe = jnp.maximum(code, 0)
        code_all = jnp.concatenate([code] * quad, 1)
        for group in range(width // quad_width):
            columns = slice(group * quad_width, (group + 1) * quad_width)
            bias = []
            for head in range(group * quad, (group + 1) * quad):
                spot = ((head // heads_local) ^ info[2]) * heads_local + head % heads_local
                line = jnp.broadcast_to(table[pl.ds(spot, 1), :], (seq, 128))
                bias.append(jnp.take_along_axis(line, safe, axis=1))
            queries = stack_heads(qkv_out[0, example, :, columns], masks)
            scores = dot_nt(qkv_out[1, example, :, columns], queries) * (
                1.0 / math.sqrt(head_dim)
            ) + jnp.concatenate(bias, 1)
            weights = softmax_keys(jnp.where(code_all >= 0, scores, -1000000000.0))
            weights_out[example, group] = weights
            mixture = dot_tn(weights.astype(narrow), qkv_out[2, example, :, columns])
            mix_held[example, :, columns] = unstack_heads(mixture, masks_wide).astype(narrow)
    mix_out[...] = mix_held[...]
    mix = mix_held[...].reshape(bundle * seq, width)
    mid_out[...] = (flat + dot_nt(mix, held[3])).reshape(bundle, seq, width)


def cross_kernel(shards, plans, soon, aliased, *refs):
    refs = list(refs)

    def take(count):
        taken = refs[:count]
        del refs[:count]
        return taken

    (info,) = take(1)
    memory_parts = take(shards)
    mid_in, gains = take(2)
    pieces = take(len(plans))
    take(aliased)
    own_output, own_grad = take(2)
    sent_parts = take(shards - 1)
    (
        early_out,
        normed_b_out,
        d_query_out,
        d_pair_out,
        mix_out,
        d_mid_out,
        normed_c_out,
        d_hidden_out,
        active_out,
        d_top_out,
        d_gain_b_out,
        d_gain_c_out,
        squares_out,
    ) = take(13)
    d_keys_out, d_values_out = d_pair_out.at[0], d_pair_out.at[1]
    held, sems, memory_held, keys_held, values_held, weights_held, rows_held, query_held = take(8)
    sem_list = [sems.at[index] for index in range(len(plans))]

    @pl.when(pl.program_id(0) == 0)
    def _():
        start_weights(info, pieces, plans, held, sem_list)
        wait_weights(plans[:soon], held, sem_list[:soon])

    masks = head_masks(narrow)
    masks_wide = head_masks(wide)
    scaling = 1.0 / math.sqrt(head_dim)
    bundle, seq, width = mid_in.shape
    memory_len = memory_held.shape[1]
    memory_rows = memory_len // shards
    groups = width // quad_width

    def flatten(block):
        return block.reshape(block.shape[0] * block.shape[1], block.shape[2])

    def unflatten(block):
        return block.reshape(bundle, block.shape[0] // bundle, block.shape[1])

    for index, part in enumerate(memory_parts):
        memory_held[:, index * memory_rows : (index + 1) * memory_rows, :] = part[
            :, :memory_rows, :
        ]
    place_rows(info, memory_parts, d_top_out, memory_rows)
    mid = flatten(mid_in[...])
    rows_b = mid.astype(narrow).astype(wide)
    normed_b = (rows_b * norm_scale(rows_b) * gains[1:2, :]).astype(narrow)
    normed_b_out[...] = unflatten(normed_b)
    query_held[...] = unflatten(dot_nn(normed_b, held[0]).astype(narrow))
    memory_flat = flatten(memory_held[...])
    keys_held[...] = unflatten(dot_nn(memory_flat, held[1]).astype(narrow))
    values_held[...] = unflatten(dot_nn(memory_flat, held[2]).astype(narrow))
    for example in range(bundle):
        for group in range(groups):
            columns = slice(group * quad_width, (group + 1) * quad_width)
            queries = stack_heads(query_held[example, :, columns], masks)
            scores = dot_nt(keys_held[example, :, columns], queries) * scaling
            weights = softmax_keys(scores)
            weights_held[example, group] = weights
            mixture = dot_tn(weights.astype(narrow), values_held[example, :, columns])
            mix_out[example, :, columns] = unstack_heads(mixture, masks_wide).astype(narrow)
    late = mid + dot_nt(flatten(mix_out[...]), held[3])

    @pl.when(pl.program_id(0) == 0)
    def _():
        wait_weights(plans[soon:], held, sem_list[soon:])

    rows_c = late.astype(narrow).astype(wide)
    normed_c = (rows_c * norm_scale(rows_c) * gains[2:3, :]).astype(narrow)
    normed_c_out[...] = unflatten(normed_c)
    d_top = flatten(d_top_out[...])
    total = late
    d_normed = jnp.zeros((bundle * seq, width), wide)
    up_grams = [jnp.zeros((seq, seq), wide) for _ in range(bundle)]
    down_grams = [jnp.zeros((seq, seq), wide) for _ in range(bundle)]
    slope = math.sqrt(2.0 / math.pi)
    for index in range(4):
        hidden = dot_nn(normed_c, held[4 + index])
        square = hidden * hidden
        bend = jnp.tanh(slope * hidden * (1.0 + 0.044715 * square))
        half = 0.5 * (1.0 + bend)
        active = (hidden * half).astype(narrow)
        steep = half + 0.5 * hidden * (1.0 - bend * bend) * (
            slope * (1.0 + (3.0 * 0.044715) * square)
        )
        total = total + dot_nt(active, held[8 + index])
        d_hidden = (dot_nn(d_top, held[8 + index]) * steep).astype(narrow)
        d_normed = d_normed + dot_nt(d_hidden, held[4 + index])
        active_out[index] = unflatten(active)
        d_hidden_out[index] = unflatten(d_hidden)
        for example in range(bundle):
            span = slice(example * seq, (example + 1) * seq)
            up_grams[example] += dot_nt(d_hidden[span], d_hidden[span])
            down_grams[example] += dot_nt(active[span], active[span])
    rows_held[...] = unflatten(total)
    for index in range(shards):
        start = pl.multiple_of((info[2] ^ index) * (seq // shards), seq // shards)
        block = rows_held[:, pl.ds(start, seq // shards), :].astype(narrow)
        if index:
            sent_parts[index - 1][:, memory_rows:, :] = block
        else:
            own_output[...] = block
    d_rows, d_gain_rows = norm_back(rows_c, gains[2:3, :], d_normed)
    d_gain_c = jnp.sum(unflatten(d_gain_rows), 1, keepdims=True)
    d_gain_c_out[...] = d_gain_c
    d_mid = d_top.astype(wide) + d_rows
    d_mid_low = d_mid.astype(narrow)
    d_mid_out[...] = unflatten(d_mid_low)
    d_mix = dot_nn(d_mid_low, held[3]).astype(narrow)
    squares = []
    for example in range(bundle):
        span = slice(example * seq, (example + 1) * seq)
        for group in range(groups):
            columns = slice(group * quad_width, (group + 1) * quad_width)
            keys = keys_held[example, :, columns]
            queries = stack_heads(query_held[example, :, columns], masks)
            d_mixes = stack_heads(d_mix[span, columns], masks)
            weights = weights_held[example, group]
            d_weights = dot_nt(values_held[example, :, columns], d_mixes)
            inner = jnp.sum(weights * d_weights, 0, keepdims=True)
            d_scores = (weights * (d_weights - inner)).astype(narrow)
            d_query_out[example, :, columns] = (
                unstack_heads(dot_tn(d_scores, keys), masks_wide) * scaling
            ).astype(narrow)
            d_keys_out[example, :, columns] = (dot_nn(d_scores, queries) * scaling).astype(narrow)
            d_values_out[example, :, columns] = dot_nn(weights.astype(narrow), d_mixes).astype(
                narrow
            )
        memory_grad = dot_nt(d_keys_out[example], held[1]) + dot_nt(d_values_out[example], held[2])
        own_grad[example] = memory_grad[:memory_rows]
        for index, part in enumerate(sent_parts):
            part[example, :memory_rows, :] = memory_grad[
                (index + 1) * memory_rows : (index + 2) * memory_rows
            ].astype(narrow)
        d_query = d_query_out[example]
        mix = mix_out[example]
        square_sum = gram_squares(normed_b[span], dot_nt(d_query, d_query))
        square_sum += gram_squares(mix, dot_nt(d_mid_low[span], d_mid_low[span]))
        square_sum += gram_squares(normed_c[span], up_grams[example])
        square_sum += gram_squares(d_top[span], down_grams[example])
        for block in (d_keys_out, d_values_out):
            product = dot_tn(memory_held[example], block[example])
            square_sum += fold_lanes(jnp.sum(product * product, 0, keepdims=True))
        square_sum += fold_lanes(d_gain_c[example] * d_gain_c[example])
        squares.append(square_sum)
    d_normed_b = dot_nt(flatten(d_query_out[...]), held[0])
    d_rows_b, d_gain_rows = norm_back(rows_b, gains[1:2, :], d_normed_b)
    d_gain_b = jnp.sum(unflatten(d_gain_rows), 1, keepdims=True)
    d_gain_b_out[...] = d_gain_b
    for example in range(bundle):
        squares_out[example] = squares[example] + fold_lanes(
            d_gain_b[example] * d_gain_b[example]
        )
    early_out[...] = unflatten(d_mid + d_rows_b)


def self_backward_kernel(shards, plans, *refs):
    refs = list(refs)

    def take(count):
        taken = refs[:count]
        del refs[:count]
        return taken

    info, early_in, rows_in, normed_in, qkv_in, weights_in, mix_in = take(7)
    squares_in, d_gain_b, d_gain_c, buckets, gains = take(5)
    pieces = take(len(plans))
    tokens_grads = take(shards)
    d_qkv_out, d_early_out, small_out, norms_out = take(4)
    held, sems, rows_held, bias_held, folded_held = take(5)
    sem_list = [sems.at[index] for index in range(len(plans))]

    @pl.when(pl.program_id(0) == 0)
    def _():
        start_weights(info, pieces, plans, held, sem_list)
        wait_weights(plans, held, sem_list)

    masks = head_masks(narrow)
    masks_wide = head_masks(wide)
    scaling = 1.0 / math.sqrt(head_dim)
    bundle, seq, width = early_in.shape
    groups = width // quad_width
    bucket_count = bias_held.shape[0] // (groups * quad)

    def flatten(block):
        return block.reshape(block.shape[0] * block.shape[1], block.shape[2])

    def unflatten(block):
        return block.reshape(bundle, block.shape[0] // bundle, block.shape[1])

    early = flatten(early_in[...])
    d_early = early.astype(narrow)
    d_early_out[...] = unflatten(d_early)
    d_mix = dot_nn(d_early, held[3]).astype(narrow)
    squares = []
    for example in range(bundle):
        span = slice(example * seq, (example + 1) * seq)
        code = buckets[example].T
        for group in range(groups):
            columns = slice(group * quad_width, (group + 1) * quad_width)
            keys = qkv_in[1, example, :, columns]
            queries = stack_heads(qkv_in[0, example, :, columns], masks)
            d_mixes = stack_heads(d_mix[span, columns], masks)
            weights = weights_in[example, group]
            d_weights = dot_nt(qkv_in[2, example, :, columns], d_mixes)
            inner = jnp.sum(weights * d_weights, 0, keepdims=True)
            d_scores = (weights * (d_weights - inner)).astype(narrow)
            d_qkv_out[0, example, :, columns] = (
                unstack_heads(dot_tn(d_scores, keys), masks_wide) * scaling
            ).astype(narrow)
            d_qkv_out[1, example, :, columns] = (dot_nn(d_scores, queries) * scaling).astype(
                narrow
            )
            d_qkv_out[2, example, :, columns] = dot_nn(weights.astype(narrow), d_mixes).astype(
                narrow
            )
            d_wide = d_scores.astype(wide)
            for head in range(quad):
                folded_held[group * quad + head] = fold_causal(
                    d_wide[:, head * seq : (head + 1) * seq]
                )
        code = fold_causal(code)
        for bucket in range(bucket_count):
            chosen = code == bucket
            for head in range(groups * quad):
                picked = jnp.where(chosen, folded_held[head], 0.0)
                spot = head * bucket_count + bucket
                bias_held[spot : spot + 1, :] = jnp.sum(picked, 0, keepdims=True)
        d_bias = lax.dot_general(
            jnp.ones((8, 128), wide),
            bias_held[...],
            (((1,), (1,)), ((), ())),
            precision=lax.Precision.HIGHEST,
            preferred_element_type=wide,
        )[:1]
        small_out[example, :, 3 * width :] = d_bias
        grams = jnp.zeros((seq, seq), wide)
        for index in range(3):
            block = d_qkv_out[index, example]
            grams = grams + dot_nt(block, block)
        square_sum = gram_squares(normed_in[example], grams)
        square_sum += gram_squares(mix_in[example], dot_nt(d_early[span], d_early[span]))
        square_sum += fold_lanes(d_bias * d_bias)
        squares.append(square_sum)
    d_normed = dot_nt(flatten(d_qkv_out[0]), held[0])
    d_normed = d_normed + dot_nt(flatten(d_qkv_out[1]), held[1])
    d_normed = d_normed + dot_nt(flatten(d_qkv_out[2]), held[2])
    d_rows, d_gain_rows = norm_back(flatten(rows_in[...]).astype(wide), gains[0:1, :], d_normed)
    d_gain = jnp.sum(unflatten(d_gain_rows), 1, keepdims=True)
    small_out[:, :, :width] = d_gain
    small_out[:, :, width : 2 * width] = d_gain_b[...]
    small_out[:, :, 2 * width : 3 * width] = d_gain_c[...]
    for example in range(bundle):
        square_sum = (
            squares[example]
            + squares_in[example]
            + fold_lanes(d_gain[example] * d_gain[example])
        )
        total = jnp.sum(square_sum, -1, keepdims=True) + epsilon
        norms_out[example] = jnp.broadcast_to(jnp.sqrt(total), (1, 128))
    rows_held[...] = unflatten(early + d_rows)
    split_rows(info, rows_held, tokens_grads)


class Gradients:
    def __init__(self, info, clip, loads, load_sems, scaled, tile, held, store_sems):
        self.info, self.clip, self.scaled = info, clip, scaled
        self.tile, self.held, self.store_sems = tile, held, store_sems
        self.copies = [
            pltpu.make_async_copy(source, target, load_sems.at[index])
            for index, (source, target) in enumerate(loads)
        ]
        self.targets = [target for source, target in loads]
        self.stores = []
        for copy in self.copies:
            copy.start()

    def read(self, index):
        self.copies[index].wait()
        return self.targets[index]

    def scale(self, index):
        block = self.read(index)
        count, rows, width = block.shape
        for example in range(count):
            self.scaled[example * rows : (example + 1) * rows, :] = (
                block[example].astype(wide) * self.clip[example]
            ).astype(narrow)

    def product(self, index):
        block = self.read(index)
        return dot_tn(self.scaled[...], block[...].reshape(self.scaled.shape[0], block.shape[-1]))

    def write(self, value, outs, unit, places):
        number = len(self.stores) // 2
        tile = self.tile.at[number % 2]
        tile[...] = value.astype(narrow)
        halves = self.held.at[number]
        count = len(places) // 2
        for slot, (dp_index, tensor_index) in enumerate(places):
            high = pl.multiple_of((dp_index ^ self.info[0]) * 64, 64)
            left = pl.multiple_of((tensor_index ^ self.info[1]) * 128, 128)
            halves[slot // count, slot % count] = tile[pl.ds(high, 64), pl.ds(left, 128)]
        for half, out in enumerate(outs):
            copy = pltpu.make_async_copy(
                halves.at[half], out.at[:, unit], self.store_sems.at[len(self.stores)]
            )
            copy.start()
            self.stores.append(copy)

    def finish(self):
        for copy in self.stores:
            copy.wait()


def inner_gradient_kernel(places, info, clip, left, right, *refs):
    outs = refs[:2]
    rows_held, load_sems, scaled, tile, held, store_sems = refs[2:]
    loads = [(left, rows_held.at[0])]
    loads += [(right.at[unit], rows_held.at[1 + unit]) for unit in range(4)]
    work = Gradients(info, clip, loads, load_sems, scaled, tile, held, store_sems)
    work.scale(0)
    for unit in range(4):
        work.write(work.product(1 + unit), outs, unit, places)
    work.finish()


def self_gradient_kernel(places, info, clip, normed, d_qkv, d_early, mix, *refs):
    outs = refs[:2]
    rows_held, load_sems, scaled, tile, held, store_sems = refs[2:]
    sources = [normed, d_qkv.at[0], d_qkv.at[1], d_qkv.at[2], d_early, mix]
    loads = [(source, rows_held.at[index]) for index, source in enumerate(sources)]
    work = Gradients(info, clip, loads, load_sems, scaled, tile, held, store_sems)
    work.scale(0)
    for unit in range(3):
        work.write(work.product(1 + unit), outs, unit, places)
    work.scale(4)
    work.write(work.product(5), outs, 3, places)
    work.finish()


def cross_gradient_kernel(shards, chunks, places, info, clip, *refs):
    normed, d_query, d_mid, mix = refs[:4]
    parts = refs[4 : 4 + shards * chunks]
    refs = refs[4 + shards * chunks :]
    d_pair = refs[0]
    outs = refs[1:3]
    rows_held, parts_held, pairs_held, memory_held = refs[3:7]
    load_sems, scaled, tile, held, store_sems = refs[7:]
    count, memory_len = d_pair.shape[1:3]
    part_len = memory_len // shards
    group = count // chunks
    sources = [normed, d_query, d_mid, mix]
    loads = [(source, rows_held.at[index]) for index, source in enumerate(sources)]
    first = len(loads)
    for chunk in range(chunks):
        for index in range(shards):
            place = chunk * shards + index
            loads.append((parts[place].at[:, pl.ds(0, part_len)], parts_held.at[place]))
        for unit in range(2):
            loads.append(
                (d_pair.at[unit, pl.ds(chunk * group, group)], pairs_held.at[2 * chunk + unit])
            )
    work = Gradients(info, clip, loads, load_sems, scaled, tile, held, store_sems)
    work.scale(0)
    work.write(work.product(1), outs, 0, places)
    work.scale(2)
    work.write(work.product(3), outs, 1, places)
    totals = [None, None]
    for chunk in range(chunks):
        start = first + chunk * (shards + 2)
        for index in range(shards):
            block = work.read(start + index)
            for example in range(group):
                top = (example * shards + index) * part_len
                memory_held[chunk, top : top + part_len, :] = (
                    block[example].astype(wide) * clip[chunk * group + example]
                ).astype(narrow)
        for unit in range(2):
            pair = work.read(start + shards + unit)
            product = dot_tn(
                memory_held[chunk], pair[...].reshape(group * memory_len, pair.shape[-1])
            )
            totals[unit] = product if chunk == 0 else totals[unit] + product
    for unit in range(2):
        work.write(totals[unit], outs, 2 + unit, places)
    work.finish()


def stepper(parameter, gradient, momentum, average, step_rate):
    velocity = momentum_decay * momentum + gradient
    updated = parameter - step_rate * (gradient + momentum_decay * velocity)
    averaged = average_decay * average + (1.0 - average_decay) * updated
    return (velocity, averaged, updated)


def update_kernel(shrink, *refs):
    sums = refs[:8]
    params, outs = refs[8:20], refs[20:]

    def gradient(piece, unit):
        total = sums[2 * piece][unit].astype(wide) + sums[2 * piece + 1][unit].astype(wide)
        return total * shrink

    def step(group, spot, value, rate):
        weight, momentum, average = params[3 * group : 3 * group + 3]
        stepped = stepper(weight[spot], value, momentum[spot], average[spot], rate)
        for out, block in zip(outs[3 * group : 3 * group + 3], stepped):
            out[spot] = block

    inside = ((2, 0), (2, 1), (2, 2), (3, 0), (3, 2), (3, 3))
    for index, (piece, unit) in enumerate(inside):
        step(0, index, gradient(piece, unit), matrix_rate)
    for index, (piece, unit) in enumerate(((2, 3), (3, 1))):
        step(1, index, gradient(piece, unit), output_rate)
    for index in range(4):
        spot = (slice(None), slice(128 * index, 128 * (index + 1)))
        step(2, spot, gradient(0, index), matrix_rate)
        step(3, spot, gradient(1, index), matrix_rate)


def assemble_kernel(shards, chunks, *refs):
    refs = list(refs[1:])

    def take(count):
        taken = refs[:count]
        del refs[:count]
        return taken

    arrived = [take(shards - 1) for _ in range(chunks)]
    tokens_parts = take(shards - 1)
    take(3)
    output, tokens_grad, memory_grad = refs
    rows = memory_grad.shape[1]
    for index in range(shards - 1):
        for chunk in range(chunks):

            @pl.when((pl.program_id(0) == index) & (pl.program_id(1) == chunk))
            def _(index=index, chunk=chunk):
                tokens_grad[...] = tokens_parts[index][...].astype(wide)
                block = arrived[chunk][index]
                output[...] = block[:, rows:, :]
                memory_grad[...] = block[:, :rows, :].astype(wide)


def swap(value, axis, bit):
    size = lax.axis_size(axis)
    return lax.ppermute(value, axis, [(index, index ^ bit) for index in range(size)])


def after(value, *earlier):
    return lax.optimization_barrier((value,) + earlier)[0]


def gather_slots(shard):
    gathered = shard[None]
    for axis, bit in gather_order[:3]:
        gathered = jnp.concatenate([gathered, swap(gathered, axis, bit)], 0)
    beside = swap(gathered, *gather_order[3])
    pieces = [gathered, beside, swap(gathered, *gather_order[4]), swap(beside, *gather_order[4])]
    places = slot_places(gather_order, False)
    count = len(places) // 4
    return [
        (piece, places[index * count : (index + 1) * count]) for index, piece in enumerate(pieces)
    ]


def add_stage(kept, arrived):
    half = kept.shape[0] // 2

    def added(start, stop):
        total = kept[start:stop].astype(wide) + arrived[start:stop].astype(wide)
        return total.astype(narrow)

    if not half:
        return added(0, 1)[0], None
    return added(0, half), added(half, 2 * half)


def on_device(
    tokens,
    memory,
    cotangent,
    buckets,
    key_mask,
    task_groups,
    weights_in,
    weights_out,
    weights_up,
    weights_down,
    gains,
    position_bias,
    momentum_in,
    average_in,
    momentum_out,
    average_out,
    momentum_up,
    average_up,
    momentum_down,
    average_down,
    momentum_gain,
    average_gain,
    momentum_bias,
    average_bias,
):
    shards = lax.axis_size("tensor")
    replicas = lax.axis_size("dp")
    me_tensor = lax.axis_index("tensor")
    me_dp = lax.axis_index("dp")
    width = tokens.shape[2]
    seq = buckets.shape[1]
    seq_rows = tokens.shape[1]
    memory_rows = memory.shape[1]
    memory_len = memory_rows * shards
    group_count = tokens.shape[0]
    local = group_count // shards
    chunks = 2 if local % 2 == 0 else 1
    per_chunk = local // chunks
    bundle = 2 if per_chunk % 2 == 0 else 1
    steps = per_chunk // bundle
    bucket_count, heads_local = position_bias.shape
    heads = heads_local * shards
    gain_width = momentum_gain.shape[1]
    staged = shards == tensor_slots and replicas == dp_slots

    slot_base = [me_dp, me_tensor] if staged else [0 * me_dp, 0 * me_tensor]
    kernel_info = jnp.stack(slot_base + [me_tensor]).astype(jnp.int32)

    def square_shards():
        high, across = weights_in.shape[1], weights_in.shape[2]
        split = lambda block: block.reshape(high, -1, across).transpose(1, 0, 2)
        return (
            weights_in.astype(narrow),
            weights_out.astype(narrow).transpose(0, 2, 1),
            split(weights_up.astype(narrow)),
            split(weights_down.astype(narrow).T),
        )

    shard_in, shard_out, shard_up, shard_down = square_shards()
    slot_count = dp_slots * tensor_slots
    plain_places = [(slot // tensor_slots, slot % tensor_slots) for slot in range(slot_count)]

    def gather_late(blocks):
        count = blocks.shape[0]
        if staged:
            whole = lax.all_gather(blocks, ("dp", "tensor"), axis=0)
        else:
            whole = lax.all_gather(blocks, "dp", axis=1, tiled=True)
            whole = lax.all_gather(whole, "tensor", axis=2, tiled=True)
            whole = whole.reshape(count, dp_slots, 64, tensor_slots, 128).transpose(1, 3, 0, 2, 4)
            whole = whole.reshape(slot_count, count, 64, 128)
        return [whole], [(0, count, plain_places, False)]

    def gather_soon(blocks):
        if not staged:
            return gather_late(blocks)
        pieces, plans = [], []
        for piece, places in gather_slots(blocks):
            pieces.append(piece)
            plans.append((0, blocks.shape[0], places, True))
        return pieces, plans

    def exchange(values, start, count):
        found = []
        for index in range(shards):
            first = (me_tensor ^ index) * local + start
            blocks = [lax.dynamic_slice_in_dim(value, first, count, 0) for value in values]
            block = jnp.concatenate(blocks, 1) if len(blocks) > 1 else blocks[0]
            found.append(swap(block, "tensor", index) if index else block)
        return found

    late_pieces, late_plans = gather_late(jnp.concatenate([shard_up, shard_down], 0))
    token_parts = exchange([tokens], 0, local)
    self_pieces, self_plans = gather_soon(jnp.concatenate([shard_in[:3], shard_out[:1]], 0))
    cross_pieces, cross_plans = gather_soon(jnp.concatenate([shard_in[3:6], shard_out[1:2]], 0))
    late_plans = cross_plans + [(4,) + plan[1:] for plan in late_plans]
    late_pieces = cross_pieces + late_pieces
    soon_count = len(cross_pieces)
    table = jnp.pad(position_bias.T, ((0, 0), (0, 128 - bucket_count)))
    table_all = jnp.concatenate(
        [swap(table, "tensor", index) if index else table for index in range(shards)], 0
    )
    memory_parts = []
    earlier = token_parts
    for chunk in range(chunks):
        source, _ = lax.optimization_barrier((memory, earlier[-1]))
        earlier = exchange([source, cotangent], chunk * per_chunk, per_chunk)
        memory_parts.append(earlier)
    bucket_mine = lax.dynamic_slice_in_dim(buckets, me_tensor * local, local, 0)
    mask_mine = lax.dynamic_slice_in_dim(key_mask, me_tensor * local, local, 0)
    groups_mine = lax.dynamic_slice_in_dim(task_groups, me_tensor * local, local, 0)

    smem = pl.BlockSpec(memory_space=pltpu.SMEM)
    anywhere = pl.BlockSpec(memory_space=pl.ANY)
    params = pltpu.CompilerParams(
        vmem_limit_bytes=vmem_bytes, dimension_semantics=("arbitrary",)
    )

    def part_spec(shape, offset=0, lead=None):
        zeros = (0,) * len(shape)
        if lead is None:
            return pl.BlockSpec(
                (bundle,) + tuple(shape), lambda step, *_: (step + offset,) + zeros
            )
        return pl.BlockSpec(
            (lead, bundle) + tuple(shape), lambda step, *_: (0, step + offset) + zeros
        )

    def own_spec(shape, offset=0):
        zeros = (0,) * len(shape)
        return pl.BlockSpec(
            (bundle,) + tuple(shape),
            lambda step, info: (info[2] * (local // bundle) + step + offset,) + zeros,
        )

    def whole_spec(shape):
        return pl.BlockSpec(tuple(shape), lambda step, *_: (0,) * len(shape))

    def shaped(shape, dtype, lead=None, count=local):
        front = (count,) if lead is None else (lead, count)
        return jax.ShapeDtypeStruct(front + tuple(shape), dtype)

    def cost(flops, moved):
        return pl.CostEstimate(
            flops=int(flops * cost_scale), bytes_accessed=int(moved * cost_scale), transcendentals=0
        )

    groups = width // quad_width
    row_block = (seq, width)
    part_rows = memory_rows + seq_rows

    normed_a, rows_a, qkv_a, weights_a, mix_a, mid = pl.pallas_call(
        functools.partial(self_forward_kernel, shards, self_plans, heads_local),
        grid=(local // bundle,),
        in_specs=[smem]
        + [part_spec((seq_rows, width))] * shards
        + [part_spec((seq, seq))] * 2
        + [whole_spec(gains.shape), whole_spec(table_all.shape)]
        + [anywhere] * len(self_pieces),
        out_specs=[
            part_spec(row_block),
            part_spec(row_block),
            part_spec(row_block, lead=3),
            part_spec((groups, seq, quad * seq)),
            part_spec(row_block),
            part_spec(row_block),
        ],
        out_shape=[
            shaped(row_block, narrow),
            shaped(row_block, narrow),
            shaped(row_block, narrow, 3),
            shaped((groups, seq, quad * seq), wide),
            shaped(row_block, narrow),
            shaped(row_block, wide),
        ],
        scratch_shapes=[
            pltpu.VMEM((4, width, width), narrow),
            pltpu.SemaphoreType.DMA((len(self_pieces),)),
            pltpu.VMEM((bundle,) + row_block, narrow),
            pltpu.VMEM((bundle,) + row_block, narrow),
        ],
        compiler_params=params,
        name="self_forward",
        cost_estimate=cost(local * 2e9, local * 2e6),
    )(
        kernel_info,
        *token_parts,
        bucket_mine,
        mask_mine,
        gains,
        table_all,
        *self_pieces,
    )

    def cross(chunk, filled):
        offset = chunk * steps
        gain_block = (1, width)
        kept_specs = [
            part_spec(row_block, offset),
            part_spec(row_block, offset),
            part_spec(row_block, offset),
            part_spec((memory_len, width), offset, 2),
            part_spec(row_block, offset),
            part_spec(row_block, offset),
            part_spec(row_block, offset),
            part_spec(row_block, offset, 4),
            part_spec(row_block, offset, 4),
            part_spec(row_block, offset),
            part_spec(gain_block, offset),
            part_spec(gain_block, offset),
            part_spec((1, 128), offset),
        ]
        kept_shapes = [
            shaped(row_block, wide),
            shaped(row_block, narrow),
            shaped(row_block, narrow),
            shaped((memory_len, width), narrow, 2),
            shaped(row_block, narrow),
            shaped(row_block, narrow),
            shaped(row_block, narrow),
            shaped(row_block, narrow, 4),
            shaped(row_block, narrow, 4),
            shaped(row_block, narrow),
            shaped(gain_block, wide),
            shaped(gain_block, wide),
            shaped((1, 128), wide),
        ]
        own_specs = [own_spec((seq_rows, width), offset), own_spec((memory_rows, width), offset)]
        own_shapes = [
            shaped((seq_rows, width), narrow, count=group_count),
            shaped((memory_rows, width), wide, count=group_count),
        ]
        operands = [kernel_info, *memory_parts[chunk], mid, gains, *late_pieces]
        aliases = {}
        for index, block in enumerate(filled):
            aliases[len(operands) + index] = index if index < 2 else index + shards - 1
        return pl.pallas_call(
            functools.partial(cross_kernel, shards, late_plans, soon_count, len(filled)),
            grid_spec=pltpu.PrefetchScalarGridSpec(
                num_scalar_prefetch=1,
                grid=(steps,),
                in_specs=[part_spec((part_rows, width))] * shards
                + [part_spec(row_block, offset), whole_spec(gains.shape)]
                + [anywhere] * (len(late_pieces) + len(filled)),
                out_specs=own_specs + [part_spec((part_rows, width))] * (shards - 1) + kept_specs,
                scratch_shapes=[
                    pltpu.VMEM((12, width, width), narrow),
                    pltpu.SemaphoreType.DMA((len(late_pieces),)),
                    pltpu.VMEM((bundle, memory_len, width), narrow),
                    pltpu.VMEM((bundle, memory_len, width), narrow),
                    pltpu.VMEM((bundle, memory_len, width), narrow),
                    pltpu.VMEM((bundle, groups, memory_len, quad * seq), wide),
                    pltpu.VMEM((bundle,) + row_block, wide),
                    pltpu.VMEM((bundle,) + row_block, narrow),
                ],
            ),
            out_shape=own_shapes
            + [shaped((part_rows, width), narrow, count=per_chunk)] * (shards - 1)
            + kept_shapes,
            input_output_aliases=aliases,
            compiler_params=params,
            name="cross",
            cost_estimate=cost(per_chunk * 8e9, per_chunk * 6e6),
        )(*operands, *filled)

    filled, sent = [], []
    for chunk in range(chunks):
        found = cross(chunk, filled)
        sent.append(found[2 : shards + 1])
        filled = list(found[:2]) + list(found[shards + 1 :])
    own_output, own_memory = filled[:2]
    (
        early,
        normed_b,
        d_query_b,
        d_pair,
        mix_b,
        d_mid,
        normed_c,
        d_hidden,
        active,
        d_top,
        d_gain_b,
        d_gain_c,
        squares,
    ) = filled[2:]
    arrived = [
        [swap(block, "tensor", index + 1) for index, block in enumerate(blocks)] for blocks in sent
    ]
    soon = [block for blocks in arrived[:-1] for block in blocks]

    found = pl.pallas_call(
        functools.partial(self_backward_kernel, shards, self_plans),
        grid_spec=pltpu.PrefetchScalarGridSpec(
            num_scalar_prefetch=1,
            grid=(local // bundle,),
            in_specs=[
            part_spec(row_block),
            part_spec(row_block),
            part_spec(row_block),
            part_spec(row_block, lead=3),
            part_spec((groups, seq, quad * seq)),
            part_spec(row_block),
            part_spec((1, 128)),
            part_spec((1, width)),
            part_spec((1, width)),
            part_spec((seq, seq)),
            whole_spec(gains.shape),
        ]
        + [anywhere] * len(self_pieces),
        out_specs=[own_spec((seq_rows, width))]
        + [part_spec((seq_rows, width))] * (shards - 1)
        + [
            part_spec(row_block, lead=3),
            part_spec(row_block),
            part_spec((1, 3 * width + heads * bucket_count)),
            part_spec((1, 128)),
        ],
        scratch_shapes=[
            pltpu.VMEM((4, width, width), narrow),
            pltpu.SemaphoreType.DMA((len(self_pieces),)),
            pltpu.VMEM((bundle,) + row_block, wide),
            pltpu.VMEM((heads * bucket_count, 128), wide),
            pltpu.VMEM((heads, seq // 2 + 8, seq), wide),
        ],
        ),
        out_shape=[shaped((seq_rows, width), wide, count=group_count)]
        + [shaped((seq_rows, width), narrow)] * (shards - 1)
        + [
            shaped(row_block, narrow, 3),
            shaped(row_block, narrow),
            shaped((1, 3 * width + heads * bucket_count), wide),
            shaped((1, 128), wide),
        ],
        compiler_params=params,
        name="self_backward",
        cost_estimate=cost(local * 3e9, local * 3e6),
    )(
        after(kernel_info, *soon),
        early,
        rows_a,
        normed_a,
        qkv_a,
        weights_a,
        mix_a,
        squares,
        d_gain_b,
        d_gain_c,
        bucket_mine,
        gains,
        *self_pieces,
    )
    own_tokens, tokens_sent = found[0], found[1:shards]
    d_qkv, d_early, small, norms = found[shards:]

    norms = after(norms.reshape(local, 128), *arrived[-1])
    norm_slots = norms
    bit = 1
    while bit < shards:
        norm_slots = jnp.concatenate([norm_slots, swap(norm_slots, "tensor", bit)], 0)
        bit *= 2
    total = jnp.broadcast_to(jnp.sum(norm_slots, 0, keepdims=True), (8, 128))
    bit = 1
    while bit < replicas:
        total = total + swap(total, "dp", bit)
        bit *= 2
    order = jnp.arange(shards, dtype=jnp.int32) ^ me_tensor
    example_norms = norm_slots[:, 0].reshape(shards, local)[order].reshape(group_count)
    mean_norm = total[0, 0] / (group_count * replicas)
    limits = jnp.sum(
        (groups_mine[:, None] == jnp.arange(len(group_limits), dtype=jnp.int32))
        * jnp.asarray(group_limits, wide),
        1,
    )
    clip_weights = jnp.minimum(1.0 / mean_norm, limits / norms[:, 0])
    small = jnp.sum(clip_weights[:, None, None] * small, 0).reshape(-1, 128)

    def places_of(index):
        return slot_places(reduce_orders[index], True) if staged else plain_places

    out_shape = jax.ShapeDtypeStruct((slot_count // 2, 4, 64, 128), narrow)

    def gradient_call(kernel, clip, operands, loads, extra, name, work):
        return tuple(
            pl.pallas_call(
                kernel,
                in_specs=[smem, smem] + [anywhere] * len(operands),
                out_specs=[anywhere] * 2,
                out_shape=[out_shape] * 2,
                scratch_shapes=extra
                + [
                    pltpu.SemaphoreType.DMA((loads,)),
                    pltpu.VMEM((local * seq, width), narrow),
                    pltpu.VMEM((2, width, width), narrow),
                    pltpu.VMEM((4, 2, slot_count // 2, 64, 128), narrow),
                    pltpu.SemaphoreType.DMA((8,)),
                ],
                compiler_params=pltpu.CompilerParams(vmem_limit_bytes=vmem_bytes),
                name=name,
                cost_estimate=work,
            )(kernel_info, clip, *operands)
        )

    def inner_gradients(index, clip, left, right):
        kernel = functools.partial(inner_gradient_kernel, places_of(index))
        extra = [pltpu.VMEM((5, local, seq, width), narrow)]
        return gradient_call(
            kernel, clip, [left, right], 5, extra, "inner_gradients", cost(5e9, 7e6)
        )

    def self_gradients(clip):
        kernel = functools.partial(self_gradient_kernel, places_of(2))
        extra = [pltpu.VMEM((6, local, seq, width), narrow)]
        operands = [normed_a, d_qkv, d_early, mix_a]
        return gradient_call(kernel, clip, operands, 6, extra, "self_gradients", cost(5e9, 8e6))

    def cross_gradients(clip):
        kernel = functools.partial(cross_gradient_kernel, shards, chunks, places_of(3))
        extra = [
            pltpu.VMEM((4, local, seq, width), narrow),
            pltpu.VMEM((chunks * shards, per_chunk, memory_rows, width), narrow),
            pltpu.VMEM((2 * chunks, per_chunk, memory_len, width), narrow),
            pltpu.VMEM((chunks, per_chunk * memory_len, width), narrow),
        ]
        operands = [normed_b, d_query_b, d_mid, mix_b]
        operands += [block for blocks in memory_parts for block in blocks] + [d_pair]
        loads = 4 + chunks * (shards + 2)
        return gradient_call(
            kernel, clip, operands, loads, extra, "cross_gradients", cost(9e9, 20e6)
        )

    tokens_arrived = [swap(block, "tensor", index + 1) for index, block in enumerate(tokens_sent)]

    def by_place(shape, index, chunk=None):
        def spot(place, step, info):
            if chunk is not None:
                return (0, 0, 0)
            return (jnp.where(place == index, step, jnp.where(place < index, 0, chunks - 1)), 0, 0)

        return pl.BlockSpec((per_chunk,) + shape, spot)

    def to_place(shape):
        return pl.BlockSpec(
            (per_chunk,) + shape,
            lambda place, step, info: ((info[2] ^ (place + 1)) * chunks + step, 0, 0),
        )

    small_rows, large_rows = (seq_rows, width), (memory_rows, width)
    operands = [block for blocks in arrived for block in blocks] + tokens_arrived
    assemble = pl.pallas_call(
        functools.partial(assemble_kernel, shards, chunks),
        grid_spec=pltpu.PrefetchScalarGridSpec(
            num_scalar_prefetch=1,
            grid=(shards - 1, chunks),
            in_specs=[
                by_place((part_rows, width), index, chunk)
                for chunk in range(chunks)
                for index in range(shards - 1)
            ]
            + [by_place(small_rows, index) for index in range(shards - 1)]
            + [anywhere] * 3,
            out_specs=[to_place(small_rows), to_place(small_rows), to_place(large_rows)],
        ),
        out_shape=[
            jax.ShapeDtypeStruct((group_count,) + small_rows, narrow),
            jax.ShapeDtypeStruct((group_count,) + small_rows, wide),
            jax.ShapeDtypeStruct((group_count,) + large_rows, wide),
        ],
        input_output_aliases={len(operands) + 1 + index: index for index in range(3)},
        compiler_params=pltpu.CompilerParams(
            vmem_limit_bytes=vmem_bytes, dimension_semantics=("arbitrary", "arbitrary")
        ),
        name="assemble",
        cost_estimate=cost(1e6, 20e6),
    )
    returned = operands + [own_output, own_tokens, own_memory]

    pairs = [None] * 4

    last_stage = len(reduce_orders[0]) - 1
    done = [0] * 4

    def travel(*indices):
        for index in indices:
            if staged and done[index] <= last_stage:
                kept, sent = pairs[index]
                order = reduce_orders[index][done[index]]
                pairs[index] = add_stage(kept, swap(sent, *order))
                done[index] += 1

    def arrive_as_one(*indices):
        (stage,) = {reduce_orders[index][done[index]] for index in indices}
        sents = [pairs[index][1] for index in indices]
        came = swap(jnp.concatenate(sents, 0), *stage)
        found, start = [], 0
        for index, sent in zip(indices, sents):
            found.append(came[start : start + sent.shape[0]])
            start += sent.shape[0]
            done[index] += 1
        return found

    def there(*indices):
        return [block for index in indices for block in pairs[index] if block is not None]

    pairs[0] = inner_gradients(0, clip_weights, normed_c, d_hidden)
    clip = after(clip_weights, *there(0))
    pairs[1] = inner_gradients(1, clip, d_top, active)
    travel(0)
    clip = after(clip_weights, *there(0, 1))
    pairs[2] = self_gradients(clip)
    travel(1)
    clip = after(clip_weights, *there(1, 2), *tokens_arrived)
    pairs[3] = cross_gradients(clip)
    travel(0, 1)
    travel(2, 3)

    def together(*extra):
        held = lax.optimization_barrier((pairs, extra))
        pairs[:] = held[0]
        return held[1]

    def assembled():
        return assemble(after(kernel_info, *there(0)), *returned)

    shrink = 1.0 / math.sqrt(group_count * replicas)
    if staged:
        small = small + swap(small, *core)
        (small,) = together(small)
        small = small + swap(small, *side)
        travel(0, 1, 2, 3)
        output, tokens_grad, memory_grad = assembled()
        small, output = together(small, output)
        small = small + swap(small, *row)
        for index, came in zip((0, 3), arrive_as_one(0, 3)):
            pairs[index] = add_stage(pairs[index][0], came)
        travel(1, 2)
        (small,) = together(small)
        small = small + swap(small, *near)
        last = [None] * 4
        came = arrive_as_one(0, 1, 2)
        for index in (0, 1):
            last[index] = (pairs[index][0][0], came[index][0])
        pairs[2] = add_stage(pairs[2][0], came[2])
        travel(3)
        small, last = lax.optimization_barrier((small, last))
        small = small + swap(small, *far)
        for index in (2, 3):
            kept, sent = pairs[index]
            last[index] = (kept[0], swap(sent, *reduce_orders[index][-1])[0])
        last = [block for pair in last for block in pair]
    else:
        output, tokens_grad, memory_grad = assembled()
        reduced = []
        for kept, sent in pairs:
            whole = jnp.concatenate([kept, sent], 0)
            count = whole.shape[1]
            whole = whole.reshape(dp_slots, tensor_slots, count, 64, 128).transpose(2, 0, 3, 1, 4)
            whole = whole.reshape(count, width, width)
            whole = lax.psum_scatter(whole, "dp", scatter_dimension=1, tiled=True)
            reduced.append(lax.psum_scatter(whole, "tensor", scatter_dimension=2, tiled=True))
        small = lax.psum(small, ("dp", "tensor"))
    small = small.reshape(-1)
    gain_total = small[: 3 * width].reshape(3, width)
    bias_total = small[3 * width :].reshape(heads, bucket_count).T

    large = [
        (weights_in, momentum_in, average_in, matrix_rate),
        (weights_out, momentum_out, average_out, output_rate),
        (weights_up, momentum_up, average_up, matrix_rate),
        (weights_down, momentum_down, average_down, matrix_rate),
    ]
    if staged:
        turns = ((0, 1, 2), (0, 2, 1), (0, 1), (1, 0))
        turned = [
            block.transpose(turn) for group, turn in zip(large, turns) for block in group[:3]
        ]
        operands = last + turned
        stepped = pl.pallas_call(
            functools.partial(update_kernel, shrink),
            out_shape=[
                jax.ShapeDtypeStruct(block.shape, wide) for block in turned
            ],
            compiler_params=pltpu.CompilerParams(vmem_limit_bytes=vmem_bytes),
            name="update",
            cost_estimate=cost(1e6, 4e6),
        )(*operands)
        stepped = [block.transpose(turns[index // 3]) for index, block in enumerate(stepped)]
    else:
        reduced = [block.astype(wide) * shrink for block in reduced]

        def merge(blocks):
            count, high, across = blocks.shape
            return blocks.transpose(1, 0, 2).reshape(high, count * across)

        inside = jnp.concatenate([reduced[2][:3], reduced[3][:1], reduced[3][2:]], 0)
        outward = jnp.stack([reduced[2][3].T, reduced[3][1].T], 0)
        gradients = [inside, outward, merge(reduced[0]), merge(reduced[1]).T]
        stepped = []
        for (weight, momentum, average, rate), gradient in zip(large, gradients):
            stepped += stepper(weight, gradient, momentum, average, rate)
    (
        velocity_in,
        averaged_in,
        updated_in,
        velocity_out,
        averaged_out,
        updated_out,
        velocity_up,
        averaged_up,
        updated_up,
        velocity_down,
        averaged_down,
        updated_down,
    ) = stepped

    gain_start = me_tensor * gain_width
    gain_shard = lax.dynamic_slice_in_dim(gains, gain_start, gain_width, 1)
    gain_grad = lax.dynamic_slice_in_dim(gain_total, gain_start, gain_width, 1) * shrink
    bias_grad = (
        lax.dynamic_slice_in_dim(bias_total, me_tensor * heads_local, heads_local, 1) * shrink
    )
    velocity_gain, averaged_gain, updated_gain = stepper(
        gain_shard, gain_grad, momentum_gain, average_gain, small_rate
    )
    velocity_bias, averaged_bias, updated_bias = stepper(
        position_bias, bias_grad, momentum_bias, average_bias, small_rate
    )
    return (
        output,
        tokens_grad,
        memory_grad,
        example_norms,
        velocity_in,
        averaged_in,
        updated_in,
        velocity_out,
        averaged_out,
        updated_out,
        velocity_up,
        averaged_up,
        updated_up,
        velocity_down,
        averaged_down,
        updated_down,
        velocity_gain,
        averaged_gain,
        updated_gain,
        velocity_bias,
        averaged_bias,
        updated_bias,
    )


def solution(mesh):
    return jax.shard_map(
        on_device,
        mesh=mesh,
        in_specs=(
            P("dp", "tensor", None),
            P("dp", "tensor", None),
            P("dp", "tensor", None),
            P("dp", None, None),
            P("dp", None, None),
            P("dp"),
            P(None, "dp", "tensor"),
            P(None, "tensor", "dp"),
            P("dp", "tensor"),
            P("tensor", "dp"),
            P(),
            P(None, "tensor"),
            P(None, "dp", "tensor"),
            P(None, "dp", "tensor"),
            P(None, "tensor", "dp"),
            P(None, "tensor", "dp"),
            P("dp", "tensor"),
            P("dp", "tensor"),
            P("tensor", "dp"),
            P("tensor", "dp"),
            P(None, "tensor"),
            P(None, "tensor"),
            P(None, "tensor"),
            P(None, "tensor"),
        ),
        out_specs=(
            P("dp", "tensor", None),
            P("dp", "tensor", None),
            P("dp", "tensor", None),
            P("dp"),
            P(None, "dp", "tensor"),
            P(None, "dp", "tensor"),
            P(None, "dp", "tensor"),
            P(None, "tensor", "dp"),
            P(None, "tensor", "dp"),
            P(None, "tensor", "dp"),
            P("dp", "tensor"),
            P("dp", "tensor"),
            P("dp", "tensor"),
            P("tensor", "dp"),
            P("tensor", "dp"),
            P("tensor", "dp"),
            P(None, "tensor"),
            P(None, "tensor"),
            P(None, "tensor"),
            P(None, "tensor"),
            P(None, "tensor"),
            P(None, "tensor"),
        ),
        check_vma=False,
    )
```

```python
import functools
import math

import jax
import jax.numpy as jnp
from jax import lax
from jax.experimental import pallas as pl
from jax.experimental.pallas import tpu as pltpu
from jax.sharding import PartitionSpec as P

epsilon = 1e-06
momentum_decay = 0.9
average_decay = 0.7
matrix_rate = 10.0
output_rate = 40.0
small_rate = 50.0
group_limits = (0.6, 0.85, 1.2, 1.7)
head_dim = 64
quad = 4
quad_width = quad * head_dim
dp_slots = 8
tensor_slots = 4
wide = jnp.float32
narrow = jnp.bfloat16
vmem_bytes = 58 * 2**20
cost_scale = 1.0

core = ("tensor", 1)
row = ("tensor", 2)
side = ("dp", 1)
near = ("dp", 2)
far = ("dp", 4)
gather_order = (far, near, row, side, core)
reduce_orders = (
    (core, side, near, row, far),
    (core, row, near, side, far),
    (core, row, near, side, far),
    (core, side, row, near, far),
)


def dot_nn(left, right):
    return lax.dot_general(left, right, (((1,), (0,)), ((), ())), preferred_element_type=wide)


def dot_nt(left, right):
    return lax.dot_general(left, right, (((1,), (1,)), ((), ())), preferred_element_type=wide)


def dot_tn(left, right):
    return lax.dot_general(left, right, (((0,), (0,)), ((), ())), preferred_element_type=wide)


def head_masks(dtype):
    lanes = lax.broadcasted_iota(jnp.int32, (1, quad_width), 1) // head_dim
    return [(lanes == head).astype(wide).astype(dtype) for head in range(quad)]


def stack_heads(block, masks):
    return jnp.concatenate([block * mask for mask in masks], 0)


def unstack_heads(block, masks):
    rows = block.shape[0] // quad
    total = block[:rows] * masks[0]
    for head in range(1, quad):
        total = total + block[head * rows : (head + 1) * rows] * masks[head]
    return total


def norm_scale(rows):
    return lax.rsqrt(jnp.mean(rows * rows, -1, keepdims=True) + epsilon)


def norm_back(rows, gain, d_normed):
    scaling = norm_scale(rows)
    weighted = d_normed * gain
    cubed = scaling * scaling * scaling
    d_rows = scaling * weighted - rows * cubed * jnp.mean(rows * weighted, -1, keepdims=True)
    return d_rows, d_normed * rows * scaling


def softmax_keys(scores):
    peak = jnp.max(scores, 0, keepdims=True)
    weights = jnp.exp(scores - peak)
    return weights * (1.0 / jnp.sum(weights, 0, keepdims=True))


def gram_squares(left, right_grams):
    return jnp.sum(dot_nt(left, left) * right_grams, 0, keepdims=True)


def fold_causal(block):
    size = block.shape[0]
    lanes = lax.broadcasted_iota(jnp.int32, (8, size), 1)
    rows = [block[:8], block[size // 2 : size // 2 + 8]]
    for start in range(8, size // 2, 8):
        other = pltpu.roll(block[size - start : size - start + 8], start, 1)
        rows.append(jnp.where(lanes >= start, block[start : start + 8], other))
    return jnp.concatenate(rows, 0)


def fold_lanes(row_sums):
    width = row_sums.shape[1]
    total = row_sums[:, :128]
    for start in range(128, width, 128):
        total = total + row_sums[:, start : start + 128]
    return total


def slot_places(order, first_is_high):
    places = []
    count = len(order)
    for slot in range(1 << count):
        index = {"dp": 0, "tensor": 0}
        for stage, (axis, bit) in enumerate(order):
            place = count - 1 - stage if first_is_high else stage
            if (slot >> place) & 1:
                index[axis] |= bit
        places.append((index["dp"], index["tensor"]))
    return places


def start_weights(info, pieces, plans, held, sems):
    for piece, (first, count, places, relative), sem in zip(pieces, plans, sems):
        for slot, (dp_index, tensor_index) in enumerate(places):
            if relative:
                high = pl.multiple_of((dp_index ^ info[0]) * 64, 64)
                left = pl.multiple_of((tensor_index ^ info[1]) * 128, 128)
            else:
                high, left = dp_index * 64, tensor_index * 128
            pltpu.make_async_copy(
                piece.at[slot],
                held.at[pl.ds(first, count), pl.ds(high, 64), pl.ds(left, 128)],
                sem,
            ).start()


def wait_weights(plans, held, sems):
    for (first, count, places, relative), sem in zip(plans, sems):
        share = 512 * len(places) // (dp_slots * tensor_slots)
        whole = held.at[pl.ds(first, count), pl.ds(0, share)]
        pltpu.make_async_copy(whole, whole, sem).wait()


def place_rows(info, parts, held, first=0):
    rows = held.shape[1] // len(parts)
    for index, part in enumerate(parts):
        start = pl.multiple_of((info[2] ^ index) * rows, rows)
        held[:, pl.ds(start, rows), :] = part[:, first : first + rows, :]


def split_rows(info, held, parts, first=0):
    rows = held.shape[1] // len(parts)
    for index, part in enumerate(parts):
        start = pl.multiple_of((info[2] ^ index) * rows, rows)
        part[:, first : first + rows, :] = held[:, pl.ds(start, rows), :].astype(part.dtype)


def self_forward_kernel(shards, plans, heads_local, *refs):
    refs = list(refs)

    def take(count):
        taken = refs[:count]
        del refs[:count]
        return taken

    (info,) = take(1)
    parts = take(shards)
    buckets, key_mask, gains, table = take(4)
    pieces = take(len(plans))
    normed_out, rows_out, qkv_out, weights_out, mix_out, mid_out = take(6)
    held, sems, rows_held, mix_held = take(4)
    sem_list = [sems.at[index] for index in range(len(plans))]

    @pl.when(pl.program_id(0) == 0)
    def _():
        start_weights(info, pieces, plans, held, sem_list)
        wait_weights(plans, held, sem_list)

    masks = head_masks(narrow)
    masks_wide = head_masks(wide)
    place_rows(info, parts, rows_held)
    rows_out[...] = rows_held[...]
    bundle, seq, width = rows_held.shape
    flat = rows_held[...].reshape(bundle * seq, width).astype(wide)
    normed = (flat * norm_scale(flat) * gains[0:1, :]).astype(narrow)
    normed_out[...] = normed.reshape(bundle, seq, width)
    for index in range(3):
        value = dot_nn(normed, held[index]).astype(narrow)
        qkv_out[index] = value.reshape(bundle, seq, width)
    for example in range(bundle):
        code = jnp.where(key_mask[example] > 0, buckets[example], -1).T
        safe = jnp.maximum(code, 0)
        code_all = jnp.concatenate([code] * quad, 1)
        for group in range(width // quad_width):
            columns = slice(group * quad_width, (group + 1) * quad_width)
            bias = []
            for head in range(group * quad, (group + 1) * quad):
                spot = ((head // heads_local) ^ info[2]) * heads_local + head % heads_local
                line = jnp.broadcast_to(table[pl.ds(spot, 1), :], (seq, 128))
                bias.append(jnp.take_along_axis(line, safe, axis=1))
            queries = stack_heads(qkv_out[0, example, :, columns], masks)
            scores = dot_nt(qkv_out[1, example, :, columns], queries) * (
                1.0 / math.sqrt(head_dim)
            ) + jnp.concatenate(bias, 1)
            weights = softmax_keys(jnp.where(code_all >= 0, scores, -1000000000.0))
            weights_out[example, group] = weights
            mixture = dot_tn(weights.astype(narrow), qkv_out[2, example, :, columns])
            mix_held[example, :, columns] = unstack_heads(mixture, masks_wide).astype(narrow)
    mix_out[...] = mix_held[...]
    mix = mix_held[...].reshape(bundle * seq, width)
    mid_out[...] = (flat + dot_nt(mix, held[3])).reshape(bundle, seq, width)


def cross_kernel(shards, plans, soon, aliased, *refs):
    refs = list(refs)

    def take(count):
        taken = refs[:count]
        del refs[:count]
        return taken

    (info,) = take(1)
    memory_parts = take(shards)
    mid_in, gains = take(2)
    pieces = take(len(plans))
    take(aliased)
    own_output, own_grad = take(2)
    sent_parts = take(shards - 1)
    (
        early_out,
        normed_b_out,
        d_query_out,
        d_pair_out,
        mix_out,
        d_mid_out,
        normed_c_out,
        d_hidden_out,
        active_out,
        d_top_out,
        d_gain_b_out,
        d_gain_c_out,
        squares_out,
    ) = take(13)
    d_keys_out, d_values_out = d_pair_out.at[0], d_pair_out.at[1]
    held, sems, memory_held, keys_held, values_held, weights_held, rows_held, query_held = take(8)
    sem_list = [sems.at[index] for index in range(len(plans))]

    @pl.when(pl.program_id(0) == 0)
    def _():
        start_weights(info, pieces, plans, held, sem_list)
        wait_weights(plans[:soon], held, sem_list[:soon])

    masks = head_masks(narrow)
    masks_wide = head_masks(wide)
    scaling = 1.0 / math.sqrt(head_dim)
    bundle, seq, width = mid_in.shape
    memory_len = memory_held.shape[1]
    memory_rows = memory_len // shards
    groups = width // quad_width

    def flatten(block):
        return block.reshape(block.shape[0] * block.shape[1], block.shape[2])

    def unflatten(block):
        return block.reshape(bundle, block.shape[0] // bundle, block.shape[1])

    for index, part in enumerate(memory_parts):
        memory_held[:, index * memory_rows : (index + 1) * memory_rows, :] = part[
            :, :memory_rows, :
        ]
    place_rows(info, memory_parts, d_top_out, memory_rows)
    mid = flatten(mid_in[...])
    rows_b = mid.astype(narrow).astype(wide)
    normed_b = (rows_b * norm_scale(rows_b) * gains[1:2, :]).astype(narrow)
    normed_b_out[...] = unflatten(normed_b)
    query_held[...] = unflatten(dot_nn(normed_b, held[0]).astype(narrow))
    memory_flat = flatten(memory_held[...])
    keys_held[...] = unflatten(dot_nn(memory_flat, held[1]).astype(narrow))
    values_held[...] = unflatten(dot_nn(memory_flat, held[2]).astype(narrow))
    for example in range(bundle):
        for group in range(groups):
            columns = slice(group * quad_width, (group + 1) * quad_width)
            queries = stack_heads(query_held[example, :, columns], masks)
            scores = dot_nt(keys_held[example, :, columns], queries) * scaling
            weights = softmax_keys(scores)
            weights_held[example, group] = weights
            mixture = dot_tn(weights.astype(narrow), values_held[example, :, columns])
            mix_out[example, :, columns] = unstack_heads(mixture, masks_wide).astype(narrow)
    late = mid + dot_nt(flatten(mix_out[...]), held[3])

    @pl.when(pl.program_id(0) == 0)
    def _():
        wait_weights(plans[soon:], held, sem_list[soon:])

    rows_c = late.astype(narrow).astype(wide)
    normed_c = (rows_c * norm_scale(rows_c) * gains[2:3, :]).astype(narrow)
    normed_c_out[...] = unflatten(normed_c)
    d_top = flatten(d_top_out[...])
    total = late
    d_normed = jnp.zeros((bundle * seq, width), wide)
    up_grams = [jnp.zeros((seq, seq), wide) for _ in range(bundle)]
    down_grams = [jnp.zeros((seq, seq), wide) for _ in range(bundle)]
    slope = math.sqrt(2.0 / math.pi)
    for index in range(4):
        hidden = dot_nn(normed_c, held[4 + index])
        square = hidden * hidden
        bend = jnp.tanh(slope * hidden * (1.0 + 0.044715 * square))
        half = 0.5 * (1.0 + bend)
        active = (hidden * half).astype(narrow)
        steep = half + 0.5 * hidden * (1.0 - bend * bend) * (
            slope * (1.0 + (3.0 * 0.044715) * square)
        )
        total = total + dot_nt(active, held[8 + index])
        d_hidden = (dot_nn(d_top, held[8 + index]) * steep).astype(narrow)
        d_normed = d_normed + dot_nt(d_hidden, held[4 + index])
        active_out[index] = unflatten(active)
        d_hidden_out[index] = unflatten(d_hidden)
        for example in range(bundle):
            span = slice(example * seq, (example + 1) * seq)
            up_grams[example] += dot_nt(d_hidden[span], d_hidden[span])
            down_grams[example] += dot_nt(active[span], active[span])
    rows_held[...] = unflatten(total)
    for index in range(shards):
        start = pl.multiple_of((info[2] ^ index) * (seq // shards), seq // shards)
        block = rows_held[:, pl.ds(start, seq // shards), :].astype(narrow)
        if index:
            sent_parts[index - 1][:, memory_rows:, :] = block
        else:
            own_output[...] = block
    d_rows, d_gain_rows = norm_back(rows_c, gains[2:3, :], d_normed)
    d_gain_c = jnp.sum(unflatten(d_gain_rows), 1, keepdims=True)
    d_gain_c_out[...] = d_gain_c
    d_mid = d_top.astype(wide) + d_rows
    d_mid_low = d_mid.astype(narrow)
    d_mid_out[...] = unflatten(d_mid_low)
    d_mix = dot_nn(d_mid_low, held[3]).astype(narrow)
    squares = []
    for example in range(bundle):
        span = slice(example * seq, (example + 1) * seq)
        for group in range(groups):
            columns = slice(group * quad_width, (group + 1) * quad_width)
            keys = keys_held[example, :, columns]
            queries = stack_heads(query_held[example, :, columns], masks)
            d_mixes = stack_heads(d_mix[span, columns], masks)
            weights = weights_held[example, group]
            d_weights = dot_nt(values_held[example, :, columns], d_mixes)
            inner = jnp.sum(weights * d_weights, 0, keepdims=True)
            d_scores = (weights * (d_weights - inner)).astype(narrow)
            d_query_out[example, :, columns] = (
                unstack_heads(dot_tn(d_scores, keys), masks_wide) * scaling
            ).astype(narrow)
            d_keys_out[example, :, columns] = (dot_nn(d_scores, queries) * scaling).astype(narrow)
            d_values_out[example, :, columns] = dot_nn(weights.astype(narrow), d_mixes).astype(
                narrow
            )
        memory_grad = dot_nt(d_keys_out[example], held[1]) + dot_nt(d_values_out[example], held[2])
        own_grad[example] = memory_grad[:memory_rows]
        for index, part in enumerate(sent_parts):
            part[example, :memory_rows, :] = memory_grad[
                (index + 1) * memory_rows : (index + 2) * memory_rows
            ].astype(narrow)
        d_query = d_query_out[example]
        mix = mix_out[example]
        square_sum = gram_squares(normed_b[span], dot_nt(d_query, d_query))
        square_sum += gram_squares(mix, dot_nt(d_mid_low[span], d_mid_low[span]))
        square_sum += gram_squares(normed_c[span], up_grams[example])
        square_sum += gram_squares(d_top[span], down_grams[example])
        for block in (d_keys_out, d_values_out):
            product = dot_tn(memory_held[example], block[example])
            square_sum += fold_lanes(jnp.sum(product * product, 0, keepdims=True))
        square_sum += fold_lanes(d_gain_c[example] * d_gain_c[example])
        squares.append(square_sum)
    d_normed_b = dot_nt(flatten(d_query_out[...]), held[0])
    d_rows_b, d_gain_rows = norm_back(rows_b, gains[1:2, :], d_normed_b)
    d_gain_b = jnp.sum(unflatten(d_gain_rows), 1, keepdims=True)
    d_gain_b_out[...] = d_gain_b
    for example in range(bundle):
        squares_out[example] = squares[example] + fold_lanes(
            d_gain_b[example] * d_gain_b[example]
        )
    early_out[...] = unflatten(d_mid + d_rows_b)


def self_backward_kernel(shards, plans, *refs):
    refs = list(refs)

    def take(count):
        taken = refs[:count]
        del refs[:count]
        return taken

    info, early_in, rows_in, normed_in, qkv_in, weights_in, mix_in = take(7)
    squares_in, d_gain_b, d_gain_c, buckets, gains = take(5)
    pieces = take(len(plans))
    tokens_grads = take(shards)
    d_qkv_out, d_early_out, small_out, norms_out = take(4)
    held, sems, rows_held, bias_held, folded_held = take(5)
    sem_list = [sems.at[index] for index in range(len(plans))]

    @pl.when(pl.program_id(0) == 0)
    def _():
        start_weights(info, pieces, plans, held, sem_list)
        wait_weights(plans, held, sem_list)

    masks = head_masks(narrow)
    masks_wide = head_masks(wide)
    scaling = 1.0 / math.sqrt(head_dim)
    bundle, seq, width = early_in.shape
    groups = width // quad_width
    bucket_count = bias_held.shape[0] // (groups * quad)

    def flatten(block):
        return block.reshape(block.shape[0] * block.shape[1], block.shape[2])

    def unflatten(block):
        return block.reshape(bundle, block.shape[0] // bundle, block.shape[1])

    early = flatten(early_in[...])
    d_early = early.astype(narrow)
    d_early_out[...] = unflatten(d_early)
    d_mix = dot_nn(d_early, held[3]).astype(narrow)
    squares = []
    for example in range(bundle):
        span = slice(example * seq, (example + 1) * seq)
        code = buckets[example].T
        for group in range(groups):
            columns = slice(group * quad_width, (group + 1) * quad_width)
            keys = qkv_in[1, example, :, columns]
            queries = stack_heads(qkv_in[0, example, :, columns], masks)
            d_mixes = stack_heads(d_mix[span, columns], masks)
            weights = weights_in[example, group]
            d_weights = dot_nt(qkv_in[2, example, :, columns], d_mixes)
            inner = jnp.sum(weights * d_weights, 0, keepdims=True)
            d_scores = (weights * (d_weights - inner)).astype(narrow)
            d_qkv_out[0, example, :, columns] = (
                unstack_heads(dot_tn(d_scores, keys), masks_wide) * scaling
            ).astype(narrow)
            d_qkv_out[1, example, :, columns] = (dot_nn(d_scores, queries) * scaling).astype(
                narrow
            )
            d_qkv_out[2, example, :, columns] = dot_nn(weights.astype(narrow), d_mixes).astype(
                narrow
            )
            d_wide = d_scores.astype(wide)
            for head in range(quad):
                folded_held[group * quad + head] = fold_causal(
                    d_wide[:, head * seq : (head + 1) * seq]
                )
        code = fold_causal(code)
        for bucket in range(bucket_count):
            chosen = code == bucket
            for head in range(groups * quad):
                picked = jnp.where(chosen, folded_held[head], 0.0)
                spot = head * bucket_count + bucket
                bias_held[spot : spot + 1, :] = jnp.sum(picked, 0, keepdims=True)
        d_bias = lax.dot_general(
            jnp.ones((8, 128), wide),
            bias_held[...],
            (((1,), (1,)), ((), ())),
            precision=lax.Precision.HIGHEST,
            preferred_element_type=wide,
        )[:1]
        small_out[example, :, 3 * width :] = d_bias
        grams = jnp.zeros((seq, seq), wide)
        for index in range(3):
            block = d_qkv_out[index, example]
            grams = grams + dot_nt(block, block)
        square_sum = gram_squares(normed_in[example], grams)
        square_sum += gram_squares(mix_in[example], dot_nt(d_early[span], d_early[span]))
        square_sum += fold_lanes(d_bias * d_bias)
        squares.append(square_sum)
    d_normed = dot_nt(flatten(d_qkv_out[0]), held[0])
    d_normed = d_normed + dot_nt(flatten(d_qkv_out[1]), held[1])
    d_normed = d_normed + dot_nt(flatten(d_qkv_out[2]), held[2])
    d_rows, d_gain_rows = norm_back(flatten(rows_in[...]).astype(wide), gains[0:1, :], d_normed)
    d_gain = jnp.sum(unflatten(d_gain_rows), 1, keepdims=True)
    small_out[:, :, :width] = d_gain
    small_out[:, :, width : 2 * width] = d_gain_b[...]
    small_out[:, :, 2 * width : 3 * width] = d_gain_c[...]
    for example in range(bundle):
        square_sum = (
            squares[example]
            + squares_in[example]
            + fold_lanes(d_gain[example] * d_gain[example])
        )
        total = jnp.sum(square_sum, -1, keepdims=True) + epsilon
        norms_out[example] = jnp.broadcast_to(jnp.sqrt(total), (1, 128))
    rows_held[...] = unflatten(early + d_rows)
    split_rows(info, rows_held, tokens_grads)


class Gradients:
    def __init__(self, info, clip, loads, load_sems, scaled, tile, held, store_sems):
        self.info, self.clip, self.scaled = info, clip, scaled
        self.tile, self.held, self.store_sems = tile, held, store_sems
        self.copies = [
            pltpu.make_async_copy(source, target, load_sems.at[index])
            for index, (source, target) in enumerate(loads)
        ]
        self.targets = [target for source, target in loads]
        self.stores = []
        for copy in self.copies:
            copy.start()

    def read(self, index):
        self.copies[index].wait()
        return self.targets[index]

    def scale(self, index):
        block = self.read(index)
        count, rows, width = block.shape
        for example in range(count):
            self.scaled[example * rows : (example + 1) * rows, :] = (
                block[example].astype(wide) * self.clip[example]
            ).astype(narrow)

    def product(self, index):
        block = self.read(index)
        return dot_tn(self.scaled[...], block[...].reshape(self.scaled.shape[0], block.shape[-1]))

    def write(self, value, outs, unit, places):
        number = len(self.stores) // 2
        tile = self.tile.at[number % 2]
        tile[...] = value.astype(narrow)
        halves = self.held.at[number]
        count = len(places) // 2
        for slot, (dp_index, tensor_index) in enumerate(places):
            high = pl.multiple_of((dp_index ^ self.info[0]) * 64, 64)
            left = pl.multiple_of((tensor_index ^ self.info[1]) * 128, 128)
            halves[slot // count, slot % count] = tile[pl.ds(high, 64), pl.ds(left, 128)]
        for half, out in enumerate(outs):
            copy = pltpu.make_async_copy(
                halves.at[half], out.at[:, unit], self.store_sems.at[len(self.stores)]
            )
            copy.start()
            self.stores.append(copy)

    def finish(self):
        for copy in self.stores:
            copy.wait()


def inner_gradient_kernel(places, info, clip, left, right, *refs):
    outs = refs[:2]
    rows_held, load_sems, scaled, tile, held, store_sems = refs[2:]
    loads = [(left, rows_held.at[0])]
    loads += [(right.at[unit], rows_held.at[1 + unit]) for unit in range(4)]
    work = Gradients(info, clip, loads, load_sems, scaled, tile, held, store_sems)
    work.scale(0)
    for unit in range(4):
        work.write(work.product(1 + unit), outs, unit, places)
    work.finish()


def self_gradient_kernel(places, info, clip, normed, d_qkv, d_early, mix, *refs):
    outs = refs[:2]
    rows_held, load_sems, scaled, tile, held, store_sems = refs[2:]
    sources = [normed, d_qkv.at[0], d_qkv.at[1], d_qkv.at[2], d_early, mix]
    loads = [(source, rows_held.at[index]) for index, source in enumerate(sources)]
    work = Gradients(info, clip, loads, load_sems, scaled, tile, held, store_sems)
    work.scale(0)
    for unit in range(3):
        work.write(work.product(1 + unit), outs, unit, places)
    work.scale(4)
    work.write(work.product(5), outs, 3, places)
    work.finish()


def cross_gradient_kernel(shards, chunks, places, info, clip, *refs):
    normed, d_query, d_mid, mix = refs[:4]
    parts = refs[4 : 4 + shards * chunks]
    refs = refs[4 + shards * chunks :]
    d_pair = refs[0]
    outs = refs[1:3]
    rows_held, parts_held, pairs_held, memory_held = refs[3:7]
    load_sems, scaled, tile, held, store_sems = refs[7:]
    count, memory_len = d_pair.shape[1:3]
    part_len = memory_len // shards
    group = count // chunks
    sources = [normed, d_query, d_mid, mix]
    loads = [(source, rows_held.at[index]) for index, source in enumerate(sources)]
    first = len(loads)
    for chunk in range(chunks):
        for index in range(shards):
            place = chunk * shards + index
            loads.append((parts[place].at[:, pl.ds(0, part_len)], parts_held.at[place]))
        for unit in range(2):
            loads.append(
                (d_pair.at[unit, pl.ds(chunk * group, group)], pairs_held.at[2 * chunk + unit])
            )
    work = Gradients(info, clip, loads, load_sems, scaled, tile, held, store_sems)
    work.scale(0)
    work.write(work.product(1), outs, 0, places)
    work.scale(2)
    work.write(work.product(3), outs, 1, places)
    totals = [None, None]
    for chunk in range(chunks):
        start = first + chunk * (shards + 2)
        for index in range(shards):
            block = work.read(start + index)
            for example in range(group):
                top = (example * shards + index) * part_len
                memory_held[chunk, top : top + part_len, :] = (
                    block[example].astype(wide) * clip[chunk * group + example]
                ).astype(narrow)
        for unit in range(2):
            pair = work.read(start + shards + unit)
            product = dot_tn(
                memory_held[chunk], pair[...].reshape(group * memory_len, pair.shape[-1])
            )
            totals[unit] = product if chunk == 0 else totals[unit] + product
    for unit in range(2):
        work.write(totals[unit], outs, 2 + unit, places)
    work.finish()


def stepper(parameter, gradient, momentum, average, step_rate):
    velocity = momentum_decay * momentum + gradient
    updated = parameter - step_rate * (gradient + momentum_decay * velocity)
    averaged = average_decay * average + (1.0 - average_decay) * updated
    return (velocity, averaged, updated)


def update_kernel(shrink, *refs):
    sums = refs[:8]
    params, outs = refs[8:20], refs[20:]

    def gradient(piece, unit):
        total = sums[2 * piece][unit].astype(wide) + sums[2 * piece + 1][unit].astype(wide)
        return total * shrink

    def step(group, spot, value, rate):
        weight, momentum, average = params[3 * group : 3 * group + 3]
        stepped = stepper(weight[spot], value, momentum[spot], average[spot], rate)
        for out, block in zip(outs[3 * group : 3 * group + 3], stepped):
            out[spot] = block

    inside = ((2, 0), (2, 1), (2, 2), (3, 0), (3, 2), (3, 3))
    for index, (piece, unit) in enumerate(inside):
        step(0, index, gradient(piece, unit), matrix_rate)
    for index, (piece, unit) in enumerate(((2, 3), (3, 1))):
        step(1, index, gradient(piece, unit), output_rate)
    for index in range(4):
        spot = (slice(None), slice(128 * index, 128 * (index + 1)))
        step(2, spot, gradient(0, index), matrix_rate)
        step(3, spot, gradient(1, index), matrix_rate)


def assemble_kernel(shards, chunks, *refs):
    refs = list(refs[1:])

    def take(count):
        taken = refs[:count]
        del refs[:count]
        return taken

    arrived = [take(shards - 1) for _ in range(chunks)]
    tokens_parts = take(shards - 1)
    take(3)
    output, tokens_grad, memory_grad = refs
    rows = memory_grad.shape[1]
    for index in range(shards - 1):
        for chunk in range(chunks):

            @pl.when((pl.program_id(0) == index) & (pl.program_id(1) == chunk))
            def _(index=index, chunk=chunk):
                tokens_grad[...] = tokens_parts[index][...].astype(wide)
                block = arrived[chunk][index]
                output[...] = block[:, rows:, :]
                memory_grad[...] = block[:, :rows, :].astype(wide)


def swap(value, axis, bit):
    size = lax.axis_size(axis)
    return lax.ppermute(value, axis, [(index, index ^ bit) for index in range(size)])


def after(value, *earlier):
    return lax.optimization_barrier((value,) + earlier)[0]


def gather_slots(shard):
    gathered = shard[None]
    for axis, bit in gather_order[:3]:
        gathered = jnp.concatenate([gathered, swap(gathered, axis, bit)], 0)
    beside = swap(gathered, *gather_order[3])
    pieces = [gathered, beside, swap(gathered, *gather_order[4]), swap(beside, *gather_order[4])]
    places = slot_places(gather_order, False)
    count = len(places) // 4
    return [
        (piece, places[index * count : (index + 1) * count]) for index, piece in enumerate(pieces)
    ]


def add_stage(kept, arrived):
    half = kept.shape[0] // 2

    def added(start, stop):
        total = kept[start:stop].astype(wide) + arrived[start:stop].astype(wide)
        return total.astype(narrow)

    if not half:
        return added(0, 1)[0], None
    return added(0, half), added(half, 2 * half)


def on_device(
    tokens,
    memory,
    cotangent,
    buckets,
    key_mask,
    task_groups,
    weights_in,
    weights_out,
    weights_up,
    weights_down,
    gains,
    position_bias,
    momentum_in,
    average_in,
    momentum_out,
    average_out,
    momentum_up,
    average_up,
    momentum_down,
    average_down,
    momentum_gain,
    average_gain,
    momentum_bias,
    average_bias,
):
    shards = lax.axis_size("tensor")
    replicas = lax.axis_size("dp")
    me_tensor = lax.axis_index("tensor")
    me_dp = lax.axis_index("dp")
    width = tokens.shape[2]
    seq = buckets.shape[1]
    seq_rows = tokens.shape[1]
    memory_rows = memory.shape[1]
    memory_len = memory_rows * shards
    group_count = tokens.shape[0]
    local = group_count // shards
    chunks = 2 if local % 2 == 0 else 1
    per_chunk = local // chunks
    bundle = 2 if per_chunk % 2 == 0 else 1
    steps = per_chunk // bundle
    bucket_count, heads_local = position_bias.shape
    heads = heads_local * shards
    gain_width = momentum_gain.shape[1]
    staged = shards == tensor_slots and replicas == dp_slots

    slot_base = [me_dp, me_tensor] if staged else [0 * me_dp, 0 * me_tensor]
    kernel_info = jnp.stack(slot_base + [me_tensor]).astype(jnp.int32)

    def square_shards():
        high, across = weights_in.shape[1], weights_in.shape[2]
        split = lambda block: block.reshape(high, -1, across).transpose(1, 0, 2)
        return (
            weights_in.astype(narrow),
            weights_out.astype(narrow).transpose(0, 2, 1),
            split(weights_up.astype(narrow)),
            split(weights_down.astype(narrow).T),
        )

    shard_in, shard_out, shard_up, shard_down = square_shards()
    slot_count = dp_slots * tensor_slots
    plain_places = [(slot // tensor_slots, slot % tensor_slots) for slot in range(slot_count)]

    def gather_late(blocks):
        count = blocks.shape[0]
        if staged:
            whole = lax.all_gather(blocks, ("dp", "tensor"), axis=0)
        else:
            whole = lax.all_gather(blocks, "dp", axis=1, tiled=True)
            whole = lax.all_gather(whole, "tensor", axis=2, tiled=True)
            whole = whole.reshape(count, dp_slots, 64, tensor_slots, 128).transpose(1, 3, 0, 2, 4)
            whole = whole.reshape(slot_count, count, 64, 128)
        return [whole], [(0, count, plain_places, False)]

    def gather_soon(blocks):
        if not staged:
            return gather_late(blocks)
        pieces, plans = [], []
        for piece, places in gather_slots(blocks):
            pieces.append(piece)
            plans.append((0, blocks.shape[0], places, True))
        return pieces, plans

    def exchange(values, start, count):
        found = []
        for index in range(shards):
            first = (me_tensor ^ index) * local + start
            blocks = [lax.dynamic_slice_in_dim(value, first, count, 0) for value in values]
            block = jnp.concatenate(blocks, 1) if len(blocks) > 1 else blocks[0]
            found.append(swap(block, "tensor", index) if index else block)
        return found

    late_pieces, late_plans = gather_late(jnp.concatenate([shard_up, shard_down], 0))
    token_parts = exchange([tokens], 0, local)
    self_pieces, self_plans = gather_soon(jnp.concatenate([shard_in[:3], shard_out[:1]], 0))
    cross_pieces, cross_plans = gather_soon(jnp.concatenate([shard_in[3:6], shard_out[1:2]], 0))
    late_plans = cross_plans + [(4,) + plan[1:] for plan in late_plans]
    late_pieces = cross_pieces + late_pieces
    soon_count = len(cross_pieces)
    table = jnp.pad(position_bias.T, ((0, 0), (0, 128 - bucket_count)))
    table_all = jnp.concatenate(
        [swap(table, "tensor", index) if index else table for index in range(shards)], 0
    )
    memory_parts = []
    earlier = token_parts
    for chunk in range(chunks):
        source, _ = lax.optimization_barrier((memory, earlier[-1]))
        earlier = exchange([source, cotangent], chunk * per_chunk, per_chunk)
        memory_parts.append(earlier)
    bucket_mine = lax.dynamic_slice_in_dim(buckets, me_tensor * local, local, 0)
    mask_mine = lax.dynamic_slice_in_dim(key_mask, me_tensor * local, local, 0)
    groups_mine = lax.dynamic_slice_in_dim(task_groups, me_tensor * local, local, 0)

    smem = pl.BlockSpec(memory_space=pltpu.SMEM)
    anywhere = pl.BlockSpec(memory_space=pl.ANY)
    params = pltpu.CompilerParams(
        vmem_limit_bytes=vmem_bytes, dimension_semantics=("arbitrary",)
    )

    def part_spec(shape, offset=0, lead=None):
        zeros = (0,) * len(shape)
        if lead is None:
            return pl.BlockSpec(
                (bundle,) + tuple(shape), lambda step, *_: (step + offset,) + zeros
            )
        return pl.BlockSpec(
            (lead, bundle) + tuple(shape), lambda step, *_: (0, step + offset) + zeros
        )

    def own_spec(shape, offset=0):
        zeros = (0,) * len(shape)
        return pl.BlockSpec(
            (bundle,) + tuple(shape),
            lambda step, info: (info[2] * (local // bundle) + step + offset,) + zeros,
        )

    def whole_spec(shape):
        return pl.BlockSpec(tuple(shape), lambda step, *_: (0,) * len(shape))

    def shaped(shape, dtype, lead=None, count=local):
        front = (count,) if lead is None else (lead, count)
        return jax.ShapeDtypeStruct(front + tuple(shape), dtype)

    def cost(flops, moved):
        return pl.CostEstimate(
            flops=int(flops * cost_scale), bytes_accessed=int(moved * cost_scale), transcendentals=0
        )

    groups = width // quad_width
    row_block = (seq, width)
    part_rows = memory_rows + seq_rows

    normed_a, rows_a, qkv_a, weights_a, mix_a, mid = pl.pallas_call(
        functools.partial(self_forward_kernel, shards, self_plans, heads_local),
        grid=(local // bundle,),
        in_specs=[smem]
        + [part_spec((seq_rows, width))] * shards
        + [part_spec((seq, seq))] * 2
        + [whole_spec(gains.shape), whole_spec(table_all.shape)]
        + [anywhere] * len(self_pieces),
        out_specs=[
            part_spec(row_block),
            part_spec(row_block),
            part_spec(row_block, lead=3),
            part_spec((groups, seq, quad * seq)),
            part_spec(row_block),
            part_spec(row_block),
        ],
        out_shape=[
            shaped(row_block, narrow),
            shaped(row_block, narrow),
            shaped(row_block, narrow, 3),
            shaped((groups, seq, quad * seq), wide),
            shaped(row_block, narrow),
            shaped(row_block, wide),
        ],
        scratch_shapes=[
            pltpu.VMEM((4, width, width), narrow),
            pltpu.SemaphoreType.DMA((len(self_pieces),)),
            pltpu.VMEM((bundle,) + row_block, narrow),
            pltpu.VMEM((bundle,) + row_block, narrow),
        ],
        compiler_params=params,
        name="self_forward",
        cost_estimate=cost(local * 2e9, local * 2e6),
    )(
        kernel_info,
        *token_parts,
        bucket_mine,
        mask_mine,
        gains,
        table_all,
        *self_pieces,
    )

    def cross(chunk, filled):
        offset = chunk * steps
        gain_block = (1, width)
        kept_specs = [
            part_spec(row_block, offset),
            part_spec(row_block, offset),
            part_spec(row_block, offset),
            part_spec((memory_len, width), offset, 2),
            part_spec(row_block, offset),
            part_spec(row_block, offset),
            part_spec(row_block, offset),
            part_spec(row_block, offset, 4),
            part_spec(row_block, offset, 4),
            part_spec(row_block, offset),
            part_spec(gain_block, offset),
            part_spec(gain_block, offset),
            part_spec((1, 128), offset),
        ]
        kept_shapes = [
            shaped(row_block, wide),
            shaped(row_block, narrow),
            shaped(row_block, narrow),
            shaped((memory_len, width), narrow, 2),
            shaped(row_block, narrow),
            shaped(row_block, narrow),
            shaped(row_block, narrow),
            shaped(row_block, narrow, 4),
            shaped(row_block, narrow, 4),
            shaped(row_block, narrow),
            shaped(gain_block, wide),
            shaped(gain_block, wide),
            shaped((1, 128), wide),
        ]
        own_specs = [own_spec((seq_rows, width), offset), own_spec((memory_rows, width), offset)]
        own_shapes = [
            shaped((seq_rows, width), narrow, count=group_count),
            shaped((memory_rows, width), wide, count=group_count),
        ]
        operands = [kernel_info, *memory_parts[chunk], mid, gains, *late_pieces]
        aliases = {}
        for index, block in enumerate(filled):
            aliases[len(operands) + index] = index if index < 2 else index + shards - 1
        return pl.pallas_call(
            functools.partial(cross_kernel, shards, late_plans, soon_count, len(filled)),
            grid_spec=pltpu.PrefetchScalarGridSpec(
                num_scalar_prefetch=1,
                grid=(steps,),
                in_specs=[part_spec((part_rows, width))] * shards
                + [part_spec(row_block, offset), whole_spec(gains.shape)]
                + [anywhere] * (len(late_pieces) + len(filled)),
                out_specs=own_specs + [part_spec((part_rows, width))] * (shards - 1) + kept_specs,
                scratch_shapes=[
                    pltpu.VMEM((12, width, width), narrow),
                    pltpu.SemaphoreType.DMA((len(late_pieces),)),
                    pltpu.VMEM((bundle, memory_len, width), narrow),
                    pltpu.VMEM((bundle, memory_len, width), narrow),
                    pltpu.VMEM((bundle, memory_len, width), narrow),
                    pltpu.VMEM((bundle, groups, memory_len, quad * seq), wide),
                    pltpu.VMEM((bundle,) + row_block, wide),
                    pltpu.VMEM((bundle,) + row_block, narrow),
                ],
            ),
            out_shape=own_shapes
            + [shaped((part_rows, width), narrow, count=per_chunk)] * (shards - 1)
            + kept_shapes,
            input_output_aliases=aliases,
            compiler_params=params,
            name="cross",
            cost_estimate=cost(per_chunk * 8e9, per_chunk * 6e6),
        )(*operands, *filled)

    filled, sent = [], []
    for chunk in range(chunks):
        found = cross(chunk, filled)
        sent.append(found[2 : shards + 1])
        filled = list(found[:2]) + list(found[shards + 1 :])
    own_output, own_memory = filled[:2]
    (
        early,
        normed_b,
        d_query_b,
        d_pair,
        mix_b,
        d_mid,
        normed_c,
        d_hidden,
        active,
        d_top,
        d_gain_b,
        d_gain_c,
        squares,
    ) = filled[2:]
    arrived = [
        [swap(block, "tensor", index + 1) for index, block in enumerate(blocks)] for blocks in sent
    ]
    soon = [block for blocks in arrived[:-1] for block in blocks]

    found = pl.pallas_call(
        functools.partial(self_backward_kernel, shards, self_plans),
        grid_spec=pltpu.PrefetchScalarGridSpec(
            num_scalar_prefetch=1,
            grid=(local // bundle,),
            in_specs=[
            part_spec(row_block),
            part_spec(row_block),
            part_spec(row_block),
            part_spec(row_block, lead=3),
            part_spec((groups, seq, quad * seq)),
            part_spec(row_block),
            part_spec((1, 128)),
            part_spec((1, width)),
            part_spec((1, width)),
            part_spec((seq, seq)),
            whole_spec(gains.shape),
        ]
        + [anywhere] * len(self_pieces),
        out_specs=[own_spec((seq_rows, width))]
        + [part_spec((seq_rows, width))] * (shards - 1)
        + [
            part_spec(row_block, lead=3),
            part_spec(row_block),
            part_spec((1, 3 * width + heads * bucket_count)),
            part_spec((1, 128)),
        ],
        scratch_shapes=[
            pltpu.VMEM((4, width, width), narrow),
            pltpu.SemaphoreType.DMA((len(self_pieces),)),
            pltpu.VMEM((bundle,) + row_block, wide),
            pltpu.VMEM((heads * bucket_count, 128), wide),
            pltpu.VMEM((heads, seq // 2 + 8, seq), wide),
        ],
        ),
        out_shape=[shaped((seq_rows, width), wide, count=group_count)]
        + [shaped((seq_rows, width), narrow)] * (shards - 1)
        + [
            shaped(row_block, narrow, 3),
            shaped(row_block, narrow),
            shaped((1, 3 * width + heads * bucket_count), wide),
            shaped((1, 128), wide),
        ],
        compiler_params=params,
        name="self_backward",
        cost_estimate=cost(local * 3e9, local * 3e6),
    )(
        after(kernel_info, *soon),
        early,
        rows_a,
        normed_a,
        qkv_a,
        weights_a,
        mix_a,
        squares,
        d_gain_b,
        d_gain_c,
        bucket_mine,
        gains,
        *self_pieces,
    )
    own_tokens, tokens_sent = found[0], found[1:shards]
    d_qkv, d_early, small, norms = found[shards:]

    norms = after(norms.reshape(local, 128), *arrived[-1])
    norm_slots = norms
    bit = 1
    while bit < shards:
        norm_slots = jnp.concatenate([norm_slots, swap(norm_slots, "tensor", bit)], 0)
        bit *= 2
    total = jnp.broadcast_to(jnp.sum(norm_slots, 0, keepdims=True), (8, 128))
    bit = 1
    while bit < replicas:
        total = total + swap(total, "dp", bit)
        bit *= 2
    order = jnp.arange(shards, dtype=jnp.int32) ^ me_tensor
    example_norms = norm_slots[:, 0].reshape(shards, local)[order].reshape(group_count)
    mean_norm = total[0, 0] / (group_count * replicas)
    limits = jnp.sum(
        (groups_mine[:, None] == jnp.arange(len(group_limits), dtype=jnp.int32))
        * jnp.asarray(group_limits, wide),
        1,
    )
    clip_weights = jnp.minimum(1.0 / mean_norm, limits / norms[:, 0])
    small = jnp.sum(clip_weights[:, None, None] * small, 0).reshape(-1, 128)

    def places_of(index):
        return slot_places(reduce_orders[index], True) if staged else plain_places

    out_shape = jax.ShapeDtypeStruct((slot_count // 2, 4, 64, 128), narrow)

    def gradient_call(kernel, clip, operands, loads, extra, name, work):
        return tuple(
            pl.pallas_call(
                kernel,
                in_specs=[smem, smem] + [anywhere] * len(operands),
                out_specs=[anywhere] * 2,
                out_shape=[out_shape] * 2,
                scratch_shapes=extra
                + [
                    pltpu.SemaphoreType.DMA((loads,)),
                    pltpu.VMEM((local * seq, width), narrow),
                    pltpu.VMEM((2, width, width), narrow),
                    pltpu.VMEM((4, 2, slot_count // 2, 64, 128), narrow),
                    pltpu.SemaphoreType.DMA((8,)),
                ],
                compiler_params=pltpu.CompilerParams(vmem_limit_bytes=vmem_bytes),
                name=name,
                cost_estimate=work,
            )(kernel_info, clip, *operands)
        )

    def inner_gradients(index, clip, left, right):
        kernel = functools.partial(inner_gradient_kernel, places_of(index))
        extra = [pltpu.VMEM((5, local, seq, width), narrow)]
        return gradient_call(
            kernel, clip, [left, right], 5, extra, "inner_gradients", cost(5e9, 7e6)
        )

    def self_gradients(clip):
        kernel = functools.partial(self_gradient_kernel, places_of(2))
        extra = [pltpu.VMEM((6, local, seq, width), narrow)]
        operands = [normed_a, d_qkv, d_early, mix_a]
        return gradient_call(kernel, clip, operands, 6, extra, "self_gradients", cost(5e9, 8e6))

    def cross_gradients(clip):
        kernel = functools.partial(cross_gradient_kernel, shards, chunks, places_of(3))
        extra = [
            pltpu.VMEM((4, local, seq, width), narrow),
            pltpu.VMEM((chunks * shards, per_chunk, memory_rows, width), narrow),
            pltpu.VMEM((2 * chunks, per_chunk, memory_len, width), narrow),
            pltpu.VMEM((chunks, per_chunk * memory_len, width), narrow),
        ]
        operands = [normed_b, d_query_b, d_mid, mix_b]
        operands += [block for blocks in memory_parts for block in blocks] + [d_pair]
        loads = 4 + chunks * (shards + 2)
        return gradient_call(
            kernel, clip, operands, loads, extra, "cross_gradients", cost(9e9, 20e6)
        )

    tokens_arrived = [swap(block, "tensor", index + 1) for index, block in enumerate(tokens_sent)]

    def by_place(shape, index, chunk=None):
        def spot(place, step, info):
            if chunk is not None:
                return (0, 0, 0)
            return (jnp.where(place == index, step, jnp.where(place < index, 0, chunks - 1)), 0, 0)

        return pl.BlockSpec((per_chunk,) + shape, spot)

    def to_place(shape):
        return pl.BlockSpec(
            (per_chunk,) + shape,
            lambda place, step, info: ((info[2] ^ (place + 1)) * chunks + step, 0, 0),
        )

    small_rows, large_rows = (seq_rows, width), (memory_rows, width)
    operands = [block for blocks in arrived for block in blocks] + tokens_arrived
    assemble = pl.pallas_call(
        functools.partial(assemble_kernel, shards, chunks),
        grid_spec=pltpu.PrefetchScalarGridSpec(
            num_scalar_prefetch=1,
            grid=(shards - 1, chunks),
            in_specs=[
                by_place((part_rows, width), index, chunk)
                for chunk in range(chunks)
                for index in range(shards - 1)
            ]
            + [by_place(small_rows, index) for index in range(shards - 1)]
            + [anywhere] * 3,
            out_specs=[to_place(small_rows), to_place(small_rows), to_place(large_rows)],
        ),
        out_shape=[
            jax.ShapeDtypeStruct((group_count,) + small_rows, narrow),
            jax.ShapeDtypeStruct((group_count,) + small_rows, wide),
            jax.ShapeDtypeStruct((group_count,) + large_rows, wide),
        ],
        input_output_aliases={len(operands) + 1 + index: index for index in range(3)},
        compiler_params=pltpu.CompilerParams(
            vmem_limit_bytes=vmem_bytes, dimension_semantics=("arbitrary", "arbitrary")
        ),
        name="assemble",
        cost_estimate=cost(1e6, 20e6),
    )
    returned = operands + [own_output, own_tokens, own_memory]

    pairs = [None] * 4

    last_stage = len(reduce_orders[0]) - 1
    done = [0] * 4

    def travel(*indices):
        for index in indices:
            if staged and done[index] <= last_stage:
                kept, sent = pairs[index]
                order = reduce_orders[index][done[index]]
                pairs[index] = add_stage(kept, swap(sent, *order))
                done[index] += 1

    def arrive_as_one(*indices):
        (stage,) = {reduce_orders[index][done[index]] for index in indices}
        sents = [pairs[index][1] for index in indices]
        came = swap(jnp.concatenate(sents, 0), *stage)
        found, start = [], 0
        for index, sent in zip(indices, sents):
            found.append(came[start : start + sent.shape[0]])
            start += sent.shape[0]
            done[index] += 1
        return found

    def there(*indices):
        return [block for index in indices for block in pairs[index] if block is not None]

    pairs[0] = inner_gradients(0, clip_weights, normed_c, d_hidden)
    clip = after(clip_weights, *there(0))
    pairs[1] = inner_gradients(1, clip, d_top, active)
    travel(0)
    clip = after(clip_weights, *there(0, 1))
    pairs[2] = self_gradients(clip)
    travel(1)
    clip = after(clip_weights, *there(1, 2), *tokens_arrived)
    pairs[3] = cross_gradients(clip)
    travel(0, 1)
    travel(2, 3)

    def together(*extra):
        held = lax.optimization_barrier((pairs, extra))
        pairs[:] = held[0]
        return held[1]

    def assembled():
        return assemble(after(kernel_info, *there(0)), *returned)

    shrink = 1.0 / math.sqrt(group_count * replicas)
    if staged:
        small = small + swap(small, *core)
        (small,) = together(small)
        small = small + swap(small, *side)
        travel(0, 1, 2, 3)
        output, tokens_grad, memory_grad = assembled()
        small, output = together(small, output)
        small = small + swap(small, *row)
        for index, came in zip((0, 3), arrive_as_one(0, 3)):
            pairs[index] = add_stage(pairs[index][0], came)
        travel(1, 2)
        (small,) = together(small)
        small = small + swap(small, *near)
        last = [None] * 4
        came = arrive_as_one(0, 1)
        for index in (0, 1):
            last[index] = (pairs[index][0][0], came[index][0])
        travel(2, 3)
        small, last = lax.optimization_barrier((small, last))
        small = small + swap(small, *far)
        for index, block in zip((2, 3), arrive_as_one(2, 3)):
            last[index] = (pairs[index][0][0], block[0])
        last = [block for pair in last for block in pair]
    else:
        output, tokens_grad, memory_grad = assembled()
        reduced = []
        for kept, sent in pairs:
            whole = jnp.concatenate([kept, sent], 0)
            count = whole.shape[1]
            whole = whole.reshape(dp_slots, tensor_slots, count, 64, 128).transpose(2, 0, 3, 1, 4)
            whole = whole.reshape(count, width, width)
            whole = lax.psum_scatter(whole, "dp", scatter_dimension=1, tiled=True)
            reduced.append(lax.psum_scatter(whole, "tensor", scatter_dimension=2, tiled=True))
        small = lax.psum(small, ("dp", "tensor"))
    small = small.reshape(-1)
    gain_total = small[: 3 * width].reshape(3, width)
    bias_total = small[3 * width :].reshape(heads, bucket_count).T

    large = [
        (weights_in, momentum_in, average_in, matrix_rate),
        (weights_out, momentum_out, average_out, output_rate),
        (weights_up, momentum_up, average_up, matrix_rate),
        (weights_down, momentum_down, average_down, matrix_rate),
    ]
    if staged:
        turns = ((0, 1, 2), (0, 2, 1), (0, 1), (1, 0))
        turned = [
            block.transpose(turn) for group, turn in zip(large, turns) for block in group[:3]
        ]
        operands = last + turned
        stepped = pl.pallas_call(
            functools.partial(update_kernel, shrink),
            out_shape=[
                jax.ShapeDtypeStruct(block.shape, wide) for block in turned
            ],
            compiler_params=pltpu.CompilerParams(vmem_limit_bytes=vmem_bytes),
            name="update",
            cost_estimate=cost(1e6, 4e6),
        )(*operands)
        stepped = [block.transpose(turns[index // 3]) for index, block in enumerate(stepped)]
    else:
        reduced = [block.astype(wide) * shrink for block in reduced]

        def merge(blocks):
            count, high, across = blocks.shape
            return blocks.transpose(1, 0, 2).reshape(high, count * across)

        inside = jnp.concatenate([reduced[2][:3], reduced[3][:1], reduced[3][2:]], 0)
        outward = jnp.stack([reduced[2][3].T, reduced[3][1].T], 0)
        gradients = [inside, outward, merge(reduced[0]), merge(reduced[1]).T]
        stepped = []
        for (weight, momentum, average, rate), gradient in zip(large, gradients):
            stepped += stepper(weight, gradient, momentum, average, rate)
    (
        velocity_in,
        averaged_in,
        updated_in,
        velocity_out,
        averaged_out,
        updated_out,
        velocity_up,
        averaged_up,
        updated_up,
        velocity_down,
        averaged_down,
        updated_down,
    ) = stepped

    gain_start = me_tensor * gain_width
    gain_shard = lax.dynamic_slice_in_dim(gains, gain_start, gain_width, 1)
    gain_grad = lax.dynamic_slice_in_dim(gain_total, gain_start, gain_width, 1) * shrink
    bias_grad = (
        lax.dynamic_slice_in_dim(bias_total, me_tensor * heads_local, heads_local, 1) * shrink
    )
    velocity_gain, averaged_gain, updated_gain = stepper(
        gain_shard, gain_grad, momentum_gain, average_gain, small_rate
    )
    velocity_bias, averaged_bias, updated_bias = stepper(
        position_bias, bias_grad, momentum_bias, average_bias, small_rate
    )
    return (
        output,
        tokens_grad,
        memory_grad,
        example_norms,
        velocity_in,
        averaged_in,
        updated_in,
        velocity_out,
        averaged_out,
        updated_out,
        velocity_up,
        averaged_up,
        updated_up,
        velocity_down,
        averaged_down,
        updated_down,
        velocity_gain,
        averaged_gain,
        updated_gain,
        velocity_bias,
        averaged_bias,
        updated_bias,
    )


def solution(mesh):
    return jax.shard_map(
        on_device,
        mesh=mesh,
        in_specs=(
            P("dp", "tensor", None),
            P("dp", "tensor", None),
            P("dp", "tensor", None),
            P("dp", None, None),
            P("dp", None, None),
            P("dp"),
            P(None, "dp", "tensor"),
            P(None, "tensor", "dp"),
            P("dp", "tensor"),
            P("tensor", "dp"),
            P(),
            P(None, "tensor"),
            P(None, "dp", "tensor"),
            P(None, "dp", "tensor"),
            P(None, "tensor", "dp"),
            P(None, "tensor", "dp"),
            P("dp", "tensor"),
            P("dp", "tensor"),
            P("tensor", "dp"),
            P("tensor", "dp"),
            P(None, "tensor"),
            P(None, "tensor"),
            P(None, "tensor"),
            P(None, "tensor"),
        ),
        out_specs=(
            P("dp", "tensor", None),
            P("dp", "tensor", None),
            P("dp", "tensor", None),
            P("dp"),
            P(None, "dp", "tensor"),
            P(None, "dp", "tensor"),
            P(None, "dp", "tensor"),
            P(None, "tensor", "dp"),
            P(None, "tensor", "dp"),
            P(None, "tensor", "dp"),
            P("dp", "tensor"),
            P("dp", "tensor"),
            P("dp", "tensor"),
            P("tensor", "dp"),
            P("tensor", "dp"),
            P("tensor", "dp"),
            P(None, "tensor"),
            P(None, "tensor"),
            P(None, "tensor"),
            P(None, "tensor"),
            P(None, "tensor"),
            P(None, "tensor"),
        ),
        check_vma=False,
    )
```
